256 devices in a mesh: ctx: 8 (over y_lo, x), head: 32 (over z, y_hi, core).
Axes of the slice: x: 4, y: 4 (y_hi: 2, y_lo: 2; y = y_hi * 2 + y_lo), z: 8, core: 2. Of those that a mesh axis runs over, the one named last changes fastest.
Arguments:
- tokens: bfloat16 [4096, 2304], P('ctx'), may hold values from -6 to 6
- w_qkv: bfloat16 [2304, 3, 4096], P(None, None, 'head'), may hold values from -0.125 to 0.125
- conv_weight: float32 [4, 3, 4096], P(None, None, 'head'), may hold values from -3 to 3
- f_down: bfloat16 [2304, 128], replicated, may hold values from -0.125 to 0.125
- f_up: bfloat16 [128, 4096], P(None, 'head'), may hold values from -0.5 to 0.5
- dt_bias: float32 [4096], P('head'), may hold values from -9 to -3
- a_log: float32 [32], P('head'), may hold values from -1 to 0.5
- w_beta: bfloat16 [2304, 32], P(None, 'head'), may hold values from -0.125 to 0.125
- o_down: bfloat16 [2304, 128], replicated, may hold values from -0.125 to 0.125
- o_up: bfloat16 [128, 4096], P(None, 'head'), may hold values from -0.5 to 0.5
- norm_gain: float32 [128], replicated, may hold values from 0.5 to 1.5
- w_out: bfloat16 [4096, 2304], P('head'), may hold values from -0.09375 to 0.09375
Outputs:
- layer_out: bfloat16 [4096, 2304], P(('ctx', 'head'))
The draws below stay inside these ranges and needn't reach their ends.
All inputs are finite; a program needn't handle non-finite values.
Results may differ from the reference program's by a relative error of at most 0.023.
Values may be sent and summed in bfloat16 or wider, within the bound.
No kernel may reach another device: no remote copies, remote signals or barrier semaphores. Data moves between devices by JAX's collectives and lax.ppermute only.
A program may use at most 128 MiB of HBM per device.

```python
import jax
import jax.numpy as jnp
from jax import lax

D = 2304
DK = 128
CONV = 4
BLOCK = 64
HEADS = 32
TOKENS = 4096


def shard_levels(own_key, extent, split, low, largest):
    def one(position, blocks):
        heights = jax.random.uniform(jax.random.fold_in(jax.random.fold_in(own_key, 6), position), (blocks,), jnp.float32, low / len(split), largest / len(split))
        return jnp.repeat(jnp.exp(heights), extent[position] // blocks).reshape((-1,) + (1,) * (len(extent) - position - 1))

    loudness = one(*split[0])
    for cut in split[1:]:
        loudness = loudness * one(*cut)
    return loudness


def noise(rng, dims, scale, bound, shards=(), held_as=jnp.bfloat16):
    result = scale * jax.random.normal(rng, dims, jnp.float32)
    if shards:
        result = result * shard_levels(rng, dims, shards, -0.22, 0.18)
    return jnp.clip(result, -bound, bound).astype(held_as)


def setup_inputs(seed: int = 0) -> dict:
    key_list = jax.random.split(jax.random.key(seed), 13)
    tokens = noise(key_list[0], (TOKENS, D), 1.0, 6.0, ((0, 8),))
    w_qkv = noise(key_list[1], (D, 3, HEADS * DK), D ** -0.5, 0.125, ((2, 32),))
    conv_weight = noise(key_list[2], (CONV, 3, HEADS * DK), CONV ** -0.5, 3.0, ((2, 32),), jnp.float32)
    f_down = noise(key_list[3], (D, DK), D ** -0.5, 0.125)
    f_up = noise(key_list[4], (DK, HEADS * DK), DK ** -0.5, 0.5, ((1, 32),))
    dt_bias = jnp.clip(-9.0 + 6.0 * jax.random.uniform(key_list[5], (HEADS * DK,), jnp.float32) ** shard_levels(key_list[5], (HEADS * DK,), ((0, 32),), -0.2, 0.2), -9.0, -3.0)
    a_log = jnp.clip(-1.0 + 1.5 * jax.random.uniform(key_list[6], (HEADS,), jnp.float32) ** shard_levels(key_list[6], (HEADS,), ((0, 32),), -0.2, 0.2), -1.0, 0.5)
    w_beta = noise(key_list[7], (D, HEADS), D ** -0.5, 0.125, ((1, 32),))
    o_down = noise(key_list[8], (D, DK), D ** -0.5, 0.125)
    o_up = noise(key_list[9], (DK, HEADS * DK), DK ** -0.5, 0.5, ((1, 32),))
    norm_gain = jnp.clip(1.0 + 0.1 * jax.random.normal(key_list[10], (DK,), jnp.float32), 0.5, 1.5)
    w_out = noise(key_list[11], (HEADS * DK, D), (HEADS * DK) ** -0.5, 0.09375, ((0, 32),))
    return {"tokens": tokens, "w_qkv": w_qkv, "conv_weight": conv_weight, "f_down": f_down, "f_up": f_up, "dt_bias": dt_bias, "a_log": a_log, "w_beta": w_beta, "o_down": o_down, "o_up": o_up, "norm_gain": norm_gain, "w_out": w_out}


HIGHEST = lax.Precision.HIGHEST

def block_update(carried, blocks):
    queries, keyset, values, decays, beta_rate = blocks
    cumulative = jnp.cumsum(decays, axis=1)
    rising = jnp.exp(cumulative)
    falling = jnp.exp(-cumulative)
    key_rise = keyset * rising
    key_fall = keyset * falling
    query_rise = queries * rising
    strict_mask = jnp.tri(BLOCK, k=-1, dtype=jnp.float32)
    causal_mask = jnp.tri(BLOCK, dtype=jnp.float32)
    inner = jnp.einsum('htc,hsc->hts', key_rise, key_fall, precision=HIGHEST)
    scores = jnp.einsum('htc,hsc->hts', query_rise, key_fall, precision=HIGHEST) * causal_mask
    system = jnp.eye(BLOCK, dtype=jnp.float32) + beta_rate[:, :, None] * inner * strict_mask
    target = beta_rate[:, :, None] * (values - jnp.einsum('htc,hcv->htv', key_rise, carried, precision=HIGHEST))
    updates = lax.linalg.triangular_solve(system, target, left_side=True, lower=True, unit_diagonal=True)
    outputs = jnp.einsum('htc,hcv->htv', query_rise, carried, precision=HIGHEST)
    outputs = outputs + jnp.einsum('hts,hsv->htv', scores, updates, precision=HIGHEST)
    tail_keys = keyset * jnp.exp(cumulative[:, -1:, :] - cumulative)
    carried = jnp.exp(cumulative[:, -1, :])[:, :, None] * carried
    carried = carried + jnp.einsum('htc,htv->hcv', tail_keys, updates, precision=HIGHEST)
    return (carried, outputs)

def to_blocks(array):
    return jnp.moveaxis(array.reshape(TOKENS // BLOCK, BLOCK, HEADS, DK), 2, 1)

def add_head(total, pair):
    head_rows, head_weight = pair
    part = jnp.dot(head_rows.astype(jnp.float32), head_weight.astype(jnp.float32), preferred_element_type=jnp.float32).astype(jnp.bfloat16)
    part = lax.optimization_barrier(part).astype(jnp.float32)
    return (total + part, None)

def reference(tokens, w_qkv, conv_weight, f_down, f_up, dt_bias, a_log, w_beta, o_down, o_up, norm_gain, w_out):
    raw = jnp.dot(tokens.astype(jnp.float32), w_qkv.reshape(D, 3 * HEADS * DK).astype(jnp.float32), preferred_element_type=jnp.float32).astype(jnp.bfloat16)
    raw = lax.optimization_barrier(raw).astype(jnp.float32).reshape(TOKENS, 3, HEADS, DK)
    kernel = conv_weight.reshape(CONV, 3, HEADS, DK)
    padded = jnp.concatenate([jnp.zeros((CONV - 1, 3, HEADS, DK), jnp.float32), raw], axis=0)
    mixed = padded[0:TOKENS] * kernel[0]
    for tap_index in range(1, CONV):
        mixed = mixed + padded[tap_index:tap_index + TOKENS] * kernel[tap_index]
    active = jax.nn.silu(mixed)
    query_raw = active[:, 0]
    key_raw = active[:, 1]
    queries = query_raw * lax.rsqrt(lax.optimization_barrier(jnp.sum(query_raw * query_raw, axis=-1, keepdims=True)) + 1e-06) * DK ** (-0.5)
    keyset = key_raw * lax.rsqrt(lax.optimization_barrier(jnp.sum(key_raw * key_raw, axis=-1, keepdims=True)) + 1e-06)
    rounded = lax.optimization_barrier((queries.astype(jnp.bfloat16), keyset.astype(jnp.bfloat16), active[:, 2].astype(jnp.bfloat16)))
    queries = rounded[0].astype(jnp.float32)
    keyset = rounded[1].astype(jnp.float32)
    values = rounded[2].astype(jnp.float32)
    gate_low = jnp.dot(tokens.astype(jnp.float32), f_down.astype(jnp.float32), preferred_element_type=jnp.float32).astype(jnp.bfloat16)
    gate_logit = jnp.dot(gate_low.astype(jnp.float32), f_up.astype(jnp.float32), preferred_element_type=jnp.float32) + dt_bias
    decays = -jnp.exp(a_log)[None, :, None] * jax.nn.softplus(gate_logit.reshape(TOKENS, HEADS, DK))
    beta_rate = jax.nn.sigmoid(jnp.dot(tokens.astype(jnp.float32), w_beta.astype(jnp.float32), preferred_element_type=jnp.float32))
    beta_blocks = jnp.moveaxis(beta_rate.reshape(TOKENS // BLOCK, BLOCK, HEADS), 2, 1)
    start = jnp.zeros((HEADS, DK, DK), jnp.float32)
    _, outputs = lax.scan(block_update, start, (to_blocks(queries), to_blocks(keyset), to_blocks(values), to_blocks(decays), beta_blocks))
    core = jnp.moveaxis(outputs, 1, 2).reshape(TOKENS, HEADS, DK)
    out_low = jnp.dot(tokens.astype(jnp.float32), o_down.astype(jnp.float32), preferred_element_type=jnp.float32).astype(jnp.bfloat16)
    out_gate = jax.nn.sigmoid(jnp.dot(out_low.astype(jnp.float32), o_up.astype(jnp.float32), preferred_element_type=jnp.float32)).reshape(TOKENS, HEADS, DK)
    scale = lax.rsqrt(lax.optimization_barrier(jnp.mean(core * core, axis=-1, keepdims=True)) + 1e-05)
    gated = (core * scale * norm_gain * out_gate).astype(jnp.bfloat16)
    total = jnp.zeros((TOKENS, D), jnp.float32)
    total, _ = lax.scan(add_head, total, (jnp.moveaxis(gated, 1, 0), w_out.reshape(HEADS, DK, D)))
    return total.astype(jnp.bfloat16)
```

```python
import functools

import jax
import jax.numpy as jnp
from jax import lax
from jax.experimental import pallas as pl
from jax.experimental.pallas import tpu as pltpu
from jax.sharding import PartitionSpec as P

BLOCK = 64
GROUP = 256
F32 = jnp.float32
BF16 = jnp.bfloat16
HIGHEST = lax.Precision.HIGHEST
VMEM = pl.BlockSpec(memory_space=pltpu.VMEM)
SMEM = pl.BlockSpec(memory_space=pltpu.SMEM)
LIMIT = pltpu.CompilerParams(vmem_limit_bytes=40 * 1024 * 1024)


def mm(left, right):
    return jnp.dot(left.astype(BF16), right.astype(BF16), preferred_element_type=F32)


def mm_nt(left, right):
    return lax.dot_general(
        left.astype(BF16), right.astype(BF16), (((1,), (1,)), ((), ())), preferred_element_type=F32
    )


def mm_tn(left, right):
    return lax.dot_general(
        left.astype(BF16), right.astype(BF16), (((0,), (0,)), ((), ())), preferred_element_type=F32
    )


def split(value):
    high = value.astype(BF16)
    return high, (value - high.astype(F32)).astype(BF16)


def mm3(left, right):
    lh, ll = split(left)
    rh, rl = split(right)
    dot = functools.partial(jnp.dot, preferred_element_type=F32)
    return dot(lh, rh) + (dot(lh, rl) + dot(ll, rh))


def project(
    alog, tokens, w3, f_down, f_up, bias, w_beta, o_down, o_up, raw_out, cum_out, beta_out, gate_out
):
    head = f_up.shape[0]
    tok = tokens[...]
    for part in range(3):
        raw_out[:, part * head : (part + 1) * head] = jnp.dot(
            tok, w3[part], preferred_element_type=F32
        ).astype(BF16)
    low = jnp.dot(tok, f_down[...], preferred_element_type=F32).astype(BF16)
    logit = jnp.dot(low, f_up[...], preferred_element_type=F32) + bias[...]
    decays = -jnp.exp(jnp.full((1, 1), alog[0], F32)) * jax.nn.softplus(logit)
    row = lax.broadcasted_iota(jnp.int32, (GROUP, GROUP), 0)
    col = lax.broadcasted_iota(jnp.int32, (GROUP, GROUP), 1)
    tri = jnp.where((row >= col) & ((row // BLOCK) == (col // BLOCK)), 1.0, 0.0).astype(F32)
    cum_out[...] = jnp.dot(tri, decays, precision=HIGHEST, preferred_element_type=F32)
    beta_out[...] = jax.nn.sigmoid(
        mm_nt(tok, jnp.broadcast_to(w_beta[...].astype(F32), (head, w_beta.shape[1])))
    )
    out_low = jnp.dot(tok, o_down[...], preferred_element_type=F32).astype(BF16)
    gate_out[...] = jax.nn.sigmoid(jnp.dot(out_low, o_up[...], preferred_element_type=F32))


def delta(raw, rim, taps, cum_ref, beta_ref, c_out, w_out, padded):
    rows, width = raw.shape
    head = width // 3
    count = rows // BLOCK
    padded[0:8, :] = rim[...].astype(F32)[rim.shape[0] - 8 :]
    padded[8:, :] = raw[...].astype(F32)
    conv_taps = taps.shape[1]
    active = []
    for part in range(3):
        lanes = slice(part * head, (part + 1) * head)
        mixed = padded[9 - conv_taps : 9 - conv_taps + rows, lanes] * taps[part, 0:1, :]
        for tap in range(1, conv_taps):
            start = 9 - conv_taps + tap
            mixed = mixed + padded[start : start + rows, lanes] * taps[part, tap : tap + 1, :]
        active.append(jax.nn.silu(mixed))
    query_raw, key_raw, value_raw = active
    queries = query_raw * lax.rsqrt(
        jnp.sum(query_raw * query_raw, axis=-1, keepdims=True) + 1e-06
    ) * (head ** (-0.5))
    keyset = key_raw * lax.rsqrt(jnp.sum(key_raw * key_raw, axis=-1, keepdims=True) + 1e-06)
    queries = queries.astype(BF16).astype(F32)
    keyset = keyset.astype(BF16).astype(F32)
    values = value_raw.astype(BF16).astype(F32)
    cumulative = cum_ref[...]
    beta = beta_ref[...]
    rising = jnp.exp(cumulative)
    falling = jnp.exp(-cumulative)
    key_rise = keyset * rising
    key_fall = (keyset * falling).astype(BF16)
    query_rise = queries * rising
    blocked = cumulative.reshape(count, BLOCK, head)
    ends = blocked[:, BLOCK - 1 : BLOCK, :]
    tail = (keyset.reshape(count, BLOCK, head) * jnp.exp(ends - blocked)).reshape(rows, head)
    tail = tail.astype(BF16)
    target = jnp.concatenate([beta * values, beta * key_rise], axis=1).astype(BF16)
    row = lax.broadcasted_iota(jnp.int32, (GROUP, GROUP), 0)
    col = lax.broadcasted_iota(jnp.int32, (GROUP, GROUP), 1)
    differ = row ^ col
    same = differ < BLOCK
    lower = row > col
    unit = jnp.where(row == col, 1.0, 0.0).astype(F32)
    systems, scores, inverse = [], [], []
    for group in range(rows // GROUP):
        rng = slice(group * GROUP, (group + 1) * GROUP)
        inner = mm_nt(key_rise[rng], key_fall[rng])
        wide = jnp.concatenate([beta[rng], beta[rng]], axis=1)
        systems.append(jnp.where(lower & same, inner * wide, 0.0))
        scores.append(
            jnp.where((row >= col) & same, mm_nt(query_rise[rng], key_fall[rng]), 0.0).astype(BF16)
        )
        inverse.append(unit - jnp.where(differ == 1, systems[-1], 0.0))
    size = 2
    while size < BLOCK:
        here = (differ >= size) & (differ < 2 * size)
        steps = [mm(jnp.where(here, s, 0.0), d) for s, d in zip(systems, inverse)]
        inverse = [d - mm(d, x) for d, x in zip(inverse, steps)]
        size *= 2
    mixing, adding, moving = [], [], []
    for group in range(rows // GROUP):
        rng = slice(group * GROUP, (group + 1) * GROUP)
        solved = mm(inverse[group], target[rng]).astype(BF16)
        local = mm(scores[group], solved)
        local_value, local_key = local[:, :head], query_rise[rng] - local[:, head:]
        for inside in range(GROUP // BLOCK):
            sub = slice(inside * BLOCK, (inside + 1) * BLOCK)
            mixing.append((local_value[sub], local_key[sub].astype(BF16)))
            pair = mm_tn(tail[group * GROUP + inside * BLOCK :][:BLOCK], solved[sub])
            adding.append(pair[:, :head])
            moving.append(pair[:, head:])
    shrink = jnp.transpose(jnp.exp(ends.reshape(count, head)))
    ident = unit[:head, :head]
    state = jnp.concatenate([jnp.zeros((head, head), F32), ident], axis=1)
    for block in range(count):
        low = state.astype(BF16)
        value_part, key_part = mixing[block]
        across = jnp.dot(key_part, low, preferred_element_type=F32)
        rng = slice(block * BLOCK, (block + 1) * BLOCK)
        c_out[rng, :head] = across[:, :head] + value_part
        c_out[rng, head:] = across[:, head:]
        step = mm(moving[block], low)
        state = shrink[:, block : block + 1] * state - step
        state = jnp.concatenate([state[:, :head] + adding[block], state[:, head:]], axis=1)
    final = state.astype(BF16)
    for copy in range(w_out.shape[0]):
        w_out[copy] = final


def finish(place, c_ref, gate, gain, states, own, to_core, to_far, to_both, gated):
    rows, head = gate.shape
    ctx, sub = place[0], place[1]
    state = jnp.zeros((head, head), F32)
    for step in range(states.shape[0] - 1):
        moved = jnp.dot(states[step, :, head:], state.astype(BF16), preferred_element_type=F32)
        state = jnp.where(step < ctx, moved + states[step, :, :head].astype(F32), state)
    core = c_ref[:, :head] + mm(c_ref[:, head:], state)
    scale = lax.rsqrt(jnp.mean(core * core, axis=-1, keepdims=True) + 1e-05)
    result = core * scale * gain[...] * gate[...]
    gated[...] = result.reshape(gated.shape)
    for out, flip in ((own, 0), (to_core, 1), (to_far, 2), (to_both, 3)):
        out[...] = gated[:, pl.ds(sub ^ flip, 1)].reshape(out.shape).astype(BF16)


def spread(place, g0, g1, g2, g3, w0, w1, w2, w3, out, left):
    zs, rows, head = g0.shape
    z = place[2]
    for lane, ref in enumerate((g0, g1, g2, g3)):
        for k in range(zs):
            left[k, :, lane * head : (lane + 1) * head] = ref[(z + k) % zs]
    full = left[...].reshape(zs * rows, 4 * head)
    total = jnp.dot(full[:, :head], w0[...], preferred_element_type=F32)
    for lane, ref in ((1, w1), (2, w2), (3, w3)):
        total = total + jnp.dot(
            full[:, lane * head : (lane + 1) * head], ref[...], preferred_element_type=F32
        )
    out[...] = total.astype(BF16).reshape(out.shape)


def on_device(
    tokens, w_qkv, conv_weight, f_down, f_up, dt_bias, a_log, w_beta, o_down, o_up, norm_gain, w_out
):
    rows, model = tokens.shape
    head = f_up.shape[1]
    ctx_count, head_count = lax.axis_size("ctx"), lax.axis_size("head")
    zs = head_count // 4
    shape = jax.ShapeDtypeStruct
    ctx, which = lax.axis_index("ctx"), lax.axis_index("head")
    place = jnp.stack([ctx, which % 4, which // 4]).astype(jnp.int32)

    def flip(value, mask):
        return lax.ppermute(value, "head", [(h, h ^ mask) for h in range(head_count)])

    with jax.named_scope("rim"):
        rim_tokens = lax.ppermute(
            tokens[rows - 16 :], "ctx", [(i, i + 1) for i in range(ctx_count - 1)]
        )
    with jax.named_scope("weights"):
        w_core, w_far = flip(w_out, 1), flip(w_out, 2)
        w_both = flip(w_far, 1)
    w3 = jnp.transpose(w_qkv, (1, 0, 2))
    tile = pl.BlockSpec((GROUP, head), lambda i: (i, 0))
    whole = lambda *dims: pl.BlockSpec(dims, lambda i: (0,) * len(dims))
    with jax.named_scope("project"):
        raw, cum, beta, gate = pl.pallas_call(
            project,
            grid=(rows // GROUP,),
            in_specs=[
                SMEM,
                pl.BlockSpec((GROUP, model), lambda i: (i, 0)),
                whole(3, model, head),
                whole(model, head),
                whole(head, head),
                whole(1, head),
                whole(1, model),
                whole(model, head),
                whole(head, head),
            ],
            out_specs=[pl.BlockSpec((GROUP, 3 * head), lambda i: (i, 0)), tile, tile, tile],
            out_shape=[
                shape((rows, 3 * head), BF16),
                shape((rows, head), F32),
                shape((rows, head), F32),
                shape((rows, head), F32),
            ],
            compiler_params=LIMIT,
            cost_estimate=pl.CostEstimate(
                flops=2 * rows * model * 6 * head, bytes_accessed=6_000_000, transcendentals=0
            ),
        )(
            a_log,
            tokens,
            w3,
            f_down,
            f_up,
            dt_bias.reshape(1, head),
            w_beta.reshape(1, model),
            o_down,
            o_up,
        )
    with jax.named_scope("rim_raw"):
        rim = lax.dot_general(
            rim_tokens, w3, (((1,), (1,)), ((), ())), preferred_element_type=F32
        ).astype(BF16).reshape(16, 3 * head)
    with jax.named_scope("delta"):
        c_parts, states = pl.pallas_call(
            delta,
            in_specs=[VMEM] * 5,
            out_specs=[VMEM] * 2,
            out_shape=[shape((rows, 2 * head), F32), shape((ctx_count, head, 2 * head), BF16)],
            scratch_shapes=[pltpu.VMEM((rows + 8, 3 * head), F32)],
            compiler_params=LIMIT,
            cost_estimate=pl.CostEstimate(
                flops=4_000_000_000, bytes_accessed=30_000_000, transcendentals=0
            ),
        )(raw, rim, jnp.transpose(conv_weight, (1, 0, 2)), cum, beta)
    with jax.named_scope("states"):
        states = lax.all_to_all(states, "ctx", 0, 0, tiled=True)
    part = shape((zs, 16, head), BF16)
    with jax.named_scope("finish"):
        own, to_core, to_far, to_both = pl.pallas_call(
            finish,
            in_specs=[SMEM] + [VMEM] * 4,
            out_specs=[VMEM] * 4,
            out_shape=[part] * 4,
            scratch_shapes=[pltpu.VMEM((zs, 4, 16, head), F32)],
            compiler_params=LIMIT,
        )(place, c_parts, gate, norm_gain.reshape(1, head), states)
    with jax.named_scope("exchange"):
        from_both, from_far, from_core = flip(to_both, 3), flip(to_far, 2), flip(to_core, 1)
    with jax.named_scope("spread"):
        parts = pl.pallas_call(
            spread,
            in_specs=[SMEM] + [VMEM] * 8,
            out_specs=VMEM,
            out_shape=shape((zs, 16, model), BF16),
            scratch_shapes=[pltpu.VMEM((zs, 16, 4 * head), BF16)],
            compiler_params=LIMIT,
        )(place, own, from_core, from_far, from_both, w_out, w_core, w_far, w_both)
    with jax.named_scope("reduce"):
        return reduce_z(parts, zs, head_count)


def reduce_z(parts, zs, head_count):
    def send(value, k):
        return lax.ppermute(
            value, "head", [(h, (h + 4 * k) % head_count) for h in range(head_count)]
        )

    total = parts[0].astype(F32)
    order = sorted(range(1, zs), key=lambda k: -min(k, zs - k))
    for got in [send(parts[k], k) for k in order]:
        total = total + got.astype(F32)
    return total.astype(BF16)


def solution(mesh):
    in_specs = (
        P("ctx", None),
        P(None, None, "head"),
        P(None, None, "head"),
        P(),
        P(None, "head"),
        P("head"),
        P("head"),
        P(None, "head"),
        P(),
        P(None, "head"),
        P(),
        P("head", None),
    )
    out_specs = P(("ctx", "head"), None)
    return jax.shard_map(
        on_device, mesh=mesh, in_specs=in_specs, out_specs=out_specs, check_vma=False
    )
```

```python
import functools

import jax
import jax.numpy as jnp
from jax import lax
from jax.experimental import pallas as pl
from jax.experimental.pallas import tpu as pltpu
from jax.sharding import PartitionSpec as P

BLOCK = 64
GROUP = 128
SPAN = 256
SUBS = 8
CHUNKS = 3
F32 = jnp.float32
BF16 = jnp.bfloat16
HIGHEST = lax.Precision.HIGHEST
VMEM = pl.BlockSpec(memory_space=pltpu.VMEM)
HBM = pl.BlockSpec(memory_space=pltpu.HBM)
SMEM = pl.BlockSpec(memory_space=pltpu.SMEM)
FULL = pltpu.CompilerParams(vmem_limit_bytes=62 * 1024 * 1024)
LIMIT = pltpu.CompilerParams(vmem_limit_bytes=16 * 1024 * 1024)


def cost(us):
    return pl.CostEstimate(flops=0, bytes_accessed=int(us * 3_690_000), transcendentals=0)


def mm(left, right):
    return jnp.dot(left.astype(BF16), right.astype(BF16), preferred_element_type=F32)


def mm_nt(left, right):
    return lax.dot_general(
        left.astype(BF16), right.astype(BF16), (((1,), (1,)), ((), ())), preferred_element_type=F32
    )


def mm_tn(left, right):
    return lax.dot_general(
        left.astype(BF16), right.astype(BF16), (((0,), (0,)), ((), ())), preferred_element_type=F32
    )


def split(value):
    high = value.astype(BF16)
    return high, (value - high.astype(F32)).astype(BF16)


def mm3(left, right):
    lh, ll = split(left)
    rh, rl = split(right)
    dot = functools.partial(jnp.dot, preferred_element_type=F32)
    return dot(lh, rh) + (dot(lh, rl) + dot(ll, rh))


def masks(size):
    row = lax.broadcasted_iota(jnp.int32, (size, size), 0)
    col = lax.broadcasted_iota(jnp.int32, (size, size), 1)
    return row, col, row ^ col


def load(pairs, sems):
    copies = []
    for place, (source, target) in enumerate(pairs):
        copies.append(pltpu.make_async_copy(source, target, sems.at[place]))
        copies[-1].start()
    return copies


def convolve(total, taps, padded, rows, part):
    head = taps.shape[2]
    conv_taps = taps.shape[1]
    lanes = slice(part * head, (part + 1) * head)
    edge = total[rows:, lanes].astype(BF16).astype(F32)[total.shape[0] - rows - 8 :]
    padded[0:8, lanes] = jnp.where(lax.axis_index("ctx") > 0, edge, 0.0)
    padded[8:, lanes] = total[:rows, lanes].astype(BF16).astype(F32)
    mixed = padded[9 - conv_taps : 9 - conv_taps + rows, lanes] * taps[part, 0:1, :]
    for tap in range(1, conv_taps):
        start = 9 - conv_taps + tap
        mixed = mixed + padded[start : start + rows, lanes] * taps[part, tap : tap + 1, :]
    return jax.nn.silu(mixed)


def unit_rows(value):
    return value * lax.rsqrt(jnp.sum(value * value, axis=-1, keepdims=True) + 1e-06)


def front(
    alog, tokens_hbm, rim_hbm, w3_hbm, f_down_hbm, o_down_hbm, f_up_hbm, o_up_hbm, bias_hbm,
    w_beta_hbm, taps_hbm, plain_out, carry_out, half_out, gate_out, sends, tok, w3, f_down, o_down,
    wide, f_up, o_up, bias, w_beta, taps, total, padded, final, sems, out_sems,
):
    rows, model = tokens_hbm.shape
    head = f_up.shape[0]
    count = rows // BLOCK
    inside = SPAN // BLOCK
    chunk = model // CHUNKS
    pairs = [(w_beta_hbm, w_beta), (rim_hbm, tok.at[pl.ds(rows, rim_hbm.shape[0])])]
    for step in range(CHUNKS):
        rng = pl.ds(step * chunk, chunk)
        pairs.append((tokens_hbm.at[:, rng], tok.at[pl.ds(0, rows), rng]))
        pairs += [(w3_hbm.at[part, rng], w3.at[part, rng]) for part in range(3)]
        pairs.append((f_down_hbm.at[rng], f_down.at[rng]))
        pairs.append((o_down_hbm.at[rng], o_down.at[rng]))
    pairs += [(f_up_hbm, f_up), (o_up_hbm, o_up), (bias_hbm, bias), (taps_hbm, taps)]
    copies = load(pairs, sems)
    wide[...] = jnp.zeros_like(wide)
    copies[0].wait()
    column = jnp.transpose(jnp.broadcast_to(w_beta[...].astype(F32), (8, model)))
    wide[:, 0:8] = column.astype(BF16)
    copies[1].wait()
    for step in range(CHUNKS):
        for copy in copies[2 + 6 * step : 8 + 6 * step]:
            copy.wait()
        rng = slice(step * chunk, (step + 1) * chunk)
        joined = [w3[part, rng] for part in range(3)] + [f_down[rng], o_down[rng], wide[rng]]
        piece = jnp.dot(tok[:, rng], jnp.concatenate(joined, axis=1), preferred_element_type=F32)
        if step == 0:
            total[...] = piece
        else:
            total[...] += piece
    for copy in copies[2 + 6 * CHUNKS :]:
        copy.wait()
    low = total[:rows, 3 * head : 4 * head].astype(BF16)
    logit = jnp.dot(low, f_up[...], preferred_element_type=F32) + bias[...]
    decays = -jnp.exp(jnp.full((1, 1), alog[0], F32)) * jax.nn.softplus(logit)
    out_low = total[:rows, 4 * head : 5 * head].astype(BF16)
    gate_out[...] = jax.nn.sigmoid(jnp.dot(out_low, o_up[...], preferred_element_type=F32))
    beta = jnp.broadcast_to(jax.nn.sigmoid(total[:rows, 5 * head : 5 * head + 1]), (rows, head))
    row, col, differ = masks(GROUP)
    strict = (row > col) & (differ < BLOCK)
    causal = (row >= col) & (differ < BLOCK)
    unit = jnp.where(row == col, 1.0, 0.0).astype(F32)
    tri = jnp.where(causal, 1.0, 0.0).astype(BF16)
    high, rest = split(decays)
    middle, least = split(decays - high.astype(F32) - rest.astype(F32))
    terms = jnp.concatenate([high, rest, middle], axis=1)
    sums = [
        jnp.dot(tri, terms[s : s + GROUP], preferred_element_type=F32) for s in range(0, rows, GROUP)
    ]
    sums = jnp.concatenate(sums, axis=0)
    cumulative = sums[:, :head] + (sums[:, head : 2 * head] + sums[:, 2 * head :])
    key_raw = convolve(total, taps, padded, rows, 1)
    value_raw = convolve(total, taps, padded, rows, 2)
    query_raw = convolve(total, taps, padded, rows, 0)
    keyset = unit_rows(key_raw).astype(BF16).astype(F32)
    values = value_raw.astype(BF16).astype(F32)
    rising = jnp.exp(cumulative)
    key_rise = keyset * rising
    key_fall = (keyset * jnp.exp(-cumulative)).astype(BF16)
    blocked = cumulative.reshape(count, BLOCK, head)
    ends = blocked[:, BLOCK - 1 : BLOCK, :]
    tail = (keyset.reshape(count, BLOCK, head) * jnp.exp(ends - blocked)).reshape(rows, head)
    tail = tail.astype(BF16)
    shrink = jnp.transpose(jnp.exp(ends.reshape(count, head)))
    target = jnp.concatenate([beta * values, beta * key_rise], axis=1).astype(BF16)
    systems, inverse = [], []
    for start in range(0, rows, GROUP):
        rng = slice(start, start + GROUP)
        inner = mm_nt(key_rise[rng], key_fall[rng])
        systems.append(jnp.where(strict, inner * beta[rng], 0.0))
        inverse.append(unit - jnp.where(differ == 1, systems[-1], 0.0))
    size = 2
    while size < BLOCK:
        here = (differ >= size) & (differ < 2 * size)
        steps = [mm(jnp.where(here, s, 0.0), d) for s, d in zip(systems, inverse)]
        inverse = [d - mm(d, x) for d, x in zip(inverse, steps)]
        size *= 2
    pairs, solves, starts = [], [], {}
    for group, start in enumerate(range(0, rows, GROUP)):
        solved = mm(inverse[group], target[start : start + GROUP]).astype(BF16)
        solves.append(solved)
        for block in range(GROUP // BLOCK):
            sub = slice(block * BLOCK, (block + 1) * BLOCK)
            pairs.append(mm_tn(tail[start + block * BLOCK :][:BLOCK], solved[sub]))
    fresh = jnp.concatenate([jnp.zeros((head, head), F32), unit], axis=1)
    states = [fresh] * (rows // SPAN)
    for block in range(inside):
        for group in range(rows // SPAN):
            at = group * inside + block
            state = states[group]
            short = state.astype(BF16)
            starts[at] = short
            step = mm(pairs[at][:, head:], short)
            state = shrink[:, at : at + 1] * state - step
            states[group] = jnp.concatenate(
                [state[:, :head] + pairs[at][:, :head], state[:, head:]], axis=1
            )
    half_out[...] = states[0].astype(BF16)
    whole = mm(states[1][:, head:], states[0])
    final[...] = jnp.concatenate(
        [whole[:, :head] + states[1][:, :head], whole[:, head:]], axis=1
    ).astype(BF16)
    copies = load([(final, sends.at[i]) for i in range(sends.shape[0])], out_sems)
    queries = (unit_rows(query_raw) * (head ** (-0.5))).astype(BF16).astype(F32)
    query_rise = queries * rising
    for group, start in enumerate(range(0, rows, GROUP)):
        rng = slice(start, start + GROUP)
        scores = jnp.where(causal, mm_nt(query_rise[rng], key_fall[rng]), 0.0)
        local = mm(scores, solves[group])
        local_key = (query_rise[rng] - local[:, head:]).astype(BF16)
        for block in range(GROUP // BLOCK):
            sub = slice(block * BLOCK, (block + 1) * BLOCK)
            out = slice(start + block * BLOCK, start + (block + 1) * BLOCK)
            across = jnp.dot(
                local_key[sub], starts[(start // BLOCK) + block], preferred_element_type=F32
            )
            plain_out[out] = across[:, :head] + local[sub, :head]
            carry_out[out] = across[:, head:].astype(BF16)
    for copy in copies:
        copy.wait()


def stage(plain, carry, half, gate, gain, plain_out, carry_out, half_out, gate_out):
    plain_out[...] = plain[...]
    carry_out[...] = carry[...]
    half_out[...] = half[...]
    gate_out[...] = gate[...] * gain[...]


def finish(plain, carry, half, gate, states, own, other, gated):
    rows, head = gate.shape
    ctx = lax.axis_index("ctx")
    core_at = lax.rem(lax.axis_index("head"), 2)
    state = jnp.zeros((head, head), F32)
    for step in range(states.shape[0] - 1):
        moved = jnp.dot(states[step, :, head:], state.astype(BF16), preferred_element_type=F32)
        state = jnp.where(step < ctx, moved + states[step, :, :head].astype(F32), state)
    middle = jnp.dot(half[:, head:], state.astype(BF16), preferred_element_type=F32)
    middle = middle + half[:, :head].astype(F32)
    cores = []
    for group, start in enumerate((state, middle)):
        rng = slice(group * SPAN, (group + 1) * SPAN)
        cores.append(plain[rng] + mm(carry[rng], start))
    core = jnp.concatenate(cores, axis=0)
    scale = lax.rsqrt(jnp.mean(core * core, axis=-1, keepdims=True) + 1e-05)
    result = core * scale * gate[...]
    gated[...] = result.astype(BF16).reshape(gated.shape)
    for pair in range(own.shape[0]):
        own[pair] = gated[:, pair, pl.ds(core_at, 1)].reshape(own.shape[1:])
        other[pair] = gated[:, pair, pl.ds(1 - core_at, 1)].reshape(own.shape[1:])


def regroup(own, sibling, *outs):
    mine = lax.rem(lax.axis_index("head") // 2, own.shape[0])
    for flip, out in enumerate(outs):
        at = mine ^ flip
        out[0] = own[pl.ds(at, 1)].reshape(out.shape[1:])
        out[1] = sibling[pl.ds(at, 1)].reshape(out.shape[1:])


def spread(part, w_one, w_two, *refs):
    rest, held, out, left = refs[:-3], refs[-3], refs[-2], refs[-1]
    turn(part, left)
    joined = jnp.concatenate([w_one[...], w_two[...]], axis=0)
    out[...] = jnp.dot(left[...], joined, preferred_element_type=F32)
    head = w_one.shape[0]
    for at, ref in enumerate(rest):
        held[at * head : (at + 1) * head] = ref[...]


def turn(part, left):
    mine = lax.axis_index("head") // SUBS
    sides, zs, rows, head = part.shape
    for side in range(sides):
        for k in range(zs):
            piece = part[side, pl.ds(mine ^ k, 1)].reshape(rows, head)
            left[k * rows : (k + 1) * rows, side * head : (side + 1) * head] = piece


def combine(begun, *refs):
    parts, (held, w_one, w_two, out, left) = refs[:3], refs[3:]
    total = begun[...]
    depth = left.shape[-1]
    for which, part in enumerate(parts):
        turn(part, left.at[which])
        if which < 2:
            weight = held[which * depth : (which + 1) * depth]
        else:
            weight = jnp.concatenate([w_one[...], w_two[...]], axis=0)
        total = total + jnp.dot(left[which], weight, preferred_element_type=F32)
    out[...] = total.astype(BF16).reshape(out.shape)


def on_device(
    tokens, w_qkv, conv_weight, f_down, f_up, dt_bias, a_log, w_beta, o_down, o_up, norm_gain, w_out
):
    rows, model = tokens.shape
    head = f_up.shape[1]
    ctx_count, head_count = lax.axis_size("ctx"), lax.axis_size("head")
    zs = head_count // SUBS
    shape = jax.ShapeDtypeStruct
    dma = pltpu.SemaphoreType.DMA

    def flip(value, mask):
        return lax.ppermute(value, "head", [(h, h ^ mask) for h in range(head_count)])

    w3 = jnp.transpose(w_qkv, (1, 0, 2))
    taps = jnp.transpose(conv_weight, (1, 0, 2))
    edge = tokens[rows - 16 :]
    with jax.named_scope("rim"):
        rim = lax.ppermute(edge, "ctx", [(i, (i + 1) % ctx_count) for i in range(ctx_count)])
    (w_sent,) = after((w_out,), edge)
    with jax.named_scope("weights"):
        w_far, w_next, w_core = flip(w_sent, 2), flip(w_sent, 4), flip(w_sent, 1)
    with jax.named_scope("front"):
        plain, carry, half, gate, sends = pl.pallas_call(
            front,
            in_specs=[SMEM] + [HBM] * 10,
            out_specs=[VMEM] * 4 + [HBM],
            out_shape=[
                shape((rows, head), F32),
                shape((rows, head), BF16),
                shape((head, 2 * head), BF16),
                shape((rows, head), F32),
                shape((ctx_count, head, 2 * head), BF16),
            ],
            scratch_shapes=[
                pltpu.VMEM((rows + 16, model), BF16),
                pltpu.VMEM((3, model, head), BF16),
                pltpu.VMEM((model, head), BF16),
                pltpu.VMEM((model, head), BF16),
                pltpu.VMEM((model, head), BF16),
                pltpu.VMEM((head, head), BF16),
                pltpu.VMEM((head, head), BF16),
                pltpu.VMEM((1, head), F32),
                pltpu.VMEM((1, model), BF16),
                pltpu.VMEM(taps.shape, F32),
                pltpu.VMEM((rows + 16, 6 * head), F32),
                pltpu.VMEM((rows + 8, 3 * head), F32),
                pltpu.VMEM((head, 2 * head), BF16),
                dma((6 + 6 * CHUNKS,)),
                dma((ctx_count,)),
            ],
            compiler_params=FULL,
            cost_estimate=cost(9),
        )(
            a_log,
            tokens,
            rim,
            w3,
            f_down,
            o_down,
            f_up,
            o_up,
            dt_bias.reshape(1, head),
            w_beta.reshape(1, model),
            taps,
        )
    with jax.named_scope("states"):
        states = lax.all_to_all(sends, "ctx", 0, 0, tiled=True)
    w_late, w_near = after((w_far, w_next), half)
    with jax.named_scope("weights"):
        w_both = flip(w_late, 4)
        w_far_core, w_next_core = flip(w_late, 1), flip(w_near, 1)
    with jax.named_scope("stage"):
        kinds = [shape(v.shape, v.dtype) for v in (plain, carry, half, gate)]
        staged = pl.pallas_call(
            stage,
            in_specs=[VMEM] * 5,
            out_specs=[VMEM] * 4,
            out_shape=kinds,
            compiler_params=LIMIT,
            cost_estimate=cost(0.5),
        )(plain, carry, half, gate, norm_gain.reshape(1, head))
    with jax.named_scope("finish"):
        own, other = pl.pallas_call(
            finish,
            in_specs=[VMEM] * 5,
            out_specs=[VMEM] * 2,
            out_shape=[shape((SUBS // 2, zs, 16, head), BF16)] * 2,
            scratch_shapes=[pltpu.VMEM((zs, SUBS // 2, 2, 16, head), BF16)],
            compiler_params=LIMIT,
            cost_estimate=cost(1.8),
        )(*staged, states)
    with jax.named_scope("exchange"):
        sibling = flip(other, 1)
        kept, *sent = pl.pallas_call(
            regroup,
            in_specs=[VMEM] * 2,
            out_specs=[VMEM] * 4,
            out_shape=[shape((2, zs, 16, head), BF16)] * 4,
            compiler_params=LIMIT,
            cost_estimate=cost(0.5),
        )(own, sibling)
        got = {f: flip(sent[f - 1], 2 * f) for f in (3, 1, 2)}
    with jax.named_scope("spread"):
        held, begun = pl.pallas_call(
            spread,
            in_specs=[VMEM] * 7,
            out_specs=[VMEM] * 2,
            out_shape=[shape((4 * head, model), BF16), shape((zs * 16, model), F32)],
            scratch_shapes=[pltpu.VMEM((zs * 16, 2 * head), BF16)],
            compiler_params=LIMIT,
            cost_estimate=cost(2.5),
        )(kept, w_out, w_core, w_far, w_far_core, w_next, w_next_core)
        (w_late,) = after((w_both,), own)
        w_both_core = flip(w_late, 1)
        parts = pl.pallas_call(
            combine,
            in_specs=[VMEM] * 7,
            out_specs=VMEM,
            out_shape=shape((zs, 16, model), BF16),
            scratch_shapes=[pltpu.VMEM((3, zs * 16, 2 * head), BF16)],
            compiler_params=LIMIT,
            cost_estimate=cost(1.0),
        )(begun, got[1], got[2], got[3], held, w_both, w_both_core)
    with jax.named_scope("reduce"):
        total = parts[0].astype(F32)
        for part in [flip(parts[k], SUBS * k) for k in (2, 1, 3)]:
            total = total + part.astype(F32)
        return total.astype(BF16)


def after(values, token):
    return lax.optimization_barrier((*values, token))[: len(values)]


def solution(mesh):
    in_specs = (
        P("ctx", None),
        P(None, None, "head"),
        P(None, None, "head"),
        P(),
        P(None, "head"),
        P("head"),
        P("head"),
        P(None, "head"),
        P(),
        P(None, "head"),
        P(),
        P("head", None),
    )
    out_specs = P(("ctx", "head"), None)
    return jax.shard_map(
        on_device, mesh=mesh, in_specs=in_specs, out_specs=out_specs, check_vma=False
    )
```

```python
import functools

import jax
import jax.numpy as jnp
from jax import lax
from jax.experimental import pallas as pl
from jax.experimental.pallas import tpu as pltpu
from jax.sharding import PartitionSpec as P

BLOCK = 64
GROUP = 128
SPAN = 256
SUBS = 8
CHUNKS = 3
F32 = jnp.float32
BF16 = jnp.bfloat16
HIGHEST = lax.Precision.HIGHEST
VMEM = pl.BlockSpec(memory_space=pltpu.VMEM)
HBM = pl.BlockSpec(memory_space=pltpu.HBM)
SMEM = pl.BlockSpec(memory_space=pltpu.SMEM)
FULL = pltpu.CompilerParams(vmem_limit_bytes=62 * 1024 * 1024)
LIMIT = pltpu.CompilerParams(vmem_limit_bytes=16 * 1024 * 1024)


def cost(us, flops=0):
    return pl.CostEstimate(
        flops=int(flops * 1_000_000_000), bytes_accessed=int(us * 3_690_000), transcendentals=0
    )


def mm(left, right):
    return jnp.dot(left.astype(BF16), right.astype(BF16), preferred_element_type=F32)


def mm_nt(left, right):
    return lax.dot_general(
        left.astype(BF16), right.astype(BF16), (((1,), (1,)), ((), ())), preferred_element_type=F32
    )


def mm_tn(left, right):
    return lax.dot_general(
        left.astype(BF16), right.astype(BF16), (((0,), (0,)), ((), ())), preferred_element_type=F32
    )


def split(value):
    high = value.astype(BF16)
    return high, (value - high.astype(F32)).astype(BF16)


def mm3(left, right):
    lh, ll = split(left)
    rh, rl = split(right)
    dot = functools.partial(jnp.dot, preferred_element_type=F32)
    return dot(lh, rh) + (dot(lh, rl) + dot(ll, rh))


def masks(size):
    row = lax.broadcasted_iota(jnp.int32, (size, size), 0)
    col = lax.broadcasted_iota(jnp.int32, (size, size), 1)
    return row, col, row ^ col


def load(pairs, sems):
    copies = []
    for place, (source, target) in enumerate(pairs):
        copies.append(pltpu.make_async_copy(source, target, sems.at[place]))
        copies[-1].start()
    return copies


def convolve(total, taps, padded, rows, part):
    head = taps.shape[2]
    conv_taps = taps.shape[1]
    lanes = slice(part * head, (part + 1) * head)
    edge = total[rows:, lanes].astype(BF16).astype(F32)[total.shape[0] - rows - 8 :]
    padded[0:8, lanes] = jnp.where(lax.axis_index("ctx") > 0, edge, 0.0)
    padded[8:, lanes] = total[:rows, lanes].astype(BF16).astype(F32)
    mixed = padded[9 - conv_taps : 9 - conv_taps + rows, lanes] * taps[part, 0:1, :]
    for tap in range(1, conv_taps):
        start = 9 - conv_taps + tap
        mixed = mixed + padded[start : start + rows, lanes] * taps[part, tap : tap + 1, :]
    return jax.nn.silu(mixed)


def unit_rows(value):
    return value * lax.rsqrt(jnp.sum(value * value, axis=-1, keepdims=True) + 1e-06)


def front(
    tokens_hbm, rim_hbm, alog_hbm, w3_hbm, f_down_hbm, o_down_hbm, f_up_hbm, o_up_hbm, bias_hbm,
    w_beta_hbm, taps_hbm, pack_hbm, sends, tok, w3, f_down, o_down,
    wide, f_up, o_up, bias, w_beta, taps, alog, total, padded, final, pack, sems, out_sems, pack_sems,
):
    rows, model = tokens_hbm.shape
    head = f_up.shape[0]
    count = rows // BLOCK
    inside = SPAN // BLOCK
    chunk = model // CHUNKS
    pairs = [(w_beta_hbm, w_beta), (rim_hbm, tok.at[pl.ds(rows, rim_hbm.shape[0])])]
    for step in range(CHUNKS):
        rng = pl.ds(step * chunk, chunk)
        pairs.append((tokens_hbm.at[:, rng], tok.at[pl.ds(0, rows), rng]))
        pairs += [(w3_hbm.at[part, rng], w3.at[part, rng]) for part in range(3)]
        pairs.append((f_down_hbm.at[rng], f_down.at[rng]))
        pairs.append((o_down_hbm.at[rng], o_down.at[rng]))
    pairs += [(f_up_hbm, f_up), (o_up_hbm, o_up), (bias_hbm, bias), (taps_hbm, taps)]
    pairs.append((alog_hbm, alog))
    copies = load(pairs, sems)
    wide[...] = jnp.zeros_like(wide)
    copies[0].wait()
    column = jnp.transpose(jnp.broadcast_to(w_beta[...].astype(F32), (8, model)))
    wide[:, 0:8] = column.astype(BF16)
    copies[1].wait()
    for step in range(CHUNKS):
        for copy in copies[2 + 6 * step : 8 + 6 * step]:
            copy.wait()
        rng = slice(step * chunk, (step + 1) * chunk)
        joined = [w3[part, rng] for part in range(3)] + [f_down[rng], o_down[rng], wide[rng]]
        piece = jnp.dot(tok[:, rng], jnp.concatenate(joined, axis=1), preferred_element_type=F32)
        if step == 0:
            total[...] = piece
        else:
            total[...] += piece
    for copy in copies[2 + 6 * CHUNKS :]:
        copy.wait()
    low = total[:rows, 3 * head : 4 * head].astype(BF16)
    logit = jnp.dot(low, f_up[...], preferred_element_type=F32) + bias[...]
    decays = -jnp.exp(alog[...]) * jax.nn.softplus(logit)
    out_low = total[:rows, 4 * head : 5 * head].astype(BF16)
    pack[:rows, 2 * head :] = jax.nn.sigmoid(jnp.dot(out_low, o_up[...], preferred_element_type=F32))
    stores = []

    def store(at):
        stores.append(pltpu.make_async_copy(pack.at[at], pack_hbm.at[at], pack_sems.at[len(stores)]))
        stores[-1].start()

    store((pl.ds(0, rows), pl.ds(2 * head, head)))
    beta = jnp.broadcast_to(jax.nn.sigmoid(total[:rows, 5 * head : 5 * head + 1]), (rows, head))
    row, col, differ = masks(GROUP)
    strict = (row > col) & (differ < BLOCK)
    causal = (row >= col) & (differ < BLOCK)
    unit = jnp.where(row == col, 1.0, 0.0).astype(F32)
    tri = jnp.where(causal, 1.0, 0.0).astype(BF16)
    high, rest = split(decays)
    middle, least = split(decays - high.astype(F32) - rest.astype(F32))
    terms = jnp.concatenate([high, rest, middle], axis=1)
    sums = [
        jnp.dot(tri, terms[s : s + GROUP], preferred_element_type=F32) for s in range(0, rows, GROUP)
    ]
    sums = jnp.concatenate(sums, axis=0)
    cumulative = sums[:, :head] + (sums[:, head : 2 * head] + sums[:, 2 * head :])
    key_raw = convolve(total, taps, padded, rows, 1)
    value_raw = convolve(total, taps, padded, rows, 2)
    query_raw = convolve(total, taps, padded, rows, 0)
    keyset = unit_rows(key_raw).astype(BF16).astype(F32)
    values = value_raw.astype(BF16).astype(F32)
    rising = jnp.exp(cumulative)
    key_rise = keyset * rising
    key_fall = (keyset * jnp.exp(-cumulative)).astype(BF16)
    blocked = cumulative.reshape(count, BLOCK, head)
    ends = blocked[:, BLOCK - 1 : BLOCK, :]
    tail = (keyset.reshape(count, BLOCK, head) * jnp.exp(ends - blocked)).reshape(rows, head)
    tail = tail.astype(BF16)
    shrink = jnp.transpose(jnp.exp(ends.reshape(count, head)))
    target = jnp.concatenate([beta * values, beta * key_rise], axis=1).astype(BF16)
    systems, inverse = [], []
    for start in range(0, rows, GROUP):
        rng = slice(start, start + GROUP)
        inner = mm_nt(key_rise[rng], key_fall[rng])
        systems.append(jnp.where(strict, inner * beta[rng], 0.0))
        inverse.append(unit - jnp.where(differ == 1, systems[-1], 0.0))
    size = 2
    while size < BLOCK:
        here = (differ >= size) & (differ < 2 * size)
        steps = [mm(jnp.where(here, s, 0.0), d) for s, d in zip(systems, inverse)]
        inverse = [d - mm(d, x) for d, x in zip(inverse, steps)]
        size *= 2
    pairs, solves, starts = [], [], {}
    for group, start in enumerate(range(0, rows, GROUP)):
        solved = mm(inverse[group], target[start : start + GROUP]).astype(BF16)
        solves.append(solved)
        for block in range(GROUP // BLOCK):
            sub = slice(block * BLOCK, (block + 1) * BLOCK)
            pairs.append(mm_tn(tail[start + block * BLOCK :][:BLOCK], solved[sub]))
    fresh = jnp.concatenate([jnp.zeros((head, head), F32), unit], axis=1)
    states = [fresh] * (rows // SPAN)
    for block in range(inside):
        for group in range(rows // SPAN):
            at = group * inside + block
            state = states[group]
            short = state.astype(BF16)
            starts[at] = short
            step = mm(pairs[at][:, head:], short)
            state = shrink[:, at : at + 1] * state - step
            states[group] = jnp.concatenate(
                [state[:, :head] + pairs[at][:, :head], state[:, head:]], axis=1
            )
    pack[rows:, : 2 * head] = states[0]
    store((pl.ds(rows, head), pl.ds(0, 2 * head)))
    whole = mm(states[1][:, head:], states[0])
    final[...] = jnp.concatenate(
        [whole[:, :head] + states[1][:, :head], whole[:, head:]], axis=1
    ).astype(BF16)
    copies = load([(final, sends.at[i]) for i in range(sends.shape[0])], out_sems)
    queries = (unit_rows(query_raw) * (head ** (-0.5))).astype(BF16).astype(F32)
    query_rise = queries * rising
    for group, start in enumerate(range(0, rows, GROUP)):
        rng = slice(start, start + GROUP)
        scores = jnp.where(causal, mm_nt(query_rise[rng], key_fall[rng]), 0.0)
        local = mm(scores, solves[group])
        local_key = (query_rise[rng] - local[:, head:]).astype(BF16)
        for block in range(GROUP // BLOCK):
            sub = slice(block * BLOCK, (block + 1) * BLOCK)
            out = slice(start + block * BLOCK, start + (block + 1) * BLOCK)
            across = jnp.dot(
                local_key[sub], starts[(start // BLOCK) + block], preferred_element_type=F32
            )
            pack[out, :head] = across[:, :head] + local[sub, :head]
            pack[out, head : 2 * head] = across[:, head:]
        store((pl.ds(start, GROUP), pl.ds(0, 2 * head)))
    for copy in copies + stores:
        copy.wait()


def stage(pack, gain, out):
    head = gain.shape[1]
    rows = pack.shape[0] - head
    out[:, : 2 * head] = pack[:, : 2 * head]
    out[:rows, 2 * head :] = pack[:rows, 2 * head :] * gain[...]


def finish(pack, states, own, other, gated):
    head = states.shape[1]
    rows = pack.shape[0] - head
    ctx = lax.axis_index("ctx")
    core_at = lax.rem(lax.axis_index("head"), 2)
    state = jnp.zeros((head, head), F32)
    for step in range(states.shape[0] - 1):
        moved = jnp.dot(states[step, :, head:], state.astype(BF16), preferred_element_type=F32)
        state = jnp.where(step < ctx, moved + states[step, :, :head].astype(F32), state)
    middle = mm(pack[rows:, head : 2 * head], state) + pack[rows:, :head]
    cores = []
    for group, start in enumerate((state, middle)):
        rng = slice(group * SPAN, (group + 1) * SPAN)
        cores.append(pack[rng, :head] + mm(pack[rng, head : 2 * head], start))
    core = jnp.concatenate(cores, axis=0)
    scale = lax.rsqrt(jnp.mean(core * core, axis=-1, keepdims=True) + 1e-05)
    result = core * scale * pack[:rows, 2 * head :]
    gated[...] = result.astype(BF16).reshape(gated.shape)
    for pair in range(own.shape[0]):
        own[pair] = gated[:, pair, pl.ds(core_at, 1)].reshape(own.shape[1:])
        other[pair] = gated[:, pair, pl.ds(1 - core_at, 1)].reshape(own.shape[1:])


def regroup(own, sibling, *outs):
    mine = lax.rem(lax.axis_index("head") // 2, own.shape[0])
    for flip, out in enumerate(outs):
        at = mine ^ flip
        out[0] = own[pl.ds(at, 1)].reshape(out.shape[1:])
        out[1] = sibling[pl.ds(at, 1)].reshape(out.shape[1:])


def spread(part, w_one, w_two, *refs):
    rest, held, out, left = refs[:-3], refs[-3], refs[-2], refs[-1]
    turn(part, left)
    joined = jnp.concatenate([w_one[...], w_two[...]], axis=0)
    out[...] = jnp.dot(left[...], joined, preferred_element_type=F32)
    head = w_one.shape[0]
    for at, ref in enumerate(rest):
        held[at * head : (at + 1) * head] = ref[...]


def turn(part, left):
    mine = lax.axis_index("head") // SUBS
    sides, zs, rows, head = part.shape
    for side in range(sides):
        for k in range(zs):
            piece = part[side, pl.ds(mine ^ k, 1)].reshape(rows, head)
            left[k * rows : (k + 1) * rows, side * head : (side + 1) * head] = piece


def combine(begun, *refs):
    parts, (held, w_one, w_two, out, left) = refs[:3], refs[3:]
    total = begun[...]
    depth = left.shape[-1]
    for which, part in enumerate(parts):
        turn(part, left.at[which])
        if which > 0:
            weight = held[(which - 1) * depth : which * depth]
        else:
            weight = jnp.concatenate([w_one[...], w_two[...]], axis=0)
        total = total + jnp.dot(left[which], weight, preferred_element_type=F32)
    out[...] = total.astype(BF16).reshape(out.shape)


def on_device(
    tokens, w_qkv, conv_weight, f_down, f_up, dt_bias, a_log, w_beta, o_down, o_up, norm_gain, w_out
):
    rows, model = tokens.shape
    head = f_up.shape[1]
    ctx_count, head_count = lax.axis_size("ctx"), lax.axis_size("head")
    zs = head_count // SUBS
    shape = jax.ShapeDtypeStruct
    dma = pltpu.SemaphoreType.DMA

    def flip(value, mask):
        return lax.ppermute(value, "head", [(h, h ^ mask) for h in range(head_count)])

    w3 = jnp.transpose(w_qkv, (1, 0, 2))
    taps = jnp.transpose(conv_weight, (1, 0, 2))
    edge = tokens[rows - 16 :]
    with jax.named_scope("rim"):
        rim = lax.ppermute(edge, "ctx", [(i, (i + 1) % ctx_count) for i in range(ctx_count)])
    (w_sent,) = after((w_out,), edge)
    with jax.named_scope("weights"):
        w_far, w_next = flip(w_sent, 2), flip(w_sent, 4)
    with jax.named_scope("front"):
        pack, sends = pl.pallas_call(
            front,
            in_specs=[HBM] * 11,
            out_specs=[HBM] * 2,
            out_shape=[
                shape((rows + head, 3 * head), F32),
                shape((ctx_count, head, 2 * head), BF16),
            ],
            scratch_shapes=[
                pltpu.VMEM((rows + 16, model), BF16),
                pltpu.VMEM((3, model, head), BF16),
                pltpu.VMEM((model, head), BF16),
                pltpu.VMEM((model, head), BF16),
                pltpu.VMEM((model, head), BF16),
                pltpu.VMEM((head, head), BF16),
                pltpu.VMEM((head, head), BF16),
                pltpu.VMEM((1, head), F32),
                pltpu.VMEM((1, model), BF16),
                pltpu.VMEM(taps.shape, F32),
                pltpu.VMEM((1, 1), F32),
                pltpu.VMEM((rows + 16, 6 * head), F32),
                pltpu.VMEM((rows + 8, 3 * head), F32),
                pltpu.VMEM((head, 2 * head), BF16),
                pltpu.VMEM((rows + head, 3 * head), F32),
                dma((7 + 6 * CHUNKS,)),
                dma((ctx_count,)),
                dma((2 + rows // GROUP,)),
            ],
            compiler_params=FULL,
            cost_estimate=cost(9, 40),
        )(
            tokens,
            rim,
            a_log.reshape(1, 1),
            w3,
            f_down,
            o_down,
            f_up,
            o_up,
            dt_bias.reshape(1, head),
            w_beta.reshape(1, model),
            taps,
        )
    with jax.named_scope("states"):
        states = lax.all_to_all(sends, "ctx", 0, 0, tiled=True)
    (w_early,) = after((w_far,), pack)
    with jax.named_scope("weights"):
        w_both = flip(w_early, 4)
    with jax.named_scope("stage"):
        staged = pl.pallas_call(
            stage,
            in_specs=[VMEM] * 2,
            out_specs=VMEM,
            out_shape=shape(pack.shape, F32),
            compiler_params=LIMIT,
            cost_estimate=cost(0.5, 0),
        )(pack, norm_gain.reshape(1, head))
    w_late, w_near, w_mine = after((w_far, w_next, w_out), staged)
    with jax.named_scope("weights"):
        w_core, w_far_core, w_next_core = flip(w_mine, 1), flip(w_late, 1), flip(w_near, 1)
    with jax.named_scope("finish"):
        own, other = pl.pallas_call(
            finish,
            in_specs=[VMEM] * 2,
            out_specs=[VMEM] * 2,
            out_shape=[shape((SUBS // 2, zs, 16, head), BF16)] * 2,
            scratch_shapes=[pltpu.VMEM((zs, SUBS // 2, 2, 16, head), BF16)],
            compiler_params=LIMIT,
            cost_estimate=cost(2, 0.5),
        )(staged, states)
    with jax.named_scope("exchange"):
        sibling = flip(other, 1)
        kept, *sent = pl.pallas_call(
            regroup,
            in_specs=[VMEM] * 2,
            out_specs=[VMEM] * 4,
            out_shape=[shape((2, zs, 16, head), BF16)] * 4,
            compiler_params=LIMIT,
            cost_estimate=cost(0.5, 0),
        )(own, sibling)
        got = {f: flip(sent[f - 1], 2 * f) for f in (3, 1, 2)}
    with jax.named_scope("spread"):
        held, begun = pl.pallas_call(
            spread,
            in_specs=[VMEM] * 7,
            out_specs=[VMEM] * 2,
            out_shape=[shape((4 * head, model), BF16), shape((zs * 16, model), F32)],
            scratch_shapes=[pltpu.VMEM((zs * 16, 2 * head), BF16)],
            compiler_params=LIMIT,
            cost_estimate=cost(2, 0),
        )(kept, w_out, w_core, w_far, w_far_core, w_next, w_next_core)
        (w_late,) = after((w_both,), kept)
        w_both_core = flip(w_late, 1)
        parts = pl.pallas_call(
            combine,
            in_specs=[VMEM] * 7,
            out_specs=VMEM,
            out_shape=shape((zs, 16, model), BF16),
            scratch_shapes=[pltpu.VMEM((3, zs * 16, 2 * head), BF16)],
            compiler_params=LIMIT,
            cost_estimate=cost(1, 0),
        )(begun, got[3], got[1], got[2], held, w_both, w_both_core)
    with jax.named_scope("reduce"):
        total = parts[0].astype(F32)
        for part in [flip(parts[k], SUBS * k) for k in (2, 1, 3)]:
            total = total + part.astype(F32)
        return total.astype(BF16)


def after(values, token):
    return lax.optimization_barrier((*values, token))[: len(values)]


def solution(mesh):
    in_specs = (
        P("ctx", None),
        P(None, None, "head"),
        P(None, None, "head"),
        P(),
        P(None, "head"),
        P("head"),
        P("head"),
        P(None, "head"),
        P(),
        P(None, "head"),
        P(),
        P("head", None),
    )
    out_specs = P(("ctx", "head"), None)
    return jax.shard_map(
        on_device, mesh=mesh, in_specs=in_specs, out_specs=out_specs, check_vma=False
    )
```

```python
import functools

import jax
import jax.numpy as jnp
from jax import lax
from jax.experimental import pallas as pl
from jax.experimental.pallas import tpu as pltpu
from jax.sharding import PartitionSpec as P

BLOCK = 64
GROUP = 128
SPAN = 256
SUBS = 8
CHUNKS = 3
F32 = jnp.float32
BF16 = jnp.bfloat16
HIGHEST = lax.Precision.HIGHEST
VMEM = pl.BlockSpec(memory_space=pltpu.VMEM)
HBM = pl.BlockSpec(memory_space=pltpu.HBM)
SMEM = pl.BlockSpec(memory_space=pltpu.SMEM)
FULL = pltpu.CompilerParams(vmem_limit_bytes=62 * 1024 * 1024)
LIMIT = pltpu.CompilerParams(vmem_limit_bytes=16 * 1024 * 1024)


def cost(us, flops=0):
    return pl.CostEstimate(
        flops=int(flops * 1_000_000_000), bytes_accessed=int(us * 3_690_000), transcendentals=0
    )


def mm(left, right):
    return jnp.dot(left.astype(BF16), right.astype(BF16), preferred_element_type=F32)


def mm_nt(left, right):
    return lax.dot_general(
        left.astype(BF16), right.astype(BF16), (((1,), (1,)), ((), ())), preferred_element_type=F32
    )


def mm_tn(left, right):
    return lax.dot_general(
        left.astype(BF16), right.astype(BF16), (((0,), (0,)), ((), ())), preferred_element_type=F32
    )


def split(value):
    high = value.astype(BF16)
    return high, (value - high.astype(F32)).astype(BF16)


def mm3(left, right):
    lh, ll = split(left)
    rh, rl = split(right)
    dot = functools.partial(jnp.dot, preferred_element_type=F32)
    return dot(lh, rh) + (dot(lh, rl) + dot(ll, rh))


def masks(size):
    row = lax.broadcasted_iota(jnp.int32, (size, size), 0)
    col = lax.broadcasted_iota(jnp.int32, (size, size), 1)
    return row, col, row ^ col


def load(pairs, sems):
    copies = []
    for place, (source, target) in enumerate(pairs):
        copies.append(pltpu.make_async_copy(source, target, sems.at[place]))
        copies[-1].start()
    return copies


def convolve(total, taps, padded, rows, part):
    head = taps.shape[2]
    conv_taps = taps.shape[1]
    lanes = slice(part * head, (part + 1) * head)
    edge = total[rows:, lanes].astype(BF16).astype(F32)[total.shape[0] - rows - 8 :]
    padded[0:8, lanes] = jnp.where(lax.axis_index("ctx") > 0, edge, 0.0)
    padded[8:, lanes] = total[:rows, lanes].astype(BF16).astype(F32)
    mixed = padded[9 - conv_taps : 9 - conv_taps + rows, lanes] * taps[part, 0:1, :]
    for tap in range(1, conv_taps):
        start = 9 - conv_taps + tap
        mixed = mixed + padded[start : start + rows, lanes] * taps[part, tap : tap + 1, :]
    return jax.nn.silu(mixed)


def unit_rows(value):
    return value * lax.rsqrt(jnp.sum(value * value, axis=-1, keepdims=True) + 1e-06)


def front(
    tokens_hbm, rim_hbm, alog_hbm, w3_hbm, f_down_hbm, o_down_hbm, f_up_hbm, o_up_hbm, bias_hbm,
    w_beta_hbm, taps_hbm, pack_hbm, sends, tok, w3, f_down, o_down,
    wide, f_up, o_up, bias, w_beta, taps, alog, total, padded, final, pack, sems, out_sems, pack_sems,
):
    rows, model = tokens_hbm.shape
    head = f_up.shape[0]
    count = rows // BLOCK
    inside = SPAN // BLOCK
    chunk = model // CHUNKS
    pairs = [(w_beta_hbm, w_beta), (rim_hbm, tok.at[pl.ds(rows, rim_hbm.shape[0])])]
    for step in range(CHUNKS):
        rng = pl.ds(step * chunk, chunk)
        pairs.append((tokens_hbm.at[:, rng], tok.at[pl.ds(0, rows), rng]))
        pairs += [(w3_hbm.at[part, rng], w3.at[part, rng]) for part in range(3)]
        pairs.append((f_down_hbm.at[rng], f_down.at[rng]))
        pairs.append((o_down_hbm.at[rng], o_down.at[rng]))
    pairs += [(f_up_hbm, f_up), (o_up_hbm, o_up), (bias_hbm, bias), (taps_hbm, taps)]
    pairs.append((alog_hbm, alog))
    copies = load(pairs, sems)
    wide[...] = jnp.zeros_like(wide)
    copies[0].wait()
    column = jnp.transpose(jnp.broadcast_to(w_beta[...].astype(F32), (8, model)))
    wide[:, 0:8] = column.astype(BF16)
    copies[1].wait()
    for step in range(CHUNKS):
        for copy in copies[2 + 6 * step : 8 + 6 * step]:
            copy.wait()
        rng = slice(step * chunk, (step + 1) * chunk)
        joined = [w3[part, rng] for part in range(3)] + [f_down[rng], o_down[rng], wide[rng]]
        piece = jnp.dot(tok[:, rng], jnp.concatenate(joined, axis=1), preferred_element_type=F32)
        if step == 0:
            total[...] = piece
        else:
            total[...] += piece
    for copy in copies[2 + 6 * CHUNKS :]:
        copy.wait()
    low = total[:rows, 3 * head : 4 * head].astype(BF16)
    logit = jnp.dot(low, f_up[...], preferred_element_type=F32) + bias[...]
    decays = -jnp.exp(alog[...]) * jax.nn.softplus(logit)
    out_low = total[:rows, 4 * head : 5 * head].astype(BF16)
    pack[:rows, 2 * head :] = jax.nn.sigmoid(jnp.dot(out_low, o_up[...], preferred_element_type=F32))
    stores = []

    def store(at):
        stores.append(pltpu.make_async_copy(pack.at[at], pack_hbm.at[at], pack_sems.at[len(stores)]))
        stores[-1].start()

    store((pl.ds(0, rows), pl.ds(2 * head, head)))
    beta = jnp.broadcast_to(jax.nn.sigmoid(total[:rows, 5 * head : 5 * head + 1]), (rows, head))
    row, col, differ = masks(GROUP)
    strict = (row > col) & (differ < BLOCK)
    causal = (row >= col) & (differ < BLOCK)
    unit = jnp.where(row == col, 1.0, 0.0).astype(F32)
    tri = jnp.where(causal, 1.0, 0.0).astype(BF16)
    high, rest = split(decays)
    middle, least = split(decays - high.astype(F32) - rest.astype(F32))
    terms = jnp.concatenate([high, rest, middle], axis=1)
    sums = [
        jnp.dot(tri, terms[s : s + GROUP], preferred_element_type=F32) for s in range(0, rows, GROUP)
    ]
    sums = jnp.concatenate(sums, axis=0)
    cumulative = sums[:, :head] + (sums[:, head : 2 * head] + sums[:, 2 * head :])
    key_raw = convolve(total, taps, padded, rows, 1)
    value_raw = convolve(total, taps, padded, rows, 2)
    query_raw = convolve(total, taps, padded, rows, 0)
    keyset = unit_rows(key_raw).astype(BF16).astype(F32)
    values = value_raw.astype(BF16).astype(F32)
    rising = jnp.exp(cumulative)
    key_rise = keyset * rising
    key_fall = (keyset * jnp.exp(-cumulative)).astype(BF16)
    blocked = cumulative.reshape(count, BLOCK, head)
    ends = blocked[:, BLOCK - 1 : BLOCK, :]
    tail = (keyset.reshape(count, BLOCK, head) * jnp.exp(ends - blocked)).reshape(rows, head)
    tail = tail.astype(BF16)
    shrink = jnp.transpose(jnp.exp(ends.reshape(count, head)))
    target = jnp.concatenate([beta * values, beta * key_rise], axis=1).astype(BF16)
    systems, inverse = [], []
    for start in range(0, rows, GROUP):
        rng = slice(start, start + GROUP)
        inner = mm_nt(key_rise[rng], key_fall[rng])
        systems.append(jnp.where(strict, inner * beta[rng], 0.0))
        inverse.append(unit - jnp.where(differ == 1, systems[-1], 0.0))
    size = 2
    while size < BLOCK:
        here = (differ >= size) & (differ < 2 * size)
        steps = [mm(jnp.where(here, s, 0.0), d) for s, d in zip(systems, inverse)]
        inverse = [d - mm(d, x) for d, x in zip(inverse, steps)]
        size *= 2
    pairs, solves, starts = [], [], {}
    for group, start in enumerate(range(0, rows, GROUP)):
        solved = mm(inverse[group], target[start : start + GROUP]).astype(BF16)
        solves.append(solved)
        for block in range(GROUP // BLOCK):
            sub = slice(block * BLOCK, (block + 1) * BLOCK)
            pairs.append(mm_tn(tail[start + block * BLOCK :][:BLOCK], solved[sub]))
    fresh = jnp.concatenate([jnp.zeros((head, head), F32), unit], axis=1)
    states = [fresh] * (rows // SPAN)
    for block in range(inside):
        for group in range(rows // SPAN):
            at = group * inside + block
            state = states[group]
            short = state.astype(BF16)
            starts[at] = short
            step = mm(pairs[at][:, head:], short)
            state = shrink[:, at : at + 1] * state - step
            states[group] = jnp.concatenate(
                [state[:, :head] + pairs[at][:, :head], state[:, head:]], axis=1
            )
    pack[rows:, : 2 * head] = states[0]
    store((pl.ds(rows, head), pl.ds(0, 2 * head)))
    whole = mm(states[1][:, head:], states[0])
    final[...] = jnp.concatenate(
        [whole[:, :head] + states[1][:, :head], whole[:, head:]], axis=1
    ).astype(BF16)
    copies = load([(final, sends.at[i]) for i in range(sends.shape[0])], out_sems)
    queries = (unit_rows(query_raw) * (head ** (-0.5))).astype(BF16).astype(F32)
    query_rise = queries * rising
    for group, start in enumerate(range(0, rows, GROUP)):
        rng = slice(start, start + GROUP)
        scores = jnp.where(causal, mm_nt(query_rise[rng], key_fall[rng]), 0.0)
        local = mm(scores, solves[group])
        local_key = (query_rise[rng] - local[:, head:]).astype(BF16)
        for block in range(GROUP // BLOCK):
            sub = slice(block * BLOCK, (block + 1) * BLOCK)
            out = slice(start + block * BLOCK, start + (block + 1) * BLOCK)
            across = jnp.dot(
                local_key[sub], starts[(start // BLOCK) + block], preferred_element_type=F32
            )
            pack[out, :head] = across[:, :head] + local[sub, :head]
            pack[out, head : 2 * head] = across[:, head:]
        store((pl.ds(start, GROUP), pl.ds(0, 2 * head)))
    for copy in copies + stores:
        copy.wait()


def stage(pack, gain, out):
    head = gain.shape[1]
    rows = pack.shape[0] - head
    out[:, : 2 * head] = pack[:, : 2 * head]
    out[:rows, 2 * head :] = pack[:rows, 2 * head :] * gain[...]


def finish(pack, states, own, other, gated):
    head = states.shape[1]
    rows = pack.shape[0] - head
    ctx = lax.axis_index("ctx")
    core_at = lax.rem(lax.axis_index("head"), 2)
    state = jnp.zeros((head, head), F32)
    for step in range(states.shape[0] - 1):
        moved = jnp.dot(states[step, :, head:], state.astype(BF16), preferred_element_type=F32)
        state = jnp.where(step < ctx, moved + states[step, :, :head].astype(F32), state)
    middle = mm(pack[rows:, head : 2 * head], state) + pack[rows:, :head]
    cores = []
    for group, start in enumerate((state, middle)):
        rng = slice(group * SPAN, (group + 1) * SPAN)
        cores.append(pack[rng, :head] + mm(pack[rng, head : 2 * head], start))
    core = jnp.concatenate(cores, axis=0)
    scale = lax.rsqrt(jnp.mean(core * core, axis=-1, keepdims=True) + 1e-05)
    result = core * scale * pack[:rows, 2 * head :]
    gated[...] = result.astype(BF16).reshape(gated.shape)
    for pair in range(own.shape[0]):
        own[pair] = gated[:, pair, pl.ds(core_at, 1)].reshape(own.shape[1:])
        other[pair] = gated[:, pair, pl.ds(1 - core_at, 1)].reshape(own.shape[1:])


def regroup(own, sibling, *outs):
    mine = lax.rem(lax.axis_index("head") // 2, own.shape[0])
    for flip, out in enumerate(outs):
        at = mine ^ flip
        out[0] = own[pl.ds(at, 1)].reshape(out.shape[1:])
        out[1] = sibling[pl.ds(at, 1)].reshape(out.shape[1:])


def spread(part, w_one, w_two, *refs):
    rest, held, out, left = refs[:-3], refs[-3], refs[-2], refs[-1]
    turn(part, left)
    joined = jnp.concatenate([w_one[...], w_two[...]], axis=0)
    out[...] = jnp.dot(left[...], joined, preferred_element_type=F32)
    head = w_one.shape[0]
    for at, ref in enumerate(rest):
        held[at * head : (at + 1) * head] = ref[...]


def turn(part, left):
    mine = lax.axis_index("head") // SUBS
    sides, zs, rows, head = part.shape
    for side in range(sides):
        for k in range(zs):
            piece = part[side, pl.ds(mine ^ k, 1)].reshape(rows, head)
            left[k * rows : (k + 1) * rows, side * head : (side + 1) * head] = piece


def combine(begun, *refs):
    parts, (held, w_one, w_two, out, left) = refs[:3], refs[3:]
    total = begun[...]
    depth = left.shape[-1]
    for which, part in enumerate(parts):
        turn(part, left.at[which])
        if which > 0:
            weight = held[(which - 1) * depth : which * depth]
        else:
            weight = jnp.concatenate([w_one[...], w_two[...]], axis=0)
        total = total + jnp.dot(left[which], weight, preferred_element_type=F32)
    out[...] = total.astype(BF16).reshape(out.shape)


def on_device(
    tokens, w_qkv, conv_weight, f_down, f_up, dt_bias, a_log, w_beta, o_down, o_up, norm_gain, w_out
):
    rows, model = tokens.shape
    head = f_up.shape[1]
    ctx_count, head_count = lax.axis_size("ctx"), lax.axis_size("head")
    zs = head_count // SUBS
    shape = jax.ShapeDtypeStruct
    dma = pltpu.SemaphoreType.DMA

    def across(value):
        half = ctx_count // 2
        pairs = [
            (c * head_count + h, ((c + half) % ctx_count) * head_count + (h ^ 2))
            for c in range(ctx_count)
            for h in range(head_count)
        ]
        return lax.ppermute(value, ("ctx", "head"), pairs)

    def flip(value, mask):
        return lax.ppermute(value, "head", [(h, h ^ mask) for h in range(head_count)])

    w3 = jnp.transpose(w_qkv, (1, 0, 2))
    taps = jnp.transpose(conv_weight, (1, 0, 2))
    edge = tokens[rows - 16 :]
    with jax.named_scope("rim"):
        rim = lax.ppermute(edge, "ctx", [(i, (i + 1) % ctx_count) for i in range(ctx_count)])
    (w_sent,) = after((w_out,), edge)
    with jax.named_scope("weights"):
        w_far, w_next = across(w_sent), flip(w_sent, 4)
    with jax.named_scope("front"):
        pack, sends = pl.pallas_call(
            front,
            in_specs=[HBM] * 11,
            out_specs=[HBM] * 2,
            out_shape=[
                shape((rows + head, 3 * head), F32),
                shape((ctx_count, head, 2 * head), BF16),
            ],
            scratch_shapes=[
                pltpu.VMEM((rows + 16, model), BF16),
                pltpu.VMEM((3, model, head), BF16),
                pltpu.VMEM((model, head), BF16),
                pltpu.VMEM((model, head), BF16),
                pltpu.VMEM((model, head), BF16),
                pltpu.VMEM((head, head), BF16),
                pltpu.VMEM((head, head), BF16),
                pltpu.VMEM((1, head), F32),
                pltpu.VMEM((1, model), BF16),
                pltpu.VMEM(taps.shape, F32),
                pltpu.VMEM((1, 1), F32),
                pltpu.VMEM((rows + 16, 6 * head), F32),
                pltpu.VMEM((rows + 8, 3 * head), F32),
                pltpu.VMEM((head, 2 * head), BF16),
                pltpu.VMEM((rows + head, 3 * head), F32),
                dma((7 + 6 * CHUNKS,)),
                dma((ctx_count,)),
                dma((2 + rows // GROUP,)),
            ],
            compiler_params=FULL,
            cost_estimate=cost(9, 40),
        )(
            tokens,
            rim,
            a_log.reshape(1, 1),
            w3,
            f_down,
            o_down,
            f_up,
            o_up,
            dt_bias.reshape(1, head),
            w_beta.reshape(1, model),
            taps,
        )
    with jax.named_scope("states"):
        states = lax.all_to_all(sends, "ctx", 0, 0, tiled=True)
    (w_early,) = after((w_far,), pack)
    with jax.named_scope("weights"):
        w_both = flip(w_early, 4)
    with jax.named_scope("stage"):
        staged = pl.pallas_call(
            stage,
            in_specs=[VMEM] * 2,
            out_specs=VMEM,
            out_shape=shape(pack.shape, F32),
            compiler_params=LIMIT,
            cost_estimate=cost(0.5, 0.5),
        )(pack, norm_gain.reshape(1, head))
    w_late, w_near, w_mine = after((w_far, w_next, w_out), staged)
    with jax.named_scope("weights"):
        w_core, w_far_core, w_next_core = flip(w_mine, 1), flip(w_late, 1), flip(w_near, 1)
    with jax.named_scope("finish"):
        own, other = pl.pallas_call(
            finish,
            in_specs=[VMEM] * 2,
            out_specs=[VMEM] * 2,
            out_shape=[shape((SUBS // 2, zs, 16, head), BF16)] * 2,
            scratch_shapes=[pltpu.VMEM((zs, SUBS // 2, 2, 16, head), BF16)],
            compiler_params=LIMIT,
            cost_estimate=cost(2, 2),
        )(staged, states)
    with jax.named_scope("exchange"):
        sibling = flip(other, 1)
        kept, *sent = pl.pallas_call(
            regroup,
            in_specs=[VMEM] * 2,
            out_specs=[VMEM] * 4,
            out_shape=[shape((2, zs, 16, head), BF16)] * 4,
            compiler_params=LIMIT,
            cost_estimate=cost(0.5, 0.5),
        )(own, sibling)
        got = {f: flip(sent[f - 1], 2 * f) for f in (3, 1, 2)}
    with jax.named_scope("spread"):
        held, begun = pl.pallas_call(
            spread,
            in_specs=[VMEM] * 7,
            out_specs=[VMEM] * 2,
            out_shape=[shape((4 * head, model), BF16), shape((zs * 16, model), F32)],
            scratch_shapes=[pltpu.VMEM((zs * 16, 2 * head), BF16)],
            compiler_params=LIMIT,
            cost_estimate=cost(2, 2),
        )(kept, w_out, w_core, w_far, w_far_core, w_next, w_next_core)
        (w_late,) = after((w_both,), kept)
        w_both_core = flip(w_late, 1)
        parts = pl.pallas_call(
            combine,
            in_specs=[VMEM] * 7,
            out_specs=VMEM,
            out_shape=shape((zs, 16, model), BF16),
            scratch_shapes=[pltpu.VMEM((3, zs * 16, 2 * head), BF16)],
            compiler_params=LIMIT,
            cost_estimate=cost(1, 1),
        )(begun, got[3], got[1], got[2], held, w_both, w_both_core)
    with jax.named_scope("reduce"):
        total = parts[0].astype(F32)
        for part in [flip(parts[k], SUBS * k) for k in (2, 1, 3)]:
            total = total + part.astype(F32)
        return total.astype(BF16)


def after(values, token):
    return lax.optimization_barrier((*values, token))[: len(values)]


def solution(mesh):
    in_specs = (
        P("ctx", None),
        P(None, None, "head"),
        P(None, None, "head"),
        P(),
        P(None, "head"),
        P("head"),
        P("head"),
        P(None, "head"),
        P(),
        P(None, "head"),
        P(),
        P("head", None),
    )
    out_specs = P(("ctx", "head"), None)
    return jax.shard_map(
        on_device, mesh=mesh, in_specs=in_specs, out_specs=out_specs, check_vma=False
    )
```

```python
import functools

import jax
import jax.numpy as jnp
from jax import lax
from jax.experimental import pallas as pl
from jax.experimental.pallas import tpu as pltpu
from jax.sharding import PartitionSpec as P

BLOCK = 64
GROUP = 128
SPAN = 256
SUBS = 8
CHUNKS = 3
F32 = jnp.float32
BF16 = jnp.bfloat16
HIGHEST = lax.Precision.HIGHEST
VMEM = pl.BlockSpec(memory_space=pltpu.VMEM)
HBM = pl.BlockSpec(memory_space=pltpu.HBM)
SMEM = pl.BlockSpec(memory_space=pltpu.SMEM)
FULL = pltpu.CompilerParams(vmem_limit_bytes=62 * 1024 * 1024)
LIMIT = pltpu.CompilerParams(vmem_limit_bytes=16 * 1024 * 1024)


def cost(us, flops=0):
    return pl.CostEstimate(
        flops=int(flops * 1_000_000_000), bytes_accessed=int(us * 3_690_000), transcendentals=0
    )


def mm(left, right):
    return jnp.dot(left.astype(BF16), right.astype(BF16), preferred_element_type=F32)


def mm_nt(left, right):
    return lax.dot_general(
        left.astype(BF16), right.astype(BF16), (((1,), (1,)), ((), ())), preferred_element_type=F32
    )


def mm_tn(left, right):
    return lax.dot_general(
        left.astype(BF16), right.astype(BF16), (((0,), (0,)), ((), ())), preferred_element_type=F32
    )


def split(value):
    high = value.astype(BF16)
    return high, (value - high.astype(F32)).astype(BF16)


def mm3(left, right):
    lh, ll = split(left)
    rh, rl = split(right)
    dot = functools.partial(jnp.dot, preferred_element_type=F32)
    return dot(lh, rh) + (dot(lh, rl) + dot(ll, rh))


def masks(size):
    row = lax.broadcasted_iota(jnp.int32, (size, size), 0)
    col = lax.broadcasted_iota(jnp.int32, (size, size), 1)
    return row, col, row ^ col


def load(pairs, sems):
    copies = []
    for place, (source, target) in enumerate(pairs):
        copies.append(pltpu.make_async_copy(source, target, sems.at[place]))
        copies[-1].start()
    return copies


def convolve(total, taps, padded, rows, part):
    head = taps.shape[2]
    conv_taps = taps.shape[1]
    lanes = slice(part * head, (part + 1) * head)
    edge = total[rows:, lanes].astype(BF16).astype(F32)[total.shape[0] - rows - 8 :]
    padded[0:8, lanes] = jnp.where(lax.axis_index("ctx") > 0, edge, 0.0)
    padded[8:, lanes] = total[:rows, lanes].astype(BF16).astype(F32)
    mixed = padded[9 - conv_taps : 9 - conv_taps + rows, lanes] * taps[part, 0:1, :]
    for tap in range(1, conv_taps):
        start = 9 - conv_taps + tap
        mixed = mixed + padded[start : start + rows, lanes] * taps[part, tap : tap + 1, :]
    return jax.nn.silu(mixed)


def unit_rows(value):
    return value * lax.rsqrt(jnp.sum(value * value, axis=-1, keepdims=True) + 1e-06)


def front(
    tokens_hbm, rim_hbm, alog_hbm, w3_hbm, f_down_hbm, o_down_hbm, f_up_hbm, o_up_hbm, bias_hbm,
    w_beta_hbm, taps_hbm, pack_hbm, sends, tok, w3, f_down, o_down,
    wide, f_up, o_up, bias, w_beta, taps, alog, total, padded, final, pack, sems, out_sems, pack_sems,
):
    rows, model = tokens_hbm.shape
    head = f_up.shape[0]
    count = rows // BLOCK
    inside = SPAN // BLOCK
    chunk = model // CHUNKS
    pairs = [(w_beta_hbm, w_beta), (rim_hbm, tok.at[pl.ds(rows, rim_hbm.shape[0])])]
    for step in range(CHUNKS):
        rng = pl.ds(step * chunk, chunk)
        pairs.append((tokens_hbm.at[:, rng], tok.at[pl.ds(0, rows), rng]))
        pairs += [(w3_hbm.at[part, rng], w3.at[part, rng]) for part in range(3)]
        pairs.append((f_down_hbm.at[rng], f_down.at[rng]))
        pairs.append((o_down_hbm.at[rng], o_down.at[rng]))
    pairs += [(f_up_hbm, f_up), (o_up_hbm, o_up), (bias_hbm, bias), (taps_hbm, taps)]
    pairs.append((alog_hbm, alog))
    copies = load(pairs, sems)
    wide[...] = jnp.zeros_like(wide)
    copies[0].wait()
    column = jnp.transpose(jnp.broadcast_to(w_beta[...].astype(F32), (8, model)))
    wide[:, 0:8] = column.astype(BF16)
    copies[1].wait()
    for step in range(CHUNKS):
        for copy in copies[2 + 6 * step : 8 + 6 * step]:
            copy.wait()
        rng = slice(step * chunk, (step + 1) * chunk)
        joined = [w3[part, rng] for part in range(3)] + [f_down[rng], o_down[rng], wide[rng]]
        piece = jnp.dot(tok[:, rng], jnp.concatenate(joined, axis=1), preferred_element_type=F32)
        if step == 0:
            total[...] = piece
        else:
            total[...] += piece
    for copy in copies[2 + 6 * CHUNKS :]:
        copy.wait()
    low = total[:rows, 3 * head : 4 * head].astype(BF16)
    logit = jnp.dot(low, f_up[...], preferred_element_type=F32) + bias[...]
    decays = -jnp.exp(alog[...]) * jax.nn.softplus(logit)
    out_low = total[:rows, 4 * head : 5 * head].astype(BF16)
    pack[:rows, 2 * head :] = jax.nn.sigmoid(jnp.dot(out_low, o_up[...], preferred_element_type=F32))
    stores = []

    def store(at):
        stores.append(pltpu.make_async_copy(pack.at[at], pack_hbm.at[at], pack_sems.at[len(stores)]))
        stores[-1].start()

    store((pl.ds(0, rows), pl.ds(2 * head, head)))
    beta = jnp.broadcast_to(jax.nn.sigmoid(total[:rows, 5 * head : 5 * head + 1]), (rows, head))
    row, col, differ = masks(GROUP)
    strict = (row > col) & (differ < BLOCK)
    causal = (row >= col) & (differ < BLOCK)
    unit = jnp.where(row == col, 1.0, 0.0).astype(F32)
    tri = jnp.where(causal, 1.0, 0.0).astype(BF16)
    high, rest = split(decays)
    middle, least = split(decays - high.astype(F32) - rest.astype(F32))
    terms = jnp.concatenate([high, rest, middle], axis=1)
    sums = [
        jnp.dot(tri, terms[s : s + GROUP], preferred_element_type=F32) for s in range(0, rows, GROUP)
    ]
    sums = jnp.concatenate(sums, axis=0)
    cumulative = sums[:, :head] + (sums[:, head : 2 * head] + sums[:, 2 * head :])
    key_raw = convolve(total, taps, padded, rows, 1)
    value_raw = convolve(total, taps, padded, rows, 2)
    query_raw = convolve(total, taps, padded, rows, 0)
    keyset = unit_rows(key_raw).astype(BF16).astype(F32)
    values = value_raw.astype(BF16).astype(F32)
    rising = jnp.exp(cumulative)
    key_rise = keyset * rising
    key_fall = (keyset * jnp.exp(-cumulative)).astype(BF16)
    blocked = cumulative.reshape(count, BLOCK, head)
    ends = blocked[:, BLOCK - 1 : BLOCK, :]
    tail = (keyset.reshape(count, BLOCK, head) * jnp.exp(ends - blocked)).reshape(rows, head)
    tail = tail.astype(BF16)
    shrink = jnp.transpose(jnp.exp(ends.reshape(count, head)))
    target = jnp.concatenate([beta * values, beta * key_rise], axis=1).astype(BF16)
    systems, inverse = [], []
    for start in range(0, rows, GROUP):
        rng = slice(start, start + GROUP)
        inner = mm_nt(key_rise[rng], key_fall[rng])
        systems.append(jnp.where(strict, inner * beta[rng], 0.0))
        inverse.append(unit - jnp.where(differ == 1, systems[-1], 0.0))
    size = 2
    while size < BLOCK:
        here = (differ >= size) & (differ < 2 * size)
        steps = [mm(jnp.where(here, s, 0.0), d) for s, d in zip(systems, inverse)]
        inverse = [d - mm(d, x) for d, x in zip(inverse, steps)]
        size *= 2
    pairs, solves, starts = [], [], {}
    for group, start in enumerate(range(0, rows, GROUP)):
        solved = mm(inverse[group], target[start : start + GROUP]).astype(BF16)
        solves.append(solved)
        for block in range(GROUP // BLOCK):
            sub = slice(block * BLOCK, (block + 1) * BLOCK)
            pairs.append(mm_tn(tail[start + block * BLOCK :][:BLOCK], solved[sub]))
    fresh = jnp.concatenate([jnp.zeros((head, head), F32), unit], axis=1)
    states = [fresh] * (rows // SPAN)
    for block in range(inside):
        for group in range(rows // SPAN):
            at = group * inside + block
            state = states[group]
            short = state.astype(BF16)
            starts[at] = short
            step = mm(pairs[at][:, head:], short)
            state = shrink[:, at : at + 1] * state - step
            states[group] = jnp.concatenate(
                [state[:, :head] + pairs[at][:, :head], state[:, head:]], axis=1
            )
    pack[rows:, : 2 * head] = states[0]
    store((pl.ds(rows, head), pl.ds(0, 2 * head)))
    whole = mm(states[1][:, head:], states[0])
    final[...] = jnp.concatenate(
        [whole[:, :head] + states[1][:, :head], whole[:, head:]], axis=1
    ).astype(BF16)
    copies = load([(final, sends.at[i]) for i in range(sends.shape[0])], out_sems)
    queries = (unit_rows(query_raw) * (head ** (-0.5))).astype(BF16).astype(F32)
    query_rise = queries * rising
    for group, start in enumerate(range(0, rows, GROUP)):
        rng = slice(start, start + GROUP)
        scores = jnp.where(causal, mm_nt(query_rise[rng], key_fall[rng]), 0.0)
        local = mm(scores, solves[group])
        local_key = (query_rise[rng] - local[:, head:]).astype(BF16)
        for block in range(GROUP // BLOCK):
            sub = slice(block * BLOCK, (block + 1) * BLOCK)
            out = slice(start + block * BLOCK, start + (block + 1) * BLOCK)
            across = jnp.dot(
                local_key[sub], starts[(start // BLOCK) + block], preferred_element_type=F32
            )
            pack[out, :head] = across[:, :head] + local[sub, :head]
            pack[out, head : 2 * head] = across[:, head:]
        store((pl.ds(start, GROUP), pl.ds(0, 2 * head)))
    for copy in copies + stores:
        copy.wait()


def stage(pack, gain, out):
    head = gain.shape[1]
    rows = pack.shape[0] - head
    out[:, : 2 * head] = pack[:, : 2 * head]
    out[:rows, 2 * head :] = pack[:rows, 2 * head :] * gain[...]


def finish(pack, states, own, other, gated):
    head = states.shape[1]
    rows = pack.shape[0] - head
    ctx = lax.axis_index("ctx")
    core_at = lax.rem(lax.axis_index("head"), 2)
    state = jnp.zeros((head, head), F32)
    for step in range(states.shape[0] - 1):
        moved = jnp.dot(states[step, :, head:], state.astype(BF16), preferred_element_type=F32)
        state = jnp.where(step < ctx, moved + states[step, :, :head].astype(F32), state)
    middle = mm(pack[rows:, head : 2 * head], state) + pack[rows:, :head]
    cores = []
    for group, start in enumerate((state, middle)):
        rng = slice(group * SPAN, (group + 1) * SPAN)
        cores.append(pack[rng, :head] + mm(pack[rng, head : 2 * head], start))
    core = jnp.concatenate(cores, axis=0)
    scale = lax.rsqrt(jnp.mean(core * core, axis=-1, keepdims=True) + 1e-05)
    result = core * scale * pack[:rows, 2 * head :]
    gated[...] = result.astype(BF16).reshape(gated.shape)
    for pair in range(own.shape[0]):
        own[pair] = gated[:, pair, pl.ds(core_at, 1)].reshape(own.shape[1:])
        other[pair] = gated[:, pair, pl.ds(1 - core_at, 1)].reshape(own.shape[1:])


def regroup(own, sibling, *outs):
    mine = lax.rem(lax.axis_index("head") // 2, own.shape[0])
    for flip, out in enumerate(outs):
        at = mine ^ flip
        out[0] = own[pl.ds(at, 1)].reshape(out.shape[1:])
        out[1] = sibling[pl.ds(at, 1)].reshape(out.shape[1:])


def spread(part, w_one, w_two, *refs):
    rest, held, out, left = refs[:-3], refs[-3], refs[-2], refs[-1]
    turn(part, left)
    joined = jnp.concatenate([w_one[...], w_two[...]], axis=0)
    out[...] = jnp.dot(left[...], joined, preferred_element_type=F32)
    head = w_one.shape[0]
    for at, ref in enumerate(rest):
        held[at * head : (at + 1) * head] = ref[...]


def turn(part, left):
    mine = lax.axis_index("head") // SUBS
    sides, zs, rows, head = part.shape
    for side in range(sides):
        for k in range(zs):
            piece = part[side, pl.ds(mine ^ k, 1)].reshape(rows, head)
            left[k * rows : (k + 1) * rows, side * head : (side + 1) * head] = piece


def combine(begun, *refs):
    parts, (held, w_one, w_two, out, left) = refs[:3], refs[3:]
    total = begun[...]
    depth = left.shape[-1]
    for which, part in enumerate(parts):
        turn(part, left.at[which])
        if which > 0:
            weight = held[(which - 1) * depth : which * depth]
        else:
            weight = jnp.concatenate([w_one[...], w_two[...]], axis=0)
        total = total + jnp.dot(left[which], weight, preferred_element_type=F32)
    out[...] = total.astype(BF16).reshape(out.shape)


def on_device(
    tokens, w_qkv, conv_weight, f_down, f_up, dt_bias, a_log, w_beta, o_down, o_up, norm_gain, w_out
):
    rows, model = tokens.shape
    head = f_up.shape[1]
    ctx_count, head_count = lax.axis_size("ctx"), lax.axis_size("head")
    zs = head_count // SUBS
    shape = jax.ShapeDtypeStruct
    dma = pltpu.SemaphoreType.DMA

    def across(value):
        half = ctx_count // 2
        pairs = [
            (c * head_count + h, ((c + half) % ctx_count) * head_count + (h ^ 2))
            for c in range(ctx_count)
            for h in range(head_count)
        ]
        return lax.ppermute(value, ("ctx", "head"), pairs)

    def flip(value, mask):
        return lax.ppermute(value, "head", [(h, h ^ mask) for h in range(head_count)])

    w3 = jnp.transpose(w_qkv, (1, 0, 2))
    taps = jnp.transpose(conv_weight, (1, 0, 2))
    edge = tokens[rows - 16 :]
    with jax.named_scope("rim"):
        rim = lax.ppermute(edge, "ctx", [(i, (i + 1) % ctx_count) for i in range(ctx_count)])
    (w_sent,) = after((w_out,), edge)
    with jax.named_scope("weights"):
        w_far, w_next = across(w_sent), flip(w_sent, 4)
    with jax.named_scope("front"):
        pack, sends = pl.pallas_call(
            front,
            in_specs=[HBM] * 11,
            out_specs=[HBM] * 2,
            out_shape=[
                shape((rows + head, 3 * head), F32),
                shape((ctx_count, head, 2 * head), BF16),
            ],
            scratch_shapes=[
                pltpu.VMEM((rows + 16, model), BF16),
                pltpu.VMEM((3, model, head), BF16),
                pltpu.VMEM((model, head), BF16),
                pltpu.VMEM((model, head), BF16),
                pltpu.VMEM((model, head), BF16),
                pltpu.VMEM((head, head), BF16),
                pltpu.VMEM((head, head), BF16),
                pltpu.VMEM((1, head), F32),
                pltpu.VMEM((1, model), BF16),
                pltpu.VMEM(taps.shape, F32),
                pltpu.VMEM((1, 1), F32),
                pltpu.VMEM((rows + 16, 6 * head), F32),
                pltpu.VMEM((rows + 8, 3 * head), F32),
                pltpu.VMEM((head, 2 * head), BF16),
                pltpu.VMEM((rows + head, 3 * head), F32),
                dma((7 + 6 * CHUNKS,)),
                dma((ctx_count,)),
                dma((2 + rows // GROUP,)),
            ],
            compiler_params=FULL,
            cost_estimate=cost(9, 40),
        )(
            tokens,
            rim,
            a_log.reshape(1, 1),
            w3,
            f_down,
            o_down,
            f_up,
            o_up,
            dt_bias.reshape(1, head),
            w_beta.reshape(1, model),
            taps,
        )
    with jax.named_scope("states"):
        states = lax.all_to_all(sends, "ctx", 0, 0, tiled=True)
    (w_early,) = after((w_far,), pack)
    with jax.named_scope("weights"):
        w_both = flip(w_early, 4)
    with jax.named_scope("stage"):
        staged = pl.pallas_call(
            stage,
            in_specs=[VMEM] * 2,
            out_specs=VMEM,
            out_shape=shape(pack.shape, F32),
            compiler_params=LIMIT,
            cost_estimate=cost(0.5, 0.5),
        )(pack, norm_gain.reshape(1, head))
    w_late, w_near, w_mine = after((w_far, w_next, w_out), staged)
    with jax.named_scope("weights"):
        w_core, w_far_core, w_next_core = flip(w_mine, 1), flip(w_late, 1), flip(w_near, 1)
    with jax.named_scope("finish"):
        own, other = pl.pallas_call(
            finish,
            in_specs=[VMEM] * 2,
            out_specs=[VMEM] * 2,
            out_shape=[shape((SUBS // 2, zs, 16, head), BF16)] * 2,
            scratch_shapes=[pltpu.VMEM((zs, SUBS // 2, 2, 16, head), BF16)],
            compiler_params=LIMIT,
            cost_estimate=cost(2, 0),
        )(staged, states)
    with jax.named_scope("exchange"):
        sibling = flip(other, 1)
        kept, *sent = pl.pallas_call(
            regroup,
            in_specs=[VMEM] * 2,
            out_specs=[VMEM] * 4,
            out_shape=[shape((2, zs, 16, head), BF16)] * 4,
            compiler_params=LIMIT,
            cost_estimate=cost(0.5, 0.5),
        )(own, sibling)
        got = {f: flip(sent[f - 1], 2 * f) for f in (3, 1, 2)}
    with jax.named_scope("spread"):
        held, begun = pl.pallas_call(
            spread,
            in_specs=[VMEM] * 7,
            out_specs=[VMEM] * 2,
            out_shape=[shape((4 * head, model), BF16), shape((zs * 16, model), F32)],
            scratch_shapes=[pltpu.VMEM((zs * 16, 2 * head), BF16)],
            compiler_params=LIMIT,
            cost_estimate=cost(2, 2),
        )(kept, w_out, w_core, w_far, w_far_core, w_next, w_next_core)
        (w_late,) = after((w_both,), kept)
        w_both_core = flip(w_late, 1)
        parts = pl.pallas_call(
            combine,
            in_specs=[VMEM] * 7,
            out_specs=VMEM,
            out_shape=shape((zs, 16, model), BF16),
            scratch_shapes=[pltpu.VMEM((3, zs * 16, 2 * head), BF16)],
            compiler_params=LIMIT,
            cost_estimate=cost(1, 1),
        )(begun, got[3], got[1], got[2], held, w_both, w_both_core)
    with jax.named_scope("reduce"):
        total = parts[0].astype(F32)
        for part in [flip(parts[k], SUBS * k) for k in (2, 1, 3)]:
            total = total + part.astype(F32)
        return total.astype(BF16)


def after(values, token):
    return lax.optimization_barrier((*values, token))[: len(values)]


def solution(mesh):
    in_specs = (
        P("ctx", None),
        P(None, None, "head"),
        P(None, None, "head"),
        P(),
        P(None, "head"),
        P("head"),
        P("head"),
        P(None, "head"),
        P(),
        P(None, "head"),
        P(),
        P("head", None),
    )
    out_specs = P(("ctx", "head"), None)
    return jax.shard_map(
        on_device, mesh=mesh, in_specs=in_specs, out_specs=out_specs, check_vma=False
    )
```

```python
import functools

import jax
import jax.numpy as jnp
from jax import lax
from jax.experimental import pallas as pl
from jax.experimental.pallas import tpu as pltpu
from jax.sharding import PartitionSpec as P

BLOCK = 64
GROUP = 128
SPAN = 256
SUBS = 8
CHUNKS = 3
F32 = jnp.float32
BF16 = jnp.bfloat16
HIGHEST = lax.Precision.HIGHEST
VMEM = pl.BlockSpec(memory_space=pltpu.VMEM)
HBM = pl.BlockSpec(memory_space=pltpu.HBM)
SMEM = pl.BlockSpec(memory_space=pltpu.SMEM)
FULL = pltpu.CompilerParams(vmem_limit_bytes=62 * 1024 * 1024)
LIMIT = pltpu.CompilerParams(vmem_limit_bytes=16 * 1024 * 1024)


def cost(us, flops=0):
    return pl.CostEstimate(
        flops=int(flops * 1_000_000_000), bytes_accessed=int(us * 3_690_000), transcendentals=0
    )


def mm(left, right):
    return jnp.dot(left.astype(BF16), right.astype(BF16), preferred_element_type=F32)


def mm_nt(left, right):
    return lax.dot_general(
        left.astype(BF16), right.astype(BF16), (((1,), (1,)), ((), ())), preferred_element_type=F32
    )


def mm_tn(left, right):
    return lax.dot_general(
        left.astype(BF16), right.astype(BF16), (((0,), (0,)), ((), ())), preferred_element_type=F32
    )


def split(value):
    high = value.astype(BF16)
    return high, (value - high.astype(F32)).astype(BF16)


def mm3(left, right):
    lh, ll = split(left)
    rh, rl = split(right)
    dot = functools.partial(jnp.dot, preferred_element_type=F32)
    return dot(lh, rh) + (dot(lh, rl) + dot(ll, rh))


def masks(size):
    row = lax.broadcasted_iota(jnp.int32, (size, size), 0)
    col = lax.broadcasted_iota(jnp.int32, (size, size), 1)
    return row, col, row ^ col


def load(pairs, sems):
    copies = []
    for place, (source, target) in enumerate(pairs):
        copies.append(pltpu.make_async_copy(source, target, sems.at[place]))
        copies[-1].start()
    return copies


def convolve(total, taps, padded, rows, part):
    head = taps.shape[2]
    conv_taps = taps.shape[1]
    lanes = slice(part * head, (part + 1) * head)
    edge = total[rows:, lanes].astype(BF16).astype(F32)[total.shape[0] - rows - 8 :]
    padded[0:8, lanes] = jnp.where(lax.axis_index("ctx") > 0, edge, 0.0)
    padded[8:, lanes] = total[:rows, lanes].astype(BF16).astype(F32)
    mixed = padded[9 - conv_taps : 9 - conv_taps + rows, lanes] * taps[part, 0:1, :]
    for tap in range(1, conv_taps):
        start = 9 - conv_taps + tap
        mixed = mixed + padded[start : start + rows, lanes] * taps[part, tap : tap + 1, :]
    return jax.nn.silu(mixed)


def unit_rows(value):
    return value * lax.rsqrt(jnp.sum(value * value, axis=-1, keepdims=True) + 1e-06)


def front(
    tokens_hbm, rim_hbm, alog_hbm, w3_hbm, f_down_hbm, o_down_hbm, f_up_hbm, o_up_hbm, bias_hbm,
    w_beta_hbm, taps_hbm, pack_hbm, sends, tok, w3, f_down, o_down,
    wide, f_up, o_up, bias, w_beta, taps, alog, total, padded, final, pack, sems, out_sems, pack_sems,
):
    rows, model = tokens_hbm.shape
    head = f_up.shape[0]
    count = rows // BLOCK
    inside = SPAN // BLOCK
    chunk = model // CHUNKS
    pairs = [(w_beta_hbm, w_beta), (rim_hbm, tok.at[pl.ds(rows, rim_hbm.shape[0])])]
    for step in range(CHUNKS):
        rng = pl.ds(step * chunk, chunk)
        pairs.append((tokens_hbm.at[:, rng], tok.at[pl.ds(0, rows), rng]))
        pairs += [(w3_hbm.at[part, rng], w3.at[part, rng]) for part in range(3)]
        pairs.append((f_down_hbm.at[rng], f_down.at[rng]))
        pairs.append((o_down_hbm.at[rng], o_down.at[rng]))
    pairs += [(f_up_hbm, f_up), (o_up_hbm, o_up), (bias_hbm, bias), (taps_hbm, taps)]
    pairs.append((alog_hbm, alog))
    copies = load(pairs, sems)
    wide[...] = jnp.zeros_like(wide)
    copies[0].wait()
    column = jnp.transpose(jnp.broadcast_to(w_beta[...].astype(F32), (8, model)))
    wide[:, 0:8] = column.astype(BF16)
    copies[1].wait()
    for step in range(CHUNKS):
        for copy in copies[2 + 6 * step : 8 + 6 * step]:
            copy.wait()
        rng = slice(step * chunk, (step + 1) * chunk)
        joined = [w3[part, rng] for part in range(3)] + [f_down[rng], o_down[rng], wide[rng]]
        piece = jnp.dot(tok[:, rng], jnp.concatenate(joined, axis=1), preferred_element_type=F32)
        if step == 0:
            total[...] = piece
        else:
            total[...] += piece
    for copy in copies[2 + 6 * CHUNKS :]:
        copy.wait()
    low = total[:rows, 3 * head : 4 * head].astype(BF16)
    logit = jnp.dot(low, f_up[...], preferred_element_type=F32) + bias[...]
    decays = -jnp.exp(alog[...]) * jax.nn.softplus(logit)
    out_low = total[:rows, 4 * head : 5 * head].astype(BF16)
    pack[:rows, 2 * head :] = jax.nn.sigmoid(jnp.dot(out_low, o_up[...], preferred_element_type=F32))
    stores = []

    def store(at):
        stores.append(pltpu.make_async_copy(pack.at[at], pack_hbm.at[at], pack_sems.at[len(stores)]))
        stores[-1].start()

    store((pl.ds(0, rows), pl.ds(2 * head, head)))
    beta = jnp.broadcast_to(jax.nn.sigmoid(total[:rows, 5 * head : 5 * head + 1]), (rows, head))
    row, col, differ = masks(GROUP)
    strict = (row > col) & (differ < BLOCK)
    causal = (row >= col) & (differ < BLOCK)
    unit = jnp.where(row == col, 1.0, 0.0).astype(F32)
    tri = jnp.where(causal, 1.0, 0.0).astype(BF16)
    high, rest = split(decays)
    middle, least = split(decays - high.astype(F32) - rest.astype(F32))
    terms = jnp.concatenate([high, rest, middle], axis=1)
    sums = [
        jnp.dot(tri, terms[s : s + GROUP], preferred_element_type=F32) for s in range(0, rows, GROUP)
    ]
    sums = jnp.concatenate(sums, axis=0)
    cumulative = sums[:, :head] + (sums[:, head : 2 * head] + sums[:, 2 * head :])
    key_raw = convolve(total, taps, padded, rows, 1)
    value_raw = convolve(total, taps, padded, rows, 2)
    query_raw = convolve(total, taps, padded, rows, 0)
    keyset = unit_rows(key_raw).astype(BF16).astype(F32)
    values = value_raw.astype(BF16).astype(F32)
    rising = jnp.exp(cumulative)
    key_rise = keyset * rising
    key_fall = (keyset * jnp.exp(-cumulative)).astype(BF16)
    blocked = cumulative.reshape(count, BLOCK, head)
    ends = blocked[:, BLOCK - 1 : BLOCK, :]
    tail = (keyset.reshape(count, BLOCK, head) * jnp.exp(ends - blocked)).reshape(rows, head)
    tail = tail.astype(BF16)
    shrink = jnp.transpose(jnp.exp(ends.reshape(count, head)))
    target = jnp.concatenate([beta * values, beta * key_rise], axis=1).astype(BF16)
    systems, inverse = [], []
    for start in range(0, rows, GROUP):
        rng = slice(start, start + GROUP)
        inner = mm_nt(key_rise[rng], key_fall[rng])
        systems.append(jnp.where(strict, inner * beta[rng], 0.0))
        inverse.append(unit - jnp.where(differ == 1, systems[-1], 0.0))
    size = 2
    while size < BLOCK:
        here = (differ >= size) & (differ < 2 * size)
        steps = [mm(jnp.where(here, s, 0.0), d) for s, d in zip(systems, inverse)]
        inverse = [d - mm(d, x) for d, x in zip(inverse, steps)]
        size *= 2
    pairs, solves, starts = [], [], {}
    for group, start in enumerate(range(0, rows, GROUP)):
        solved = mm(inverse[group], target[start : start + GROUP]).astype(BF16)
        solves.append(solved)
        for block in range(GROUP // BLOCK):
            sub = slice(block * BLOCK, (block + 1) * BLOCK)
            pairs.append(mm_tn(tail[start + block * BLOCK :][:BLOCK], solved[sub]))
    fresh = jnp.concatenate([jnp.zeros((head, head), F32), unit], axis=1)
    states = [fresh] * (rows // SPAN)
    for block in range(inside):
        for group in range(rows // SPAN):
            at = group * inside + block
            state = states[group]
            short = state.astype(BF16)
            starts[at] = short
            step = mm(pairs[at][:, head:], short)
            state = shrink[:, at : at + 1] * state - step
            states[group] = jnp.concatenate(
                [state[:, :head] + pairs[at][:, :head], state[:, head:]], axis=1
            )
    pack[rows:, : 2 * head] = states[0]
    store((pl.ds(rows, head), pl.ds(0, 2 * head)))
    whole = mm(states[1][:, head:], states[0])
    final[...] = jnp.concatenate(
        [whole[:, :head] + states[1][:, :head], whole[:, head:]], axis=1
    ).astype(BF16)
    copies = load([(final, sends)], out_sems)
    queries = (unit_rows(query_raw) * (head ** (-0.5))).astype(BF16).astype(F32)
    query_rise = queries * rising
    for group, start in enumerate(range(0, rows, GROUP)):
        rng = slice(start, start + GROUP)
        scores = jnp.where(causal, mm_nt(query_rise[rng], key_fall[rng]), 0.0)
        local = mm(scores, solves[group])
        local_key = (query_rise[rng] - local[:, head:]).astype(BF16)
        for block in range(GROUP // BLOCK):
            sub = slice(block * BLOCK, (block + 1) * BLOCK)
            out = slice(start + block * BLOCK, start + (block + 1) * BLOCK)
            across = jnp.dot(
                local_key[sub], starts[(start // BLOCK) + block], preferred_element_type=F32
            )
            pack[out, :head] = across[:, :head] + local[sub, :head]
            pack[out, head : 2 * head] = across[:, head:]
        store((pl.ds(start, GROUP), pl.ds(0, 2 * head)))
    for copy in copies + stores:
        copy.wait()


def fold(*refs):
    found, (before, total, held) = refs[:-3], refs[-3:]
    count = len(found)
    mine = lax.rem(lax.axis_index("ctx"), count)
    head = found[0].shape[0]
    for back, ref in enumerate(found):
        held[back] = ref[...]
    row = lax.broadcasted_iota(jnp.int32, (head, 2 * head), 0)
    col = lax.broadcasted_iota(jnp.int32, (head, 2 * head), 1)
    state = jnp.where(row + head == col, 1.0, 0.0).astype(F32)
    seen = state
    for step in range(count):
        seen = jnp.where(mine == step, state, seen)
        item = held[lax.rem(mine - step + count, count)]
        moved = jnp.dot(item[:, head:], state.astype(BF16), preferred_element_type=F32)
        state = jnp.concatenate(
            [moved[:, :head] + item[:, :head].astype(F32), moved[:, head:]], axis=1
        )
    before[...] = seen
    total[...] = state[:, :head].astype(BF16)


def stage(pack, gain, out):
    head = gain.shape[1]
    rows = pack.shape[0] - head
    out[:, : 2 * head] = pack[:, : 2 * head]
    out[:rows, 2 * head :] = pack[:rows, 2 * head :] * gain[...]


def finish(pack, before, came, own, other, gated):
    head = came.shape[0]
    rows = pack.shape[0] - head
    core_at = lax.rem(lax.axis_index("head"), 2)
    later = lax.axis_index("ctx") >= lax.axis_size("ctx") // 2
    state = jnp.where(later, came[...].astype(F32), 0.0)
    state = mm(before[:, head:], state) + before[:, :head]
    middle = mm(pack[rows:, head : 2 * head], state) + pack[rows:, :head]
    cores = []
    for group, start in enumerate((state, middle)):
        rng = slice(group * SPAN, (group + 1) * SPAN)
        cores.append(pack[rng, :head] + mm(pack[rng, head : 2 * head], start))
    core = jnp.concatenate(cores, axis=0)
    scale = lax.rsqrt(jnp.mean(core * core, axis=-1, keepdims=True) + 1e-05)
    result = core * scale * pack[:rows, 2 * head :]
    gated[...] = result.astype(BF16).reshape(gated.shape)
    for pair in range(own.shape[0]):
        own[pair] = gated[:, pair, pl.ds(core_at, 1)].reshape(own.shape[1:])
        other[pair] = gated[:, pair, pl.ds(1 - core_at, 1)].reshape(own.shape[1:])


def regroup(own, sibling, *outs):
    mine = lax.rem(lax.axis_index("head") // 2, own.shape[0])
    for flip, out in enumerate(outs):
        at = mine ^ flip
        out[0] = own[pl.ds(at, 1)].reshape(out.shape[1:])
        out[1] = sibling[pl.ds(at, 1)].reshape(out.shape[1:])


def spread(part, w_one, w_two, *refs):
    rest, held, out, left = refs[:-3], refs[-3], refs[-2], refs[-1]
    turn(part, left)
    joined = jnp.concatenate([w_one[...], w_two[...]], axis=0)
    out[...] = jnp.dot(left[...], joined, preferred_element_type=F32)
    head = w_one.shape[0]
    for at, ref in enumerate(rest):
        held[at * head : (at + 1) * head] = ref[...]


def turn(part, left):
    mine = lax.axis_index("head") // SUBS
    sides, zs, rows, head = part.shape
    for side in range(sides):
        for k in range(zs):
            piece = part[side, pl.ds(mine ^ k, 1)].reshape(rows, head)
            left[k * rows : (k + 1) * rows, side * head : (side + 1) * head] = piece


def combine(begun, *refs):
    parts, (held, w_one, w_two, out, left) = refs[:3], refs[3:]
    total = begun[...]
    depth = left.shape[-1]
    for which, part in enumerate(parts):
        turn(part, left.at[which])
        if which > 0:
            weight = held[(which - 1) * depth : which * depth]
        else:
            weight = jnp.concatenate([w_one[...], w_two[...]], axis=0)
        total = total + jnp.dot(left[which], weight, preferred_element_type=F32)
    out[...] = total.astype(BF16).reshape(out.shape)


def on_device(
    tokens, w_qkv, conv_weight, f_down, f_up, dt_bias, a_log, w_beta, o_down, o_up, norm_gain, w_out
):
    rows, model = tokens.shape
    head = f_up.shape[1]
    ctx_count, head_count = lax.axis_size("ctx"), lax.axis_size("head")
    zs = head_count // SUBS
    shape = jax.ShapeDtypeStruct
    dma = pltpu.SemaphoreType.DMA

    def across(value):
        half = ctx_count // 2
        pairs = [
            (c * head_count + h, ((c + half) % ctx_count) * head_count + (h ^ 2))
            for c in range(ctx_count)
            for h in range(head_count)
        ]
        return lax.ppermute(value, ("ctx", "head"), pairs)

    def flip(value, mask):
        return lax.ppermute(value, "head", [(h, h ^ mask) for h in range(head_count)])

    w3 = jnp.transpose(w_qkv, (1, 0, 2))
    taps = jnp.transpose(conv_weight, (1, 0, 2))
    edge = tokens[rows - 16 :]
    with jax.named_scope("rim"):
        rim = lax.ppermute(edge, "ctx", [(i, (i + 1) % ctx_count) for i in range(ctx_count)])
    (w_sent,) = after((w_out,), edge)
    with jax.named_scope("weights"):
        w_far, w_next = across(w_sent), flip(w_sent, 4)
    with jax.named_scope("front"):
        pack, sends = pl.pallas_call(
            front,
            in_specs=[HBM] * 11,
            out_specs=[HBM] * 2,
            out_shape=[
                shape((rows + head, 3 * head), F32),
                shape((head, 2 * head), BF16),
            ],
            scratch_shapes=[
                pltpu.VMEM((rows + 16, model), BF16),
                pltpu.VMEM((3, model, head), BF16),
                pltpu.VMEM((model, head), BF16),
                pltpu.VMEM((model, head), BF16),
                pltpu.VMEM((model, head), BF16),
                pltpu.VMEM((head, head), BF16),
                pltpu.VMEM((head, head), BF16),
                pltpu.VMEM((1, head), F32),
                pltpu.VMEM((1, model), BF16),
                pltpu.VMEM(taps.shape, F32),
                pltpu.VMEM((1, 1), F32),
                pltpu.VMEM((rows + 16, 6 * head), F32),
                pltpu.VMEM((rows + 8, 3 * head), F32),
                pltpu.VMEM((head, 2 * head), BF16),
                pltpu.VMEM((rows + head, 3 * head), F32),
                dma((7 + 6 * CHUNKS,)),
                dma((1,)),
                dma((2 + rows // GROUP,)),
            ],
            compiler_params=FULL,
            cost_estimate=cost(9, 40),
        )(
            tokens,
            rim,
            a_log.reshape(1, 1),
            w3,
            f_down,
            o_down,
            f_up,
            o_up,
            dt_bias.reshape(1, head),
            w_beta.reshape(1, model),
            taps,
        )
    with jax.named_scope("states"):
        half = ctx_count // 2

        def around(step):
            pairs = [(c, c // half * half + (c + step) % half) for c in range(ctx_count)]
            return lax.ppermute(sends, "ctx", pairs)

        found = {step: around(step) for step in range(1, half)}
        before, total = pl.pallas_call(
            fold,
            in_specs=[VMEM] * half,
            out_specs=[VMEM] * 2,
            out_shape=[shape((head, 2 * head), F32), shape((head, head), BF16)],
            scratch_shapes=[pltpu.VMEM((half, head, 2 * head), BF16)],
            compiler_params=LIMIT,
            cost_estimate=cost(0.5, 0),
        )(sends, *(found[step] for step in range(1, half)))
        came = lax.ppermute(total, "ctx", [(c, (c + half) % ctx_count) for c in range(ctx_count)])
    (w_early,) = after((w_far,), pack)
    with jax.named_scope("weights"):
        w_both = flip(w_early, 4)
    with jax.named_scope("stage"):
        staged = pl.pallas_call(
            stage,
            in_specs=[VMEM] * 2,
            out_specs=VMEM,
            out_shape=shape(pack.shape, F32),
            compiler_params=LIMIT,
            cost_estimate=cost(0.5, 0.5),
        )(pack, norm_gain.reshape(1, head))
    w_late, w_near, w_mine = after((w_far, w_next, w_out), staged)
    with jax.named_scope("weights"):
        w_core, w_far_core, w_next_core = flip(w_mine, 1), flip(w_late, 1), flip(w_near, 1)
    with jax.named_scope("finish"):
        own, other = pl.pallas_call(
            finish,
            in_specs=[VMEM] * 3,
            out_specs=[VMEM] * 2,
            out_shape=[shape((SUBS // 2, zs, 16, head), BF16)] * 2,
            scratch_shapes=[pltpu.VMEM((zs, SUBS // 2, 2, 16, head), BF16)],
            compiler_params=LIMIT,
            cost_estimate=cost(2, 0),
        )(staged, before, came)
    with jax.named_scope("exchange"):
        sibling = flip(other, 1)
        kept, *sent = pl.pallas_call(
            regroup,
            in_specs=[VMEM] * 2,
            out_specs=[VMEM] * 4,
            out_shape=[shape((2, zs, 16, head), BF16)] * 4,
            compiler_params=LIMIT,
            cost_estimate=cost(0.5, 0.5),
        )(own, sibling)
        got = {f: flip(sent[f - 1], 2 * f) for f in (3, 1, 2)}
    with jax.named_scope("spread"):
        held, begun = pl.pallas_call(
            spread,
            in_specs=[VMEM] * 7,
            out_specs=[VMEM] * 2,
            out_shape=[shape((4 * head, model), BF16), shape((zs * 16, model), F32)],
            scratch_shapes=[pltpu.VMEM((zs * 16, 2 * head), BF16)],
            compiler_params=LIMIT,
            cost_estimate=cost(2, 2),
        )(kept, w_out, w_core, w_far, w_far_core, w_next, w_next_core)
        (w_late,) = after((w_both,), kept)
        w_both_core = flip(w_late, 1)
        parts = pl.pallas_call(
            combine,
            in_specs=[VMEM] * 7,
            out_specs=VMEM,
            out_shape=shape((zs, 16, model), BF16),
            scratch_shapes=[pltpu.VMEM((3, zs * 16, 2 * head), BF16)],
            compiler_params=LIMIT,
            cost_estimate=cost(1, 1),
        )(begun, got[3], got[1], got[2], held, w_both, w_both_core)
    with jax.named_scope("reduce"):
        total = parts[0].astype(F32)
        for part in [flip(parts[k], SUBS * k) for k in (2, 1, 3)]:
            total = total + part.astype(F32)
        return total.astype(BF16)


def after(values, token):
    return lax.optimization_barrier((*values, token))[: len(values)]


def solution(mesh):
    in_specs = (
        P("ctx", None),
        P(None, None, "head"),
        P(None, None, "head"),
        P(),
        P(None, "head"),
        P("head"),
        P("head"),
        P(None, "head"),
        P(),
        P(None, "head"),
        P(),
        P("head", None),
    )
    out_specs = P(("ctx", "head"), None)
    return jax.shard_map(
        on_device, mesh=mesh, in_specs=in_specs, out_specs=out_specs, check_vma=False
    )
```

```python
import functools

import jax
import jax.numpy as jnp
from jax import lax
from jax.experimental import pallas as pl
from jax.experimental.pallas import tpu as pltpu
from jax.sharding import PartitionSpec as P

BLOCK = 64
GROUP = 128
SPAN = 256
SUBS = 8
CHUNKS = 3
F32 = jnp.float32
BF16 = jnp.bfloat16
HIGHEST = lax.Precision.HIGHEST
VMEM = pl.BlockSpec(memory_space=pltpu.VMEM)
HBM = pl.BlockSpec(memory_space=pltpu.HBM)
SMEM = pl.BlockSpec(memory_space=pltpu.SMEM)
FULL = pltpu.CompilerParams(vmem_limit_bytes=62 * 1024 * 1024)
LIMIT = pltpu.CompilerParams(vmem_limit_bytes=16 * 1024 * 1024)


def cost(us, flops=0):
    return pl.CostEstimate(
        flops=int(flops * 1_000_000_000), bytes_accessed=int(us * 3_690_000), transcendentals=0
    )


def mm(left, right):
    return jnp.dot(left.astype(BF16), right.astype(BF16), preferred_element_type=F32)


def mm_nt(left, right):
    return lax.dot_general(
        left.astype(BF16), right.astype(BF16), (((1,), (1,)), ((), ())), preferred_element_type=F32
    )


def mm_tn(left, right):
    return lax.dot_general(
        left.astype(BF16), right.astype(BF16), (((0,), (0,)), ((), ())), preferred_element_type=F32
    )


def split(value):
    high = value.astype(BF16)
    return high, (value - high.astype(F32)).astype(BF16)


def mm3(left, right):
    lh, ll = split(left)
    rh, rl = split(right)
    dot = functools.partial(jnp.dot, preferred_element_type=F32)
    return dot(lh, rh) + (dot(lh, rl) + dot(ll, rh))


def masks(size):
    row = lax.broadcasted_iota(jnp.int32, (size, size), 0)
    col = lax.broadcasted_iota(jnp.int32, (size, size), 1)
    return row, col, row ^ col


def load(pairs, sems):
    copies = []
    for place, (source, target) in enumerate(pairs):
        copies.append(pltpu.make_async_copy(source, target, sems.at[place]))
        copies[-1].start()
    return copies


def convolve(total, taps, padded, rows, part):
    head = taps.shape[2]
    conv_taps = taps.shape[1]
    lanes = slice(part * head, (part + 1) * head)
    edge = total[rows:, lanes].astype(BF16).astype(F32)[total.shape[0] - rows - 8 :]
    padded[0:8, lanes] = jnp.where(lax.axis_index("ctx") > 0, edge, 0.0)
    padded[8:, lanes] = total[:rows, lanes].astype(BF16).astype(F32)
    mixed = padded[9 - conv_taps : 9 - conv_taps + rows, lanes] * taps[part, 0:1, :]
    for tap in range(1, conv_taps):
        start = 9 - conv_taps + tap
        mixed = mixed + padded[start : start + rows, lanes] * taps[part, tap : tap + 1, :]
    return jax.nn.silu(mixed)


def unit_rows(value):
    return value * lax.rsqrt(jnp.sum(value * value, axis=-1, keepdims=True) + 1e-06)


def front(
    tokens_hbm, rim_hbm, alog_hbm, w3_hbm, f_down_hbm, o_down_hbm, f_up_hbm, o_up_hbm, bias_hbm,
    w_beta_hbm, taps_hbm, pack_hbm, sends, tok, w3, f_down, o_down,
    wide, f_up, o_up, bias, w_beta, taps, alog, total, padded, final, pack, sems, out_sems, pack_sems,
):
    rows, model = tokens_hbm.shape
    head = f_up.shape[0]
    count = rows // BLOCK
    inside = SPAN // BLOCK
    chunk = model // CHUNKS
    pairs = [(w_beta_hbm, w_beta), (rim_hbm, tok.at[pl.ds(rows, rim_hbm.shape[0])])]
    for step in range(CHUNKS):
        rng = pl.ds(step * chunk, chunk)
        pairs.append((tokens_hbm.at[:, rng], tok.at[pl.ds(0, rows), rng]))
        pairs += [(w3_hbm.at[part, rng], w3.at[part, rng]) for part in range(3)]
        pairs.append((f_down_hbm.at[rng], f_down.at[rng]))
        pairs.append((o_down_hbm.at[rng], o_down.at[rng]))
    pairs += [(f_up_hbm, f_up), (o_up_hbm, o_up), (bias_hbm, bias), (taps_hbm, taps)]
    pairs.append((alog_hbm, alog))
    copies = load(pairs, sems)
    wide[...] = jnp.zeros_like(wide)
    copies[0].wait()
    column = jnp.transpose(jnp.broadcast_to(w_beta[...].astype(F32), (8, model)))
    wide[:, 0:8] = column.astype(BF16)
    copies[1].wait()
    for step in range(CHUNKS):
        for copy in copies[2 + 6 * step : 8 + 6 * step]:
            copy.wait()
        rng = slice(step * chunk, (step + 1) * chunk)
        joined = [w3[part, rng] for part in range(3)] + [f_down[rng], o_down[rng], wide[rng]]
        piece = jnp.dot(tok[:, rng], jnp.concatenate(joined, axis=1), preferred_element_type=F32)
        if step == 0:
            total[...] = piece
        else:
            total[...] += piece
    for copy in copies[2 + 6 * CHUNKS :]:
        copy.wait()
    low = total[:rows, 3 * head : 4 * head].astype(BF16)
    logit = jnp.dot(low, f_up[...], preferred_element_type=F32) + bias[...]
    decays = -jnp.exp(alog[...]) * jax.nn.softplus(logit)
    out_low = total[:rows, 4 * head : 5 * head].astype(BF16)
    pack[:rows, 2 * head :] = jax.nn.sigmoid(jnp.dot(out_low, o_up[...], preferred_element_type=F32))
    stores = []

    def store(at):
        stores.append(pltpu.make_async_copy(pack.at[at], pack_hbm.at[at], pack_sems.at[len(stores)]))
        stores[-1].start()

    store((pl.ds(0, rows), pl.ds(2 * head, head)))
    beta = jnp.broadcast_to(jax.nn.sigmoid(total[:rows, 5 * head : 5 * head + 1]), (rows, head))
    row, col, differ = masks(GROUP)
    strict = (row > col) & (differ < BLOCK)
    causal = (row >= col) & (differ < BLOCK)
    unit = jnp.where(row == col, 1.0, 0.0).astype(F32)
    tri = jnp.where(causal, 1.0, 0.0).astype(BF16)
    high, rest = split(decays)
    middle, least = split(decays - high.astype(F32) - rest.astype(F32))
    terms = jnp.concatenate([high, rest, middle], axis=1)
    sums = [
        jnp.dot(tri, terms[s : s + GROUP], preferred_element_type=F32) for s in range(0, rows, GROUP)
    ]
    sums = jnp.concatenate(sums, axis=0)
    cumulative = sums[:, :head] + (sums[:, head : 2 * head] + sums[:, 2 * head :])
    key_raw = convolve(total, taps, padded, rows, 1)
    value_raw = convolve(total, taps, padded, rows, 2)
    query_raw = convolve(total, taps, padded, rows, 0)
    keyset = unit_rows(key_raw).astype(BF16).astype(F32)
    values = value_raw.astype(BF16).astype(F32)
    rising = jnp.exp(cumulative)
    key_rise = keyset * rising
    key_fall = (keyset * jnp.exp(-cumulative)).astype(BF16)
    blocked = cumulative.reshape(count, BLOCK, head)
    ends = blocked[:, BLOCK - 1 : BLOCK, :]
    tail = (keyset.reshape(count, BLOCK, head) * jnp.exp(ends - blocked)).reshape(rows, head)
    tail = tail.astype(BF16)
    shrink = jnp.transpose(jnp.exp(ends.reshape(count, head)))
    target = jnp.concatenate([beta * values, beta * key_rise], axis=1).astype(BF16)
    systems, inverse = [], []
    for start in range(0, rows, GROUP):
        rng = slice(start, start + GROUP)
        inner = mm_nt(key_rise[rng], key_fall[rng])
        systems.append(jnp.where(strict, inner * beta[rng], 0.0))
        inverse.append(unit - jnp.where(differ == 1, systems[-1], 0.0))
    size = 2
    while size < BLOCK:
        here = (differ >= size) & (differ < 2 * size)
        steps = [mm(jnp.where(here, s, 0.0), d) for s, d in zip(systems, inverse)]
        inverse = [d - mm(d, x) for d, x in zip(inverse, steps)]
        size *= 2
    pairs, solves, starts = [], [], {}
    for group, start in enumerate(range(0, rows, GROUP)):
        solved = mm(inverse[group], target[start : start + GROUP]).astype(BF16)
        solves.append(solved)
        for block in range(GROUP // BLOCK):
            sub = slice(block * BLOCK, (block + 1) * BLOCK)
            pairs.append(mm_tn(tail[start + block * BLOCK :][:BLOCK], solved[sub]))
    fresh = jnp.concatenate([jnp.zeros((head, head), F32), unit], axis=1)
    states = [fresh] * (rows // SPAN)
    for block in range(inside):
        for group in range(rows // SPAN):
            at = group * inside + block
            state = states[group]
            short = state.astype(BF16)
            starts[at] = short
            step = mm(pairs[at][:, head:], short)
            state = shrink[:, at : at + 1] * state - step
            states[group] = jnp.concatenate(
                [state[:, :head] + pairs[at][:, :head], state[:, head:]], axis=1
            )
    pack[rows:, : 2 * head] = states[0]
    store((pl.ds(rows, head), pl.ds(0, 2 * head)))
    whole = mm(states[1][:, head:], states[0])
    final[...] = jnp.concatenate(
        [whole[:, :head] + states[1][:, :head], whole[:, head:]], axis=1
    ).astype(BF16)
    copies = load([(final, sends)], out_sems)
    queries = (unit_rows(query_raw) * (head ** (-0.5))).astype(BF16).astype(F32)
    query_rise = queries * rising
    for group, start in enumerate(range(0, rows, GROUP)):
        rng = slice(start, start + GROUP)
        scores = jnp.where(causal, mm_nt(query_rise[rng], key_fall[rng]), 0.0)
        local = mm(scores, solves[group])
        local_key = (query_rise[rng] - local[:, head:]).astype(BF16)
        for block in range(GROUP // BLOCK):
            sub = slice(block * BLOCK, (block + 1) * BLOCK)
            out = slice(start + block * BLOCK, start + (block + 1) * BLOCK)
            across = jnp.dot(
                local_key[sub], starts[(start // BLOCK) + block], preferred_element_type=F32
            )
            pack[out, :head] = across[:, :head] + local[sub, :head]
            pack[out, head : 2 * head] = across[:, head:]
        store((pl.ds(start, GROUP), pl.ds(0, 2 * head)))
    for copy in copies + stores:
        copy.wait()


def fold(*refs):
    found, (before, total, held) = refs[:-3], refs[-3:]
    count = len(found)
    mine = lax.rem(lax.axis_index("ctx"), count)
    head = found[0].shape[0]
    for back, ref in enumerate(found):
        held[back] = ref[...]
    row = lax.broadcasted_iota(jnp.int32, (head, 2 * head), 0)
    col = lax.broadcasted_iota(jnp.int32, (head, 2 * head), 1)
    state = jnp.where(row + head == col, 1.0, 0.0).astype(F32)
    seen = state
    for step in range(count):
        seen = jnp.where(mine == step, state, seen)
        item = held[lax.rem(mine - step + count, count)]
        moved = jnp.dot(item[:, head:], state.astype(BF16), preferred_element_type=F32)
        state = jnp.concatenate(
            [moved[:, :head] + item[:, :head].astype(F32), moved[:, head:]], axis=1
        )
    before[...] = seen
    total[...] = state[:, :head].astype(BF16)


def stage(pack, gain, out):
    head = gain.shape[1]
    rows = pack.shape[0] - head
    out[:, : 2 * head] = pack[:, : 2 * head]
    out[:rows, 2 * head :] = pack[:rows, 2 * head :] * gain[...]


def finish(pack, before, came, own, other, gated):
    head = came.shape[0]
    rows = pack.shape[0] - head
    core_at = lax.rem(lax.axis_index("head"), 2)
    later = lax.axis_index("ctx") >= lax.axis_size("ctx") // 2
    state = jnp.where(later, came[...].astype(F32), 0.0)
    state = mm(before[:, head:], state) + before[:, :head]
    middle = mm(pack[rows:, head : 2 * head], state) + pack[rows:, :head]
    cores = []
    for group, start in enumerate((state, middle)):
        rng = slice(group * SPAN, (group + 1) * SPAN)
        cores.append(pack[rng, :head] + mm(pack[rng, head : 2 * head], start))
    core = jnp.concatenate(cores, axis=0)
    scale = lax.rsqrt(jnp.mean(core * core, axis=-1, keepdims=True) + 1e-05)
    result = core * scale * pack[:rows, 2 * head :]
    gated[...] = result.astype(BF16).reshape(gated.shape)
    for pair in range(own.shape[0]):
        own[pair] = gated[:, pair, pl.ds(core_at, 1)].reshape(own.shape[1:])
        other[pair] = gated[:, pair, pl.ds(1 - core_at, 1)].reshape(own.shape[1:])


def regroup(own, sibling, *outs):
    mine = lax.rem(lax.axis_index("head") // 2, own.shape[0])
    for flip, out in enumerate(outs):
        at = mine ^ flip
        out[0] = own[pl.ds(at, 1)].reshape(out.shape[1:])
        out[1] = sibling[pl.ds(at, 1)].reshape(out.shape[1:])


def spread(part, w_one, w_two, *refs):
    rest, held, out, left = refs[:-3], refs[-3], refs[-2], refs[-1]
    turn(part, left)
    joined = jnp.concatenate([w_one[...], w_two[...]], axis=0)
    out[...] = jnp.dot(left[...], joined, preferred_element_type=F32)
    head = w_one.shape[0]
    for at, ref in enumerate(rest):
        held[at * head : (at + 1) * head] = ref[...]


def turn(part, left):
    mine = lax.axis_index("head") // SUBS
    sides, zs, rows, head = part.shape
    for side in range(sides):
        for k in range(zs):
            piece = part[side, pl.ds(mine ^ k, 1)].reshape(rows, head)
            left[k * rows : (k + 1) * rows, side * head : (side + 1) * head] = piece


def combine(begun, *refs):
    parts, (held, w_one, w_two, out, left) = refs[:3], refs[3:]
    total = begun[...]
    depth = left.shape[-1]
    for which, part in enumerate(parts):
        turn(part, left.at[which])
        if which > 0:
            weight = held[(which - 1) * depth : which * depth]
        else:
            weight = jnp.concatenate([w_one[...], w_two[...]], axis=0)
        total = total + jnp.dot(left[which], weight, preferred_element_type=F32)
    out[...] = total.astype(BF16).reshape(out.shape)


def on_device(
    tokens, w_qkv, conv_weight, f_down, f_up, dt_bias, a_log, w_beta, o_down, o_up, norm_gain, w_out
):
    rows, model = tokens.shape
    head = f_up.shape[1]
    ctx_count, head_count = lax.axis_size("ctx"), lax.axis_size("head")
    zs = head_count // SUBS
    shape = jax.ShapeDtypeStruct
    dma = pltpu.SemaphoreType.DMA

    def across(value):
        half = ctx_count // 2
        pairs = [
            (c * head_count + h, ((c + half) % ctx_count) * head_count + (h ^ 2))
            for c in range(ctx_count)
            for h in range(head_count)
        ]
        return lax.ppermute(value, ("ctx", "head"), pairs)

    def flip(value, mask):
        return lax.ppermute(value, "head", [(h, h ^ mask) for h in range(head_count)])

    w3 = jnp.transpose(w_qkv, (1, 0, 2))
    taps = jnp.transpose(conv_weight, (1, 0, 2))
    edge = tokens[rows - 16 :]
    with jax.named_scope("rim"):
        rim = lax.ppermute(edge, "ctx", [(i, (i + 1) % ctx_count) for i in range(ctx_count)])
    (w_sent,) = after((w_out,), edge)
    with jax.named_scope("weights"):
        w_far, w_next = across(w_sent), flip(w_sent, 4)
    with jax.named_scope("front"):
        pack, sends = pl.pallas_call(
            front,
            in_specs=[HBM] * 11,
            out_specs=[HBM] * 2,
            out_shape=[
                shape((rows + head, 3 * head), F32),
                shape((head, 2 * head), BF16),
            ],
            scratch_shapes=[
                pltpu.VMEM((rows + 16, model), BF16),
                pltpu.VMEM((3, model, head), BF16),
                pltpu.VMEM((model, head), BF16),
                pltpu.VMEM((model, head), BF16),
                pltpu.VMEM((model, head), BF16),
                pltpu.VMEM((head, head), BF16),
                pltpu.VMEM((head, head), BF16),
                pltpu.VMEM((1, head), F32),
                pltpu.VMEM((1, model), BF16),
                pltpu.VMEM(taps.shape, F32),
                pltpu.VMEM((1, 1), F32),
                pltpu.VMEM((rows + 16, 6 * head), F32),
                pltpu.VMEM((rows + 8, 3 * head), F32),
                pltpu.VMEM((head, 2 * head), BF16),
                pltpu.VMEM((rows + head, 3 * head), F32),
                dma((7 + 6 * CHUNKS,)),
                dma((1,)),
                dma((2 + rows // GROUP,)),
            ],
            compiler_params=FULL,
            cost_estimate=cost(9, 40),
        )(
            tokens,
            rim,
            a_log.reshape(1, 1),
            w3,
            f_down,
            o_down,
            f_up,
            o_up,
            dt_bias.reshape(1, head),
            w_beta.reshape(1, model),
            taps,
        )
    with jax.named_scope("states"):
        half = ctx_count // 2

        def around(step):
            pairs = [(c, c // half * half + (c + step) % half) for c in range(ctx_count)]
            return lax.ppermute(sends, "ctx", pairs)

        found = {step: around(step) for step in range(1, half)}
        before, total = pl.pallas_call(
            fold,
            in_specs=[VMEM] * half,
            out_specs=[VMEM] * 2,
            out_shape=[shape((head, 2 * head), F32), shape((head, head), BF16)],
            scratch_shapes=[pltpu.VMEM((half, head, 2 * head), BF16)],
            compiler_params=LIMIT,
            cost_estimate=cost(0.5, 0),
        )(sends, *(found[step] for step in range(1, half)))
        came = lax.ppermute(total, "ctx", [(c, (c + half) % ctx_count) for c in range(ctx_count)])
    (w_early,) = after((w_far,), pack)
    with jax.named_scope("weights"):
        w_both = flip(w_early, 4)
    (late_pack,) = after((pack,), total)
    with jax.named_scope("stage"):
        staged = pl.pallas_call(
            stage,
            in_specs=[VMEM] * 2,
            out_specs=VMEM,
            out_shape=shape(pack.shape, F32),
            compiler_params=LIMIT,
            cost_estimate=cost(0.5, 0.5),
        )(late_pack, norm_gain.reshape(1, head))
    w_late, w_near, w_mine = after((w_far, w_next, w_out), pack)
    with jax.named_scope("weights"):
        w_core, w_far_core, w_next_core = flip(w_mine, 1), flip(w_late, 1), flip(w_near, 1)
    with jax.named_scope("finish"):
        own, other = pl.pallas_call(
            finish,
            in_specs=[VMEM] * 3,
            out_specs=[VMEM] * 2,
            out_shape=[shape((SUBS // 2, zs, 16, head), BF16)] * 2,
            scratch_shapes=[pltpu.VMEM((zs, SUBS // 2, 2, 16, head), BF16)],
            compiler_params=LIMIT,
            cost_estimate=cost(2, 0),
        )(staged, before, came)
    with jax.named_scope("exchange"):
        sibling = flip(other, 1)
        kept, *sent = pl.pallas_call(
            regroup,
            in_specs=[VMEM] * 2,
            out_specs=[VMEM] * 4,
            out_shape=[shape((2, zs, 16, head), BF16)] * 4,
            compiler_params=LIMIT,
            cost_estimate=cost(0.5, 0.5),
        )(own, sibling)
        got = {f: flip(sent[f - 1], 2 * f) for f in (3, 1, 2)}
    with jax.named_scope("spread"):
        held, begun = pl.pallas_call(
            spread,
            in_specs=[VMEM] * 7,
            out_specs=[VMEM] * 2,
            out_shape=[shape((4 * head, model), BF16), shape((zs * 16, model), F32)],
            scratch_shapes=[pltpu.VMEM((zs * 16, 2 * head), BF16)],
            compiler_params=LIMIT,
            cost_estimate=cost(2, 2),
        )(kept, w_out, w_core, w_far, w_far_core, w_next, w_next_core)
        (w_late,) = after((w_both,), kept)
        w_both_core = flip(w_late, 1)
        parts = pl.pallas_call(
            combine,
            in_specs=[VMEM] * 7,
            out_specs=VMEM,
            out_shape=shape((zs, 16, model), BF16),
            scratch_shapes=[pltpu.VMEM((3, zs * 16, 2 * head), BF16)],
            compiler_params=LIMIT,
            cost_estimate=cost(1, 1),
        )(begun, got[3], got[1], got[2], held, w_both, w_both_core)
    with jax.named_scope("reduce"):
        total = parts[0].astype(F32)
        for part in [flip(parts[k], SUBS * k) for k in (2, 1, 3)]:
            total = total + part.astype(F32)
        return total.astype(BF16)


def after(values, token):
    return lax.optimization_barrier((*values, token))[: len(values)]


def solution(mesh):
    in_specs = (
        P("ctx", None),
        P(None, None, "head"),
        P(None, None, "head"),
        P(),
        P(None, "head"),
        P("head"),
        P("head"),
        P(None, "head"),
        P(),
        P(None, "head"),
        P(),
        P("head", None),
    )
    out_specs = P(("ctx", "head"), None)
    return jax.shard_map(
        on_device, mesh=mesh, in_specs=in_specs, out_specs=out_specs, check_vma=False
    )
```

```python
import functools

import jax
import jax.numpy as jnp
from jax import lax
from jax.experimental import pallas as pl
from jax.experimental.pallas import tpu as pltpu
from jax.sharding import PartitionSpec as P

BLOCK = 64
GROUP = 128
SPAN = 256
SUBS = 8
CHUNKS = 3
F32 = jnp.float32
BF16 = jnp.bfloat16
HIGHEST = lax.Precision.HIGHEST
VMEM = pl.BlockSpec(memory_space=pltpu.VMEM)
HBM = pl.BlockSpec(memory_space=pltpu.HBM)
SMEM = pl.BlockSpec(memory_space=pltpu.SMEM)
FULL = pltpu.CompilerParams(vmem_limit_bytes=62 * 1024 * 1024)
LIMIT = pltpu.CompilerParams(vmem_limit_bytes=16 * 1024 * 1024)


def cost(us, flops=0):
    return pl.CostEstimate(
        flops=int(flops * 1_000_000_000), bytes_accessed=int(us * 3_690_000), transcendentals=0
    )


def mm(left, right):
    return jnp.dot(left.astype(BF16), right.astype(BF16), preferred_element_type=F32)


def mm_nt(left, right):
    return lax.dot_general(
        left.astype(BF16), right.astype(BF16), (((1,), (1,)), ((), ())), preferred_element_type=F32
    )


def mm_tn(left, right):
    return lax.dot_general(
        left.astype(BF16), right.astype(BF16), (((0,), (0,)), ((), ())), preferred_element_type=F32
    )


def split(value):
    high = value.astype(BF16)
    return high, (value - high.astype(F32)).astype(BF16)


def mm3(left, right):
    lh, ll = split(left)
    rh, rl = split(right)
    dot = functools.partial(jnp.dot, preferred_element_type=F32)
    return dot(lh, rh) + (dot(lh, rl) + dot(ll, rh))


def masks(size):
    row = lax.broadcasted_iota(jnp.int32, (size, size), 0)
    col = lax.broadcasted_iota(jnp.int32, (size, size), 1)
    return row, col, row ^ col


def load(pairs, sems):
    copies = []
    for place, (source, target) in enumerate(pairs):
        copies.append(pltpu.make_async_copy(source, target, sems.at[place]))
        copies[-1].start()
    return copies


def convolve(total, taps, padded, rows, part):
    head = taps.shape[2]
    conv_taps = taps.shape[1]
    lanes = slice(part * head, (part + 1) * head)
    edge = total[rows:, lanes].astype(BF16).astype(F32)[total.shape[0] - rows - 8 :]
    padded[0:8, lanes] = jnp.where(lax.axis_index("ctx") > 0, edge, 0.0)
    padded[8:, lanes] = total[:rows, lanes].astype(BF16).astype(F32)
    mixed = padded[9 - conv_taps : 9 - conv_taps + rows, lanes] * taps[part, 0:1, :]
    for tap in range(1, conv_taps):
        start = 9 - conv_taps + tap
        mixed = mixed + padded[start : start + rows, lanes] * taps[part, tap : tap + 1, :]
    return jax.nn.silu(mixed)


def unit_rows(value):
    return value * lax.rsqrt(jnp.sum(value * value, axis=-1, keepdims=True) + 1e-06)


def front(
    tokens_hbm, rim_hbm, alog_hbm, w3_hbm, f_down_hbm, o_down_hbm, f_up_hbm, o_up_hbm, bias_hbm,
    w_beta_hbm, taps_hbm, pack_hbm, sends, tok, w3, f_down, o_down,
    wide, f_up, o_up, bias, w_beta, taps, alog, total, padded, final, pack, sems, out_sems, pack_sems,
):
    rows, model = tokens_hbm.shape
    head = f_up.shape[0]
    count = rows // BLOCK
    inside = SPAN // BLOCK
    chunk = model // CHUNKS
    pairs = [(w_beta_hbm, w_beta), (rim_hbm, tok.at[pl.ds(rows, rim_hbm.shape[0])])]
    for step in range(CHUNKS):
        rng = pl.ds(step * chunk, chunk)
        pairs.append((tokens_hbm.at[:, rng], tok.at[pl.ds(0, rows), rng]))
        pairs += [(w3_hbm.at[part, rng], w3.at[part, rng]) for part in range(3)]
        pairs.append((f_down_hbm.at[rng], f_down.at[rng]))
        pairs.append((o_down_hbm.at[rng], o_down.at[rng]))
    pairs += [(f_up_hbm, f_up), (o_up_hbm, o_up), (bias_hbm, bias), (taps_hbm, taps)]
    pairs.append((alog_hbm, alog))
    copies = load(pairs, sems)
    wide[...] = jnp.zeros_like(wide)
    copies[0].wait()
    column = jnp.transpose(jnp.broadcast_to(w_beta[...].astype(F32), (8, model)))
    wide[:, 0:8] = column.astype(BF16)
    copies[1].wait()
    for step in range(CHUNKS):
        for copy in copies[2 + 6 * step : 8 + 6 * step]:
            copy.wait()
        rng = slice(step * chunk, (step + 1) * chunk)
        joined = [w3[part, rng] for part in range(3)] + [f_down[rng], o_down[rng], wide[rng]]
        piece = jnp.dot(tok[:, rng], jnp.concatenate(joined, axis=1), preferred_element_type=F32)
        if step == 0:
            total[...] = piece
        else:
            total[...] += piece
    for copy in copies[2 + 6 * CHUNKS :]:
        copy.wait()
    low = total[:rows, 3 * head : 4 * head].astype(BF16)
    logit = jnp.dot(low, f_up[...], preferred_element_type=F32) + bias[...]
    decays = -jnp.exp(alog[...]) * jax.nn.softplus(logit)
    out_low = total[:rows, 4 * head : 5 * head].astype(BF16)
    pack[:rows, 2 * head :] = jax.nn.sigmoid(jnp.dot(out_low, o_up[...], preferred_element_type=F32))
    stores = []

    def store(at):
        stores.append(pltpu.make_async_copy(pack.at[at], pack_hbm.at[at], pack_sems.at[len(stores)]))
        stores[-1].start()

    store((pl.ds(0, rows), pl.ds(2 * head, head)))
    beta = jnp.broadcast_to(jax.nn.sigmoid(total[:rows, 5 * head : 5 * head + 1]), (rows, head))
    row, col, differ = masks(GROUP)
    strict = (row > col) & (differ < BLOCK)
    causal = (row >= col) & (differ < BLOCK)
    unit = jnp.where(row == col, 1.0, 0.0).astype(F32)
    tri = jnp.where(causal, 1.0, 0.0).astype(BF16)
    high, rest = split(decays)
    middle, least = split(decays - high.astype(F32) - rest.astype(F32))
    terms = jnp.concatenate([high, rest, middle], axis=1)
    sums = [
        jnp.dot(tri, terms[s : s + GROUP], preferred_element_type=F32) for s in range(0, rows, GROUP)
    ]
    sums = jnp.concatenate(sums, axis=0)
    cumulative = sums[:, :head] + (sums[:, head : 2 * head] + sums[:, 2 * head :])
    key_raw = convolve(total, taps, padded, rows, 1)
    value_raw = convolve(total, taps, padded, rows, 2)
    query_raw = convolve(total, taps, padded, rows, 0)
    keyset = unit_rows(key_raw).astype(BF16).astype(F32)
    values = value_raw.astype(BF16).astype(F32)
    rising = jnp.exp(cumulative)
    key_rise = keyset * rising
    key_fall = (keyset * jnp.exp(-cumulative)).astype(BF16)
    blocked = cumulative.reshape(count, BLOCK, head)
    ends = blocked[:, BLOCK - 1 : BLOCK, :]
    tail = (keyset.reshape(count, BLOCK, head) * jnp.exp(ends - blocked)).reshape(rows, head)
    tail = tail.astype(BF16)
    shrink = jnp.transpose(jnp.exp(ends.reshape(count, head)))
    target = jnp.concatenate([beta * values, beta * key_rise], axis=1).astype(BF16)
    systems, inverse = [], []
    for start in range(0, rows, GROUP):
        rng = slice(start, start + GROUP)
        inner = mm_nt(key_rise[rng], key_fall[rng])
        systems.append(jnp.where(strict, inner * beta[rng], 0.0))
        inverse.append(unit - jnp.where(differ == 1, systems[-1], 0.0))
    size = 2
    while size < BLOCK:
        here = (differ >= size) & (differ < 2 * size)
        steps = [mm(jnp.where(here, s, 0.0), d) for s, d in zip(systems, inverse)]
        inverse = [d - mm(d, x) for d, x in zip(inverse, steps)]
        size *= 2
    pairs, solves, starts = [], [], {}
    for group, start in enumerate(range(0, rows, GROUP)):
        solved = mm(inverse[group], target[start : start + GROUP]).astype(BF16)
        solves.append(solved)
        for block in range(GROUP // BLOCK):
            sub = slice(block * BLOCK, (block + 1) * BLOCK)
            pairs.append(mm_tn(tail[start + block * BLOCK :][:BLOCK], solved[sub]))
    fresh = jnp.concatenate([jnp.zeros((head, head), F32), unit], axis=1)
    states = [fresh] * (rows // SPAN)
    for block in range(inside):
        for group in range(rows // SPAN):
            at = group * inside + block
            state = states[group]
            short = state.astype(BF16)
            starts[at] = short
            step = mm(pairs[at][:, head:], short)
            state = shrink[:, at : at + 1] * state - step
            states[group] = jnp.concatenate(
                [state[:, :head] + pairs[at][:, :head], state[:, head:]], axis=1
            )
    pack[rows : rows + head, : 2 * head] = states[0]
    store((pl.ds(rows, head), pl.ds(0, 2 * head)))
    whole = mm(states[1][:, head:], states[0])
    final[...] = jnp.concatenate(
        [whole[:, :head] + states[1][:, :head], whole[:, head:]], axis=1
    ).astype(BF16)
    copies = load([(final, sends)], out_sems)
    pack[rows + head :, : 2 * head] = final[...].astype(F32)
    store((pl.ds(rows + head, head), pl.ds(0, 2 * head)))
    queries = (unit_rows(query_raw) * (head ** (-0.5))).astype(BF16).astype(F32)
    query_rise = queries * rising
    for group, start in enumerate(range(0, rows, GROUP)):
        rng = slice(start, start + GROUP)
        scores = jnp.where(causal, mm_nt(query_rise[rng], key_fall[rng]), 0.0)
        local = mm(scores, solves[group])
        local_key = (query_rise[rng] - local[:, head:]).astype(BF16)
        for block in range(GROUP // BLOCK):
            sub = slice(block * BLOCK, (block + 1) * BLOCK)
            out = slice(start + block * BLOCK, start + (block + 1) * BLOCK)
            across = jnp.dot(
                local_key[sub], starts[(start // BLOCK) + block], preferred_element_type=F32
            )
            pack[out, :head] = across[:, :head] + local[sub, :head]
            pack[out, head : 2 * head] = across[:, head:]
        store((pl.ds(start, GROUP), pl.ds(0, 2 * head)))
    for copy in copies + stores:
        copy.wait()


def fold(pack, *refs):
    found, (before, total, held) = refs[:-3], refs[-3:]
    count = len(found) + 1
    mine = lax.rem(lax.axis_index("ctx"), count)
    head = found[0].shape[0]
    held[0] = pack[pack.shape[0] - head :, : 2 * head].astype(BF16)
    for back, ref in enumerate(found):
        held[back + 1] = ref[...]
    row = lax.broadcasted_iota(jnp.int32, (head, 2 * head), 0)
    col = lax.broadcasted_iota(jnp.int32, (head, 2 * head), 1)
    state = jnp.where(row + head == col, 1.0, 0.0).astype(F32)
    seen = state
    for step in range(count):
        seen = jnp.where(mine == step, state, seen)
        item = held[lax.rem(mine - step + count, count)]
        moved = jnp.dot(item[:, head:], state.astype(BF16), preferred_element_type=F32)
        state = jnp.concatenate(
            [moved[:, :head] + item[:, :head].astype(F32), moved[:, head:]], axis=1
        )
    before[...] = seen
    total[...] = state[:, :head].astype(BF16)


def stage(pack, gain, out):
    head = gain.shape[1]
    rows = pack.shape[0] - 2 * head
    out[:, : 2 * head] = pack[:, : 2 * head]
    out[:rows, 2 * head :] = pack[:rows, 2 * head :] * gain[...]


def finish(pack, before, came, own, other, gated):
    head = came.shape[0]
    rows = pack.shape[0] - 2 * head
    core_at = lax.rem(lax.axis_index("head"), 2)
    later = lax.axis_index("ctx") >= lax.axis_size("ctx") // 2
    state = jnp.where(later, came[...].astype(F32), 0.0)
    state = mm(before[:, head:], state) + before[:, :head]
    middle = mm(pack[rows : rows + head, head : 2 * head], state)
    middle = middle + pack[rows : rows + head, :head]
    cores = []
    for group, start in enumerate((state, middle)):
        rng = slice(group * SPAN, (group + 1) * SPAN)
        cores.append(pack[rng, :head] + mm(pack[rng, head : 2 * head], start))
    core = jnp.concatenate(cores, axis=0)
    scale = lax.rsqrt(jnp.mean(core * core, axis=-1, keepdims=True) + 1e-05)
    result = core * scale * pack[:rows, 2 * head :]
    gated[...] = result.astype(BF16).reshape(gated.shape)
    for pair in range(own.shape[0]):
        own[pair] = gated[:, pair, pl.ds(core_at, 1)].reshape(own.shape[1:])
        other[pair] = gated[:, pair, pl.ds(1 - core_at, 1)].reshape(own.shape[1:])


def regroup(own, sibling, *outs):
    mine = lax.rem(lax.axis_index("head") // 2, own.shape[0])
    for flip, out in enumerate(outs):
        at = mine ^ flip
        out[0] = own[pl.ds(at, 1)].reshape(out.shape[1:])
        out[1] = sibling[pl.ds(at, 1)].reshape(out.shape[1:])


def spread(part, w_one, w_two, *refs):
    rest, held, out, left = refs[:-3], refs[-3], refs[-2], refs[-1]
    turn(part, left)
    joined = jnp.concatenate([w_one[...], w_two[...]], axis=0)
    out[...] = jnp.dot(left[...], joined, preferred_element_type=F32)
    head = w_one.shape[0]
    for at, ref in enumerate(rest):
        held[at * head : (at + 1) * head] = ref[...]


def turn(part, left):
    mine = lax.axis_index("head") // SUBS
    sides, zs, rows, head = part.shape
    for side in range(sides):
        for k in range(zs):
            piece = part[side, pl.ds(mine ^ k, 1)].reshape(rows, head)
            left[k * rows : (k + 1) * rows, side * head : (side + 1) * head] = piece


def combine(begun, *refs):
    parts, (held, w_one, w_two, out, left) = refs[:3], refs[3:]
    total = begun[...]
    depth = left.shape[-1]
    for which, part in enumerate(parts):
        turn(part, left.at[which])
        if which > 0:
            weight = held[(which - 1) * depth : which * depth]
        else:
            weight = jnp.concatenate([w_one[...], w_two[...]], axis=0)
        total = total + jnp.dot(left[which], weight, preferred_element_type=F32)
    out[...] = total.astype(BF16).reshape(out.shape)


def on_device(
    tokens, w_qkv, conv_weight, f_down, f_up, dt_bias, a_log, w_beta, o_down, o_up, norm_gain, w_out
):
    rows, model = tokens.shape
    head = f_up.shape[1]
    ctx_count, head_count = lax.axis_size("ctx"), lax.axis_size("head")
    zs = head_count // SUBS
    shape = jax.ShapeDtypeStruct
    dma = pltpu.SemaphoreType.DMA

    def across(value):
        half = ctx_count // 2
        pairs = [
            (c * head_count + h, ((c + half) % ctx_count) * head_count + (h ^ 2))
            for c in range(ctx_count)
            for h in range(head_count)
        ]
        return lax.ppermute(value, ("ctx", "head"), pairs)

    def flip(value, mask):
        return lax.ppermute(value, "head", [(h, h ^ mask) for h in range(head_count)])

    w3 = jnp.transpose(w_qkv, (1, 0, 2))
    taps = jnp.transpose(conv_weight, (1, 0, 2))
    edge = tokens[rows - 16 :]
    with jax.named_scope("rim"):
        rim = lax.ppermute(edge, "ctx", [(i, (i + 1) % ctx_count) for i in range(ctx_count)])
    (w_sent,) = after((w_out,), edge)
    with jax.named_scope("weights"):
        w_far, w_next = across(w_sent), flip(w_sent, 4)
    with jax.named_scope("front"):
        pack, sends = pl.pallas_call(
            front,
            in_specs=[HBM] * 11,
            out_specs=[HBM] * 2,
            out_shape=[
                shape((rows + 2 * head, 3 * head), F32),
                shape((head, 2 * head), BF16),
            ],
            scratch_shapes=[
                pltpu.VMEM((rows + 16, model), BF16),
                pltpu.VMEM((3, model, head), BF16),
                pltpu.VMEM((model, head), BF16),
                pltpu.VMEM((model, head), BF16),
                pltpu.VMEM((model, head), BF16),
                pltpu.VMEM((head, head), BF16),
                pltpu.VMEM((head, head), BF16),
                pltpu.VMEM((1, head), F32),
                pltpu.VMEM((1, model), BF16),
                pltpu.VMEM(taps.shape, F32),
                pltpu.VMEM((1, 1), F32),
                pltpu.VMEM((rows + 16, 6 * head), F32),
                pltpu.VMEM((rows + 8, 3 * head), F32),
                pltpu.VMEM((head, 2 * head), BF16),
                pltpu.VMEM((rows + 2 * head, 3 * head), F32),
                dma((7 + 6 * CHUNKS,)),
                dma((1,)),
                dma((3 + rows // GROUP,)),
            ],
            compiler_params=FULL,
            cost_estimate=cost(9, 40),
        )(
            tokens,
            rim,
            a_log.reshape(1, 1),
            w3,
            f_down,
            o_down,
            f_up,
            o_up,
            dt_bias.reshape(1, head),
            w_beta.reshape(1, model),
            taps,
        )
    with jax.named_scope("states"):
        half = ctx_count // 2

        def around(step):
            pairs = [(c, c // half * half + (c + step) % half) for c in range(ctx_count)]
            return lax.ppermute(sends, "ctx", pairs)

        found = {step: around(step) for step in range(1, half)}
    (w_early,) = after((w_far,), pack)
    with jax.named_scope("weights"):
        w_both = flip(w_early, 4)
    with jax.named_scope("stage"):
        staged = pl.pallas_call(
            stage,
            in_specs=[VMEM] * 2,
            out_specs=VMEM,
            out_shape=shape(pack.shape, F32),
            compiler_params=LIMIT,
            cost_estimate=cost(0.5, 0.5),
        )(pack, norm_gain.reshape(1, head))
    with jax.named_scope("states"):
        before, total = pl.pallas_call(
            fold,
            in_specs=[VMEM] * half,
            out_specs=[VMEM] * 2,
            out_shape=[shape((head, 2 * head), F32), shape((head, head), BF16)],
            scratch_shapes=[pltpu.VMEM((half, head, 2 * head), BF16)],
            compiler_params=LIMIT,
            cost_estimate=cost(0.5, 0),
        )(staged, *(found[step] for step in range(1, half)))
        came = lax.ppermute(total, "ctx", [(c, (c + half) % ctx_count) for c in range(ctx_count)])
    w_late, w_near, w_mine = after((w_far, w_next, w_out), staged)
    with jax.named_scope("weights"):
        w_core, w_far_core, w_next_core = flip(w_mine, 1), flip(w_late, 1), flip(w_near, 1)
    with jax.named_scope("finish"):
        own, other = pl.pallas_call(
            finish,
            in_specs=[VMEM] * 3,
            out_specs=[VMEM] * 2,
            out_shape=[shape((SUBS // 2, zs, 16, head), BF16)] * 2,
            scratch_shapes=[pltpu.VMEM((zs, SUBS // 2, 2, 16, head), BF16)],
            compiler_params=LIMIT,
            cost_estimate=cost(2, 0),
        )(staged, before, came)
    with jax.named_scope("exchange"):
        sibling = flip(other, 1)
        kept, *sent = pl.pallas_call(
            regroup,
            in_specs=[VMEM] * 2,
            out_specs=[VMEM] * 4,
            out_shape=[shape((2, zs, 16, head), BF16)] * 4,
            compiler_params=LIMIT,
            cost_estimate=cost(0.5, 0.5),
        )(own, sibling)
        got = {f: flip(sent[f - 1], 2 * f) for f in (3, 1, 2)}
    with jax.named_scope("spread"):
        held, begun = pl.pallas_call(
            spread,
            in_specs=[VMEM] * 7,
            out_specs=[VMEM] * 2,
            out_shape=[shape((4 * head, model), BF16), shape((zs * 16, model), F32)],
            scratch_shapes=[pltpu.VMEM((zs * 16, 2 * head), BF16)],
            compiler_params=LIMIT,
            cost_estimate=cost(2, 2),
        )(kept, w_out, w_core, w_far, w_far_core, w_next, w_next_core)
        (w_late,) = after((w_both,), kept)
        w_both_core = flip(w_late, 1)
        parts = pl.pallas_call(
            combine,
            in_specs=[VMEM] * 7,
            out_specs=VMEM,
            out_shape=shape((zs, 16, model), BF16),
            scratch_shapes=[pltpu.VMEM((3, zs * 16, 2 * head), BF16)],
            compiler_params=LIMIT,
            cost_estimate=cost(1, 1),
        )(begun, got[3], got[1], got[2], held, w_both, w_both_core)
    with jax.named_scope("reduce"):
        total = parts[0].astype(F32)
        for part in [flip(parts[k], SUBS * k) for k in (2, 1, 3)]:
            total = total + part.astype(F32)
        return total.astype(BF16)


def after(values, token):
    return lax.optimization_barrier((*values, token))[: len(values)]


def solution(mesh):
    in_specs = (
        P("ctx", None),
        P(None, None, "head"),
        P(None, None, "head"),
        P(),
        P(None, "head"),
        P("head"),
        P("head"),
        P(None, "head"),
        P(),
        P(None, "head"),
        P(),
        P("head", None),
    )
    out_specs = P(("ctx", "head"), None)
    return jax.shard_map(
        on_device, mesh=mesh, in_specs=in_specs, out_specs=out_specs, check_vma=False
    )
```

```python
import functools

import jax
import jax.numpy as jnp
from jax import lax
from jax.experimental import pallas as pl
from jax.experimental.pallas import tpu as pltpu
from jax.sharding import PartitionSpec as P

BLOCK = 64
GROUP = 128
SPAN = 256
SUBS = 8
CHUNKS = 3
F32 = jnp.float32
BF16 = jnp.bfloat16
HIGHEST = lax.Precision.HIGHEST
VMEM = pl.BlockSpec(memory_space=pltpu.VMEM)
HBM = pl.BlockSpec(memory_space=pltpu.HBM)
SMEM = pl.BlockSpec(memory_space=pltpu.SMEM)
FULL = pltpu.CompilerParams(vmem_limit_bytes=62 * 1024 * 1024)
LIMIT = pltpu.CompilerParams(vmem_limit_bytes=16 * 1024 * 1024)


def cost(us, flops=0):
    return pl.CostEstimate(
        flops=int(flops * 1_000_000_000), bytes_accessed=int(us * 3_690_000), transcendentals=0
    )


def mm(left, right):
    return jnp.dot(left.astype(BF16), right.astype(BF16), preferred_element_type=F32)


def mm_nt(left, right):
    return lax.dot_general(
        left.astype(BF16), right.astype(BF16), (((1,), (1,)), ((), ())), preferred_element_type=F32
    )


def mm_tn(left, right):
    return lax.dot_general(
        left.astype(BF16), right.astype(BF16), (((0,), (0,)), ((), ())), preferred_element_type=F32
    )


def split(value):
    high = value.astype(BF16)
    return high, (value - high.astype(F32)).astype(BF16)


def mm3(left, right):
    lh, ll = split(left)
    rh, rl = split(right)
    dot = functools.partial(jnp.dot, preferred_element_type=F32)
    return dot(lh, rh) + (dot(lh, rl) + dot(ll, rh))


def masks(size):
    row = lax.broadcasted_iota(jnp.int32, (size, size), 0)
    col = lax.broadcasted_iota(jnp.int32, (size, size), 1)
    return row, col, row ^ col


def load(pairs, sems):
    copies = []
    for place, (source, target) in enumerate(pairs):
        copies.append(pltpu.make_async_copy(source, target, sems.at[place]))
        copies[-1].start()
    return copies


def convolve(total, taps, padded, rows, part):
    head = taps.shape[2]
    conv_taps = taps.shape[1]
    lanes = slice(part * head, (part + 1) * head)
    edge = total[rows:, lanes].astype(BF16).astype(F32)[total.shape[0] - rows - 8 :]
    padded[0:8, lanes] = jnp.where(lax.axis_index("ctx") > 0, edge, 0.0)
    padded[8:, lanes] = total[:rows, lanes].astype(BF16).astype(F32)
    mixed = padded[9 - conv_taps : 9 - conv_taps + rows, lanes] * taps[part, 0:1, :]
    for tap in range(1, conv_taps):
        start = 9 - conv_taps + tap
        mixed = mixed + padded[start : start + rows, lanes] * taps[part, tap : tap + 1, :]
    return jax.nn.silu(mixed)


def unit_rows(value):
    return value * lax.rsqrt(jnp.sum(value * value, axis=-1, keepdims=True) + 1e-06)


def front(
    tokens_hbm, rim_hbm, alog_hbm, w3_hbm, f_down_hbm, o_down_hbm, f_up_hbm, o_up_hbm, bias_hbm,
    w_beta_hbm, taps_hbm, pack_hbm, sends, tok, w3, f_down, o_down,
    wide, f_up, o_up, bias, w_beta, taps, alog, total, padded, final, pack, sems, out_sems, pack_sems,
):
    rows, model = tokens_hbm.shape
    head = f_up.shape[0]
    count = rows // BLOCK
    inside = SPAN // BLOCK
    chunk = model // CHUNKS
    pairs = [(w_beta_hbm, w_beta), (rim_hbm, tok.at[pl.ds(rows, rim_hbm.shape[0])])]
    for step in range(CHUNKS):
        rng = pl.ds(step * chunk, chunk)
        pairs.append((tokens_hbm.at[:, rng], tok.at[pl.ds(0, rows), rng]))
        pairs += [(w3_hbm.at[part, rng], w3.at[part, rng]) for part in range(3)]
        pairs.append((f_down_hbm.at[rng], f_down.at[rng]))
        pairs.append((o_down_hbm.at[rng], o_down.at[rng]))
    pairs += [(f_up_hbm, f_up), (o_up_hbm, o_up), (bias_hbm, bias), (taps_hbm, taps)]
    pairs.append((alog_hbm, alog))
    copies = load(pairs, sems)
    wide[...] = jnp.zeros_like(wide)
    copies[0].wait()
    column = jnp.transpose(jnp.broadcast_to(w_beta[...].astype(F32), (8, model)))
    wide[:, 0:8] = column.astype(BF16)
    copies[1].wait()
    for step in range(CHUNKS):
        for copy in copies[2 + 6 * step : 8 + 6 * step]:
            copy.wait()
        rng = slice(step * chunk, (step + 1) * chunk)
        joined = [w3[part, rng] for part in range(3)] + [f_down[rng], o_down[rng], wide[rng]]
        piece = jnp.dot(tok[:, rng], jnp.concatenate(joined, axis=1), preferred_element_type=F32)
        if step == 0:
            total[...] = piece
        else:
            total[...] += piece
    for copy in copies[2 + 6 * CHUNKS :]:
        copy.wait()
    low = total[:rows, 3 * head : 4 * head].astype(BF16)
    logit = jnp.dot(low, f_up[...], preferred_element_type=F32) + bias[...]
    decays = -jnp.exp(alog[...]) * jax.nn.softplus(logit)
    out_low = total[:rows, 4 * head : 5 * head].astype(BF16)
    pack[:rows, 2 * head :] = jax.nn.sigmoid(jnp.dot(out_low, o_up[...], preferred_element_type=F32))
    stores = []

    def store(at):
        stores.append(pltpu.make_async_copy(pack.at[at], pack_hbm.at[at], pack_sems.at[len(stores)]))
        stores[-1].start()

    store((pl.ds(0, rows), pl.ds(2 * head, head)))
    beta = jnp.broadcast_to(jax.nn.sigmoid(total[:rows, 5 * head : 5 * head + 1]), (rows, head))
    row, col, differ = masks(GROUP)
    strict = (row > col) & (differ < BLOCK)
    causal = (row >= col) & (differ < BLOCK)
    unit = jnp.where(row == col, 1.0, 0.0).astype(F32)
    tri = jnp.where(causal, 1.0, 0.0).astype(BF16)
    high, rest = split(decays)
    middle, least = split(decays - high.astype(F32) - rest.astype(F32))
    terms = jnp.concatenate([high, rest, middle], axis=1)
    sums = [
        jnp.dot(tri, terms[s : s + GROUP], preferred_element_type=F32) for s in range(0, rows, GROUP)
    ]
    sums = jnp.concatenate(sums, axis=0)
    cumulative = sums[:, :head] + (sums[:, head : 2 * head] + sums[:, 2 * head :])
    key_raw = convolve(total, taps, padded, rows, 1)
    value_raw = convolve(total, taps, padded, rows, 2)
    query_raw = convolve(total, taps, padded, rows, 0)
    keyset = unit_rows(key_raw).astype(BF16).astype(F32)
    values = value_raw.astype(BF16).astype(F32)
    rising = jnp.exp(cumulative)
    key_rise = keyset * rising
    key_fall = (keyset * jnp.exp(-cumulative)).astype(BF16)
    blocked = cumulative.reshape(count, BLOCK, head)
    ends = blocked[:, BLOCK - 1 : BLOCK, :]
    tail = (keyset.reshape(count, BLOCK, head) * jnp.exp(ends - blocked)).reshape(rows, head)
    tail = tail.astype(BF16)
    shrink = jnp.transpose(jnp.exp(ends.reshape(count, head)))
    target = jnp.concatenate([beta * values, beta * key_rise], axis=1).astype(BF16)
    systems, inverse = [], []
    for start in range(0, rows, GROUP):
        rng = slice(start, start + GROUP)
        inner = mm_nt(key_rise[rng], key_fall[rng])
        systems.append(jnp.where(strict, inner * beta[rng], 0.0))
        inverse.append(unit - jnp.where(differ == 1, systems[-1], 0.0))
    size = 2
    while size < BLOCK:
        here = (differ >= size) & (differ < 2 * size)
        steps = [mm(jnp.where(here, s, 0.0), d) for s, d in zip(systems, inverse)]
        inverse = [d - mm(d, x) for d, x in zip(inverse, steps)]
        size *= 2
    pairs, solves, starts = [], [], {}
    for group, start in enumerate(range(0, rows, GROUP)):
        solved = mm(inverse[group], target[start : start + GROUP]).astype(BF16)
        solves.append(solved)
        for block in range(GROUP // BLOCK):
            sub = slice(block * BLOCK, (block + 1) * BLOCK)
            pairs.append(mm_tn(tail[start + block * BLOCK :][:BLOCK], solved[sub]))
    fresh = jnp.concatenate([jnp.zeros((head, head), F32), unit], axis=1)
    states = [fresh] * (rows // SPAN)
    for block in range(inside):
        for group in range(rows // SPAN):
            at = group * inside + block
            state = states[group]
            short = state.astype(BF16)
            starts[at] = short
            step = mm(pairs[at][:, head:], short)
            state = shrink[:, at : at + 1] * state - step
            states[group] = jnp.concatenate(
                [state[:, :head] + pairs[at][:, :head], state[:, head:]], axis=1
            )
    pack[rows : rows + head, : 2 * head] = states[0]
    store((pl.ds(rows, head), pl.ds(0, 2 * head)))
    whole = mm(states[1][:, head:], states[0])
    final[...] = jnp.concatenate(
        [whole[:, :head] + states[1][:, :head], whole[:, head:]], axis=1
    ).astype(BF16)
    copies = load([(final, sends)], out_sems)
    pack[rows + head :, : 2 * head] = final[...].astype(F32)
    store((pl.ds(rows + head, head), pl.ds(0, 2 * head)))
    queries = (unit_rows(query_raw) * (head ** (-0.5))).astype(BF16).astype(F32)
    query_rise = queries * rising
    for group, start in enumerate(range(0, rows, GROUP)):
        rng = slice(start, start + GROUP)
        scores = jnp.where(causal, mm_nt(query_rise[rng], key_fall[rng]), 0.0)
        local = mm(scores, solves[group])
        local_key = (query_rise[rng] - local[:, head:]).astype(BF16)
        for block in range(GROUP // BLOCK):
            sub = slice(block * BLOCK, (block + 1) * BLOCK)
            out = slice(start + block * BLOCK, start + (block + 1) * BLOCK)
            across = jnp.dot(
                local_key[sub], starts[(start // BLOCK) + block], preferred_element_type=F32
            )
            pack[out, :head] = across[:, :head] + local[sub, :head]
            pack[out, head : 2 * head] = across[:, head:]
        store((pl.ds(start, GROUP), pl.ds(0, 2 * head)))
    for copy in copies + stores:
        copy.wait()


def fold(pack, *refs):
    found, (before, total, held) = refs[:-3], refs[-3:]
    count = len(found) + 1
    mine = lax.rem(lax.axis_index("ctx"), count)
    head = found[0].shape[0]
    held[0] = pack[pack.shape[0] - head :, : 2 * head].astype(BF16)
    for back, ref in enumerate(found):
        held[back + 1] = ref[...]
    row = lax.broadcasted_iota(jnp.int32, (head, 2 * head), 0)
    col = lax.broadcasted_iota(jnp.int32, (head, 2 * head), 1)
    state = jnp.where(row + head == col, 1.0, 0.0).astype(F32)
    seen = state
    for step in range(count):
        seen = jnp.where(mine == step, state, seen)
        item = held[lax.rem(mine - step + count, count)]
        moved = jnp.dot(item[:, head:], state.astype(BF16), preferred_element_type=F32)
        state = jnp.concatenate(
            [moved[:, :head] + item[:, :head].astype(F32), moved[:, head:]], axis=1
        )
    before[...] = seen
    total[...] = state[:, :head].astype(BF16)


def stage(pack, gain, out):
    head = gain.shape[1]
    rows = pack.shape[0] - 2 * head
    out[:, : 2 * head] = pack[:, : 2 * head]
    out[:rows, 2 * head :] = pack[:rows, 2 * head :] * gain[...]


def finish(pack, before, came, own, other, gated):
    head = came.shape[0]
    rows = pack.shape[0] - 2 * head
    core_at = lax.rem(lax.axis_index("head"), 2)
    later = lax.axis_index("ctx") >= lax.axis_size("ctx") // 2
    state = jnp.where(later, came[...].astype(F32), 0.0)
    state = mm(before[:, head:], state) + before[:, :head]
    middle = mm(pack[rows : rows + head, head : 2 * head], state)
    middle = middle + pack[rows : rows + head, :head]
    cores = []
    for group, start in enumerate((state, middle)):
        rng = slice(group * SPAN, (group + 1) * SPAN)
        cores.append(pack[rng, :head] + mm(pack[rng, head : 2 * head], start))
    core = jnp.concatenate(cores, axis=0)
    scale = lax.rsqrt(jnp.mean(core * core, axis=-1, keepdims=True) + 1e-05)
    result = core * scale * pack[:rows, 2 * head :]
    gated[...] = result.astype(BF16).reshape(gated.shape)
    for pair in range(own.shape[0]):
        own[pair] = gated[:, pair, pl.ds(core_at, 1)].reshape(own.shape[1:])
        other[pair] = gated[:, pair, pl.ds(1 - core_at, 1)].reshape(own.shape[1:])


def regroup(own, sibling, *outs):
    mine = lax.rem(lax.axis_index("head") // 2, own.shape[0])
    for flip, out in enumerate(outs):
        at = mine ^ flip
        out[0] = own[pl.ds(at, 1)].reshape(out.shape[1:])
        out[1] = sibling[pl.ds(at, 1)].reshape(out.shape[1:])


def spread(part, w_one, w_two, *refs):
    rest, held, out, left = refs[:-3], refs[-3], refs[-2], refs[-1]
    turn(part, left)
    joined = jnp.concatenate([w_one[...], w_two[...]], axis=0)
    out[...] = jnp.dot(left[...], joined, preferred_element_type=F32)
    head = w_one.shape[0]
    for at, ref in enumerate(rest):
        held[at * head : (at + 1) * head] = ref[...]


def turn(part, left):
    mine = lax.axis_index("head") // SUBS
    sides, zs, rows, head = part.shape
    for side in range(sides):
        for k in range(zs):
            piece = part[side, pl.ds(mine ^ k, 1)].reshape(rows, head)
            left[k * rows : (k + 1) * rows, side * head : (side + 1) * head] = piece


def combine(begun, *refs):
    parts, (held, w_one, w_two, out, left) = refs[:3], refs[3:]
    total = begun[...]
    depth = left.shape[-1]
    for which, part in enumerate(parts):
        turn(part, left.at[which])
        if which > 0:
            weight = held[(which - 1) * depth : which * depth]
        else:
            weight = jnp.concatenate([w_one[...], w_two[...]], axis=0)
        total = total + jnp.dot(left[which], weight, preferred_element_type=F32)
    out[...] = total.astype(BF16).reshape(out.shape)


def on_device(
    tokens, w_qkv, conv_weight, f_down, f_up, dt_bias, a_log, w_beta, o_down, o_up, norm_gain, w_out
):
    rows, model = tokens.shape
    head = f_up.shape[1]
    ctx_count, head_count = lax.axis_size("ctx"), lax.axis_size("head")
    zs = head_count // SUBS
    shape = jax.ShapeDtypeStruct
    dma = pltpu.SemaphoreType.DMA

    def across(value):
        half = ctx_count // 2
        pairs = [
            (c * head_count + h, ((c + half) % ctx_count) * head_count + (h ^ 2))
            for c in range(ctx_count)
            for h in range(head_count)
        ]
        return lax.ppermute(value, ("ctx", "head"), pairs)

    def flip(value, mask):
        return lax.ppermute(value, "head", [(h, h ^ mask) for h in range(head_count)])

    w3 = jnp.transpose(w_qkv, (1, 0, 2))
    taps = jnp.transpose(conv_weight, (1, 0, 2))
    edge = tokens[rows - 16 :]
    with jax.named_scope("rim"):
        rim = lax.ppermute(edge, "ctx", [(i, (i + 1) % ctx_count) for i in range(ctx_count)])
    (w_sent,) = after((w_out,), edge)
    with jax.named_scope("weights"):
        w_far, w_next = across(w_sent), flip(w_sent, 4)
    with jax.named_scope("front"):
        pack, sends = pl.pallas_call(
            front,
            in_specs=[HBM] * 11,
            out_specs=[HBM] * 2,
            out_shape=[
                shape((rows + 2 * head, 3 * head), F32),
                shape((head, 2 * head), BF16),
            ],
            scratch_shapes=[
                pltpu.VMEM((rows + 16, model), BF16),
                pltpu.VMEM((3, model, head), BF16),
                pltpu.VMEM((model, head), BF16),
                pltpu.VMEM((model, head), BF16),
                pltpu.VMEM((model, head), BF16),
                pltpu.VMEM((head, head), BF16),
                pltpu.VMEM((head, head), BF16),
                pltpu.VMEM((1, head), F32),
                pltpu.VMEM((1, model), BF16),
                pltpu.VMEM(taps.shape, F32),
                pltpu.VMEM((1, 1), F32),
                pltpu.VMEM((rows + 16, 6 * head), F32),
                pltpu.VMEM((rows + 8, 3 * head), F32),
                pltpu.VMEM((head, 2 * head), BF16),
                pltpu.VMEM((rows + 2 * head, 3 * head), F32),
                dma((7 + 6 * CHUNKS,)),
                dma((1,)),
                dma((3 + rows // GROUP,)),
            ],
            compiler_params=FULL,
            cost_estimate=cost(9, 40),
        )(
            tokens,
            rim,
            a_log.reshape(1, 1),
            w3,
            f_down,
            o_down,
            f_up,
            o_up,
            dt_bias.reshape(1, head),
            w_beta.reshape(1, model),
            taps,
        )
    with jax.named_scope("states"):
        half = ctx_count // 2

        def around(step):
            pairs = [(c, c // half * half + (c + step) % half) for c in range(ctx_count)]
            return lax.ppermute(sends, "ctx", pairs)

        found = {step: around(step) for step in range(1, half)}
    with jax.named_scope("stage"):
        staged = pl.pallas_call(
            stage,
            in_specs=[VMEM] * 2,
            out_specs=VMEM,
            out_shape=shape(pack.shape, F32),
            compiler_params=LIMIT,
            cost_estimate=cost(0.5, 0.5),
        )(pack, norm_gain.reshape(1, head))
    (w_early,) = after((w_far,), staged)
    with jax.named_scope("weights"):
        w_both = flip(w_early, 4)
    with jax.named_scope("states"):
        before, total = pl.pallas_call(
            fold,
            in_specs=[VMEM] * half,
            out_specs=[VMEM] * 2,
            out_shape=[shape((head, 2 * head), F32), shape((head, head), BF16)],
            scratch_shapes=[pltpu.VMEM((half, head, 2 * head), BF16)],
            compiler_params=LIMIT,
            cost_estimate=cost(0.5, 0),
        )(staged, *(found[step] for step in range(1, half)))
        came = lax.ppermute(total, "ctx", [(c, (c + half) % ctx_count) for c in range(ctx_count)])
    w_late, w_near, w_mine = after((w_far, w_next, w_out), staged)
    with jax.named_scope("weights"):
        w_core, w_far_core, w_next_core = flip(w_mine, 1), flip(w_late, 1), flip(w_near, 1)
    with jax.named_scope("finish"):
        own, other = pl.pallas_call(
            finish,
            in_specs=[VMEM] * 3,
            out_specs=[VMEM] * 2,
            out_shape=[shape((SUBS // 2, zs, 16, head), BF16)] * 2,
            scratch_shapes=[pltpu.VMEM((zs, SUBS // 2, 2, 16, head), BF16)],
            compiler_params=LIMIT,
            cost_estimate=cost(2, 0),
        )(staged, before, came)
    with jax.named_scope("exchange"):
        sibling = flip(other, 1)
        kept, *sent = pl.pallas_call(
            regroup,
            in_specs=[VMEM] * 2,
            out_specs=[VMEM] * 4,
            out_shape=[shape((2, zs, 16, head), BF16)] * 4,
            compiler_params=LIMIT,
            cost_estimate=cost(0.5, 0.5),
        )(own, sibling)
        got = {f: flip(sent[f - 1], 2 * f) for f in (3, 1, 2)}
    with jax.named_scope("spread"):
        held, begun = pl.pallas_call(
            spread,
            in_specs=[VMEM] * 7,
            out_specs=[VMEM] * 2,
            out_shape=[shape((4 * head, model), BF16), shape((zs * 16, model), F32)],
            scratch_shapes=[pltpu.VMEM((zs * 16, 2 * head), BF16)],
            compiler_params=LIMIT,
            cost_estimate=cost(2, 2),
        )(kept, w_out, w_core, w_far, w_far_core, w_next, w_next_core)
        (w_late,) = after((w_both,), kept)
        w_both_core = flip(w_late, 1)
        parts = pl.pallas_call(
            combine,
            in_specs=[VMEM] * 7,
            out_specs=VMEM,
            out_shape=shape((zs, 16, model), BF16),
            scratch_shapes=[pltpu.VMEM((3, zs * 16, 2 * head), BF16)],
            compiler_params=LIMIT,
            cost_estimate=cost(1, 1),
        )(begun, got[3], got[1], got[2], held, w_both, w_both_core)
    with jax.named_scope("reduce"):
        total = parts[0].astype(F32)
        for part in [flip(parts[k], SUBS * k) for k in (2, 1, 3)]:
            total = total + part.astype(F32)
        return total.astype(BF16)


def after(values, token):
    return lax.optimization_barrier((*values, token))[: len(values)]


def solution(mesh):
    in_specs = (
        P("ctx", None),
        P(None, None, "head"),
        P(None, None, "head"),
        P(),
        P(None, "head"),
        P("head"),
        P("head"),
        P(None, "head"),
        P(),
        P(None, "head"),
        P(),
        P("head", None),
    )
    out_specs = P(("ctx", "head"), None)
    return jax.shard_map(
        on_device, mesh=mesh, in_specs=in_specs, out_specs=out_specs, check_vma=False
    )
```

```python
import functools

import jax
import jax.numpy as jnp
from jax import lax
from jax.experimental import pallas as pl
from jax.experimental.pallas import tpu as pltpu
from jax.sharding import PartitionSpec as P

BLOCK = 64
GROUP = 128
SPAN = 256
SUBS = 8
CHUNKS = 3
F32 = jnp.float32
BF16 = jnp.bfloat16
HIGHEST = lax.Precision.HIGHEST
VMEM = pl.BlockSpec(memory_space=pltpu.VMEM)
HBM = pl.BlockSpec(memory_space=pltpu.HBM)
SMEM = pl.BlockSpec(memory_space=pltpu.SMEM)
FULL = pltpu.CompilerParams(vmem_limit_bytes=62 * 1024 * 1024)
LIMIT = pltpu.CompilerParams(vmem_limit_bytes=16 * 1024 * 1024)


def cost(us, flops=0):
    return pl.CostEstimate(
        flops=int(flops * 1_000_000_000), bytes_accessed=int(us * 3_690_000), transcendentals=0
    )


def mm(left, right):
    return jnp.dot(left.astype(BF16), right.astype(BF16), preferred_element_type=F32)


def mm_nt(left, right):
    return lax.dot_general(
        left.astype(BF16), right.astype(BF16), (((1,), (1,)), ((), ())), preferred_element_type=F32
    )


def mm_tn(left, right):
    return lax.dot_general(
        left.astype(BF16), right.astype(BF16), (((0,), (0,)), ((), ())), preferred_element_type=F32
    )


def split(value):
    high = value.astype(BF16)
    return high, (value - high.astype(F32)).astype(BF16)


def mm3(left, right):
    lh, ll = split(left)
    rh, rl = split(right)
    dot = functools.partial(jnp.dot, preferred_element_type=F32)
    return dot(lh, rh) + (dot(lh, rl) + dot(ll, rh))


def masks(size):
    row = lax.broadcasted_iota(jnp.int32, (size, size), 0)
    col = lax.broadcasted_iota(jnp.int32, (size, size), 1)
    return row, col, row ^ col


def load(pairs, sems):
    copies = []
    for place, (source, target) in enumerate(pairs):
        copies.append(pltpu.make_async_copy(source, target, sems.at[place]))
        copies[-1].start()
    return copies


def convolve(total, taps, padded, rows, part):
    head = taps.shape[2]
    conv_taps = taps.shape[1]
    lanes = slice(part * head, (part + 1) * head)
    edge = total[rows:, lanes].astype(BF16).astype(F32)[total.shape[0] - rows - 8 :]
    padded[0:8, lanes] = jnp.where(lax.axis_index("ctx") > 0, edge, 0.0)
    padded[8:, lanes] = total[:rows, lanes].astype(BF16).astype(F32)
    mixed = padded[9 - conv_taps : 9 - conv_taps + rows, lanes] * taps[part, 0:1, :]
    for tap in range(1, conv_taps):
        start = 9 - conv_taps + tap
        mixed = mixed + padded[start : start + rows, lanes] * taps[part, tap : tap + 1, :]
    return jax.nn.silu(mixed)


def unit_rows(value):
    return value * lax.rsqrt(jnp.sum(value * value, axis=-1, keepdims=True) + 1e-06)


def front(
    tokens_hbm, rim_hbm, alog_hbm, w3_hbm, f_down_hbm, o_down_hbm, f_up_hbm, o_up_hbm, bias_hbm,
    w_beta_hbm, taps_hbm, pack_hbm, sends, tok, w3, f_down, o_down,
    wide, f_up, o_up, bias, w_beta, taps, alog, total, padded, final, pack, sems, out_sems, pack_sems,
):
    rows, model = tokens_hbm.shape
    head = f_up.shape[0]
    count = rows // BLOCK
    inside = SPAN // BLOCK
    chunk = model // CHUNKS
    pairs = [(w_beta_hbm, w_beta), (rim_hbm, tok.at[pl.ds(rows, rim_hbm.shape[0])])]
    for step in range(CHUNKS):
        rng = pl.ds(step * chunk, chunk)
        pairs.append((tokens_hbm.at[:, rng], tok.at[pl.ds(0, rows), rng]))
        pairs += [(w3_hbm.at[part, rng], w3.at[part, rng]) for part in range(3)]
        pairs.append((f_down_hbm.at[rng], f_down.at[rng]))
        pairs.append((o_down_hbm.at[rng], o_down.at[rng]))
    pairs += [(f_up_hbm, f_up), (o_up_hbm, o_up), (bias_hbm, bias), (taps_hbm, taps)]
    pairs.append((alog_hbm, alog))
    copies = load(pairs, sems)
    wide[...] = jnp.zeros_like(wide)
    copies[0].wait()
    column = jnp.transpose(jnp.broadcast_to(w_beta[...].astype(F32), (8, model)))
    wide[:, 0:8] = column.astype(BF16)
    copies[1].wait()
    for step in range(CHUNKS):
        for copy in copies[2 + 6 * step : 8 + 6 * step]:
            copy.wait()
        rng = slice(step * chunk, (step + 1) * chunk)
        joined = [w3[part, rng] for part in range(3)] + [f_down[rng], o_down[rng], wide[rng]]
        piece = jnp.dot(tok[:, rng], jnp.concatenate(joined, axis=1), preferred_element_type=F32)
        if step == 0:
            total[...] = piece
        else:
            total[...] += piece
    for copy in copies[2 + 6 * CHUNKS :]:
        copy.wait()
    low = total[:rows, 3 * head : 4 * head].astype(BF16)
    logit = jnp.dot(low, f_up[...], preferred_element_type=F32) + bias[...]
    decays = -jnp.exp(alog[...]) * jax.nn.softplus(logit)
    out_low = total[:rows, 4 * head : 5 * head].astype(BF16)
    pack[:rows, 2 * head :] = jax.nn.sigmoid(jnp.dot(out_low, o_up[...], preferred_element_type=F32))
    stores = []

    def store(at):
        stores.append(pltpu.make_async_copy(pack.at[at], pack_hbm.at[at], pack_sems.at[len(stores)]))
        stores[-1].start()

    store((pl.ds(0, rows), pl.ds(2 * head, head)))
    beta = jnp.broadcast_to(jax.nn.sigmoid(total[:rows, 5 * head : 5 * head + 1]), (rows, head))
    row, col, differ = masks(GROUP)
    strict = (row > col) & (differ < BLOCK)
    causal = (row >= col) & (differ < BLOCK)
    unit = jnp.where(row == col, 1.0, 0.0).astype(F32)
    tri = jnp.where(causal, 1.0, 0.0).astype(BF16)
    high, rest = split(decays)
    middle, least = split(decays - high.astype(F32) - rest.astype(F32))
    terms = jnp.concatenate([high, rest, middle], axis=1)
    sums = [
        jnp.dot(tri, terms[s : s + GROUP], preferred_element_type=F32) for s in range(0, rows, GROUP)
    ]
    sums = jnp.concatenate(sums, axis=0)
    cumulative = sums[:, :head] + (sums[:, head : 2 * head] + sums[:, 2 * head :])
    key_raw = convolve(total, taps, padded, rows, 1)
    value_raw = convolve(total, taps, padded, rows, 2)
    query_raw = convolve(total, taps, padded, rows, 0)
    keyset = unit_rows(key_raw).astype(BF16).astype(F32)
    values = value_raw.astype(BF16).astype(F32)
    rising = jnp.exp(cumulative)
    key_rise = keyset * rising
    key_fall = (keyset * jnp.exp(-cumulative)).astype(BF16)
    blocked = cumulative.reshape(count, BLOCK, head)
    ends = blocked[:, BLOCK - 1 : BLOCK, :]
    tail = (keyset.reshape(count, BLOCK, head) * jnp.exp(ends - blocked)).reshape(rows, head)
    tail = tail.astype(BF16)
    shrink = jnp.transpose(jnp.exp(ends.reshape(count, head)))
    target = jnp.concatenate([beta * values, beta * key_rise], axis=1).astype(BF16)
    systems, inverse = [], []
    for start in range(0, rows, GROUP):
        rng = slice(start, start + GROUP)
        inner = mm_nt(key_rise[rng], key_fall[rng])
        systems.append(jnp.where(strict, inner * beta[rng], 0.0))
        inverse.append(unit - jnp.where(differ == 1, systems[-1], 0.0))
    size = 2
    while size < BLOCK:
        here = (differ >= size) & (differ < 2 * size)
        steps = [mm(jnp.where(here, s, 0.0), d) for s, d in zip(systems, inverse)]
        inverse = [d - mm(d, x) for d, x in zip(inverse, steps)]
        size *= 2
    pairs, solves, starts = [], [], {}
    for group, start in enumerate(range(0, rows, GROUP)):
        solved = mm(inverse[group], target[start : start + GROUP]).astype(BF16)
        solves.append(solved)
        for block in range(GROUP // BLOCK):
            sub = slice(block * BLOCK, (block + 1) * BLOCK)
            pairs.append(mm_tn(tail[start + block * BLOCK :][:BLOCK], solved[sub]))
    fresh = jnp.concatenate([jnp.zeros((head, head), F32), unit], axis=1)
    states = [fresh] * (rows // SPAN)
    for block in range(inside):
        for group in range(rows // SPAN):
            at = group * inside + block
            state = states[group]
            short = state.astype(BF16)
            starts[at] = short
            step = mm(pairs[at][:, head:], short)
            state = shrink[:, at : at + 1] * state - step
            states[group] = jnp.concatenate(
                [state[:, :head] + pairs[at][:, :head], state[:, head:]], axis=1
            )
    pack[rows : rows + head, : 2 * head] = states[0]
    store((pl.ds(rows, head), pl.ds(0, 2 * head)))
    whole = mm(states[1][:, head:], states[0])
    final[...] = jnp.concatenate(
        [whole[:, :head] + states[1][:, :head], whole[:, head:]], axis=1
    ).astype(BF16)
    copies = load([(final, sends)], out_sems)
    pack[rows + head :, : 2 * head] = final[...].astype(F32)
    store((pl.ds(rows + head, head), pl.ds(0, 2 * head)))
    queries = (unit_rows(query_raw) * (head ** (-0.5))).astype(BF16).astype(F32)
    query_rise = queries * rising
    for group, start in enumerate(range(0, rows, GROUP)):
        rng = slice(start, start + GROUP)
        scores = jnp.where(causal, mm_nt(query_rise[rng], key_fall[rng]), 0.0)
        local = mm(scores, solves[group])
        local_key = (query_rise[rng] - local[:, head:]).astype(BF16)
        for block in range(GROUP // BLOCK):
            sub = slice(block * BLOCK, (block + 1) * BLOCK)
            out = slice(start + block * BLOCK, start + (block + 1) * BLOCK)
            across = jnp.dot(
                local_key[sub], starts[(start // BLOCK) + block], preferred_element_type=F32
            )
            pack[out, :head] = across[:, :head] + local[sub, :head]
            pack[out, head : 2 * head] = across[:, head:]
        store((pl.ds(start, GROUP), pl.ds(0, 2 * head)))
    for copy in copies + stores:
        copy.wait()


def fold(pack, *refs):
    found, (before, total, held) = refs[:-3], refs[-3:]
    count = len(found) + 1
    mine = lax.rem(lax.axis_index("ctx"), count)
    head = found[0].shape[0]
    held[0] = pack[pack.shape[0] - head :, : 2 * head].astype(BF16)
    for back, ref in enumerate(found):
        held[back + 1] = ref[...]
    row = lax.broadcasted_iota(jnp.int32, (head, 2 * head), 0)
    col = lax.broadcasted_iota(jnp.int32, (head, 2 * head), 1)
    state = jnp.where(row + head == col, 1.0, 0.0).astype(F32)
    seen = state
    for step in range(count):
        seen = jnp.where(mine == step, state, seen)
        item = held[lax.rem(mine - step + count, count)]
        moved = jnp.dot(item[:, head:], state.astype(BF16), preferred_element_type=F32)
        state = jnp.concatenate(
            [moved[:, :head] + item[:, :head].astype(F32), moved[:, head:]], axis=1
        )
    before[...] = seen
    total[...] = state[:, :head].astype(BF16)


def stage(pack, gain, out):
    head = gain.shape[1]
    rows = pack.shape[0] - 2 * head
    out[:, : 2 * head] = pack[:, : 2 * head]
    out[:rows, 2 * head :] = pack[:rows, 2 * head :] * gain[...]


def finish(pack, before, came, own, other, gated):
    head = came.shape[0]
    rows = pack.shape[0] - 2 * head
    core_at = lax.rem(lax.axis_index("head"), 2)
    later = lax.axis_index("ctx") >= lax.axis_size("ctx") // 2
    state = jnp.where(later, came[...].astype(F32), 0.0)
    state = mm(before[:, head:], state) + before[:, :head]
    middle = mm(pack[rows : rows + head, head : 2 * head], state)
    middle = middle + pack[rows : rows + head, :head]
    cores = []
    for group, start in enumerate((state, middle)):
        rng = slice(group * SPAN, (group + 1) * SPAN)
        cores.append(pack[rng, :head] + mm(pack[rng, head : 2 * head], start))
    core = jnp.concatenate(cores, axis=0)
    scale = lax.rsqrt(jnp.mean(core * core, axis=-1, keepdims=True) + 1e-05)
    result = core * scale * pack[:rows, 2 * head :]
    gated[...] = result.astype(BF16).reshape(gated.shape)
    for pair in range(own.shape[0]):
        own[pair] = gated[:, pair, pl.ds(core_at, 1)].reshape(own.shape[1:])
        other[pair] = gated[:, pair, pl.ds(1 - core_at, 1)].reshape(own.shape[1:])


def regroup(own, sibling, *outs):
    mine = lax.rem(lax.axis_index("head") // 2, own.shape[0])
    for flip, out in enumerate(outs):
        at = mine ^ flip
        out[0] = own[pl.ds(at, 1)].reshape(out.shape[1:])
        out[1] = sibling[pl.ds(at, 1)].reshape(out.shape[1:])


def spread(part, w_one, w_two, *refs):
    rest, held, out, left = refs[:-3], refs[-3], refs[-2], refs[-1]
    turn(part, left)
    joined = jnp.concatenate([w_one[...], w_two[...]], axis=0)
    out[...] = jnp.dot(left[...], joined, preferred_element_type=F32)
    head = w_one.shape[0]
    for at, ref in enumerate(rest):
        held[at * head : (at + 1) * head] = ref[...]


def turn(part, left):
    mine = lax.axis_index("head") // SUBS
    sides, zs, rows, head = part.shape
    for side in range(sides):
        for k in range(zs):
            piece = part[side, pl.ds(mine ^ k, 1)].reshape(rows, head)
            left[k * rows : (k + 1) * rows, side * head : (side + 1) * head] = piece


def combine(begun, *refs):
    parts, (held, w_one, w_two, out, left) = refs[:3], refs[3:]
    total = begun[...]
    depth = left.shape[-1]
    for which, part in enumerate(parts):
        turn(part, left.at[which])
        if which > 0:
            weight = held[(which - 1) * depth : which * depth]
        else:
            weight = jnp.concatenate([w_one[...], w_two[...]], axis=0)
        total = total + jnp.dot(left[which], weight, preferred_element_type=F32)
    out[...] = total.astype(BF16).reshape(out.shape)


def on_device(
    tokens, w_qkv, conv_weight, f_down, f_up, dt_bias, a_log, w_beta, o_down, o_up, norm_gain, w_out
):
    rows, model = tokens.shape
    head = f_up.shape[1]
    ctx_count, head_count = lax.axis_size("ctx"), lax.axis_size("head")
    zs = head_count // SUBS
    shape = jax.ShapeDtypeStruct
    dma = pltpu.SemaphoreType.DMA

    def across(value):
        half = ctx_count // 2
        pairs = [
            (c * head_count + h, ((c + half) % ctx_count) * head_count + (h ^ 2))
            for c in range(ctx_count)
            for h in range(head_count)
        ]
        return lax.ppermute(value, ("ctx", "head"), pairs)

    def flip(value, mask):
        return lax.ppermute(value, "head", [(h, h ^ mask) for h in range(head_count)])

    w3 = jnp.transpose(w_qkv, (1, 0, 2))
    taps = jnp.transpose(conv_weight, (1, 0, 2))
    edge = tokens[rows - 16 :]
    with jax.named_scope("rim"):
        rim = lax.ppermute(edge, "ctx", [(i, (i + 1) % ctx_count) for i in range(ctx_count)])
    (w_sent,) = after((w_out,), edge)
    with jax.named_scope("weights"):
        w_far, w_next = across(w_sent), flip(w_sent, 4)
    with jax.named_scope("front"):
        pack, sends = pl.pallas_call(
            front,
            in_specs=[HBM] * 11,
            out_specs=[HBM] * 2,
            out_shape=[
                shape((rows + 2 * head, 3 * head), F32),
                shape((head, 2 * head), BF16),
            ],
            scratch_shapes=[
                pltpu.VMEM((rows + 16, model), BF16),
                pltpu.VMEM((3, model, head), BF16),
                pltpu.VMEM((model, head), BF16),
                pltpu.VMEM((model, head), BF16),
                pltpu.VMEM((model, head), BF16),
                pltpu.VMEM((head, head), BF16),
                pltpu.VMEM((head, head), BF16),
                pltpu.VMEM((1, head), F32),
                pltpu.VMEM((1, model), BF16),
                pltpu.VMEM(taps.shape, F32),
                pltpu.VMEM((1, 1), F32),
                pltpu.VMEM((rows + 16, 6 * head), F32),
                pltpu.VMEM((rows + 8, 3 * head), F32),
                pltpu.VMEM((head, 2 * head), BF16),
                pltpu.VMEM((rows + 2 * head, 3 * head), F32),
                dma((7 + 6 * CHUNKS,)),
                dma((1,)),
                dma((3 + rows // GROUP,)),
            ],
            compiler_params=FULL,
            cost_estimate=cost(9, 40),
        )(
            tokens,
            rim,
            a_log.reshape(1, 1),
            w3,
            f_down,
            o_down,
            f_up,
            o_up,
            dt_bias.reshape(1, head),
            w_beta.reshape(1, model),
            taps,
        )
    with jax.named_scope("states"):
        half = ctx_count // 2

        def around(step):
            pairs = [(c, c // half * half + (c + step) % half) for c in range(ctx_count)]
            return lax.ppermute(sends, "ctx", pairs)

        found = {step: around(step) for step in range(1, half)}
    with jax.named_scope("stage"):
        staged = pl.pallas_call(
            stage,
            in_specs=[VMEM] * 2,
            out_specs=VMEM,
            out_shape=shape(pack.shape, F32),
            compiler_params=LIMIT,
            cost_estimate=cost(0.5, 0.5),
        )(pack, norm_gain.reshape(1, head))
    (w_early,) = after((w_far,), staged)
    with jax.named_scope("weights"):
        w_both = flip(w_early, 4)
    with jax.named_scope("states"):
        before, total = pl.pallas_call(
            fold,
            in_specs=[VMEM] * half,
            out_specs=[VMEM] * 2,
            out_shape=[shape((head, 2 * head), F32), shape((head, head), BF16)],
            scratch_shapes=[pltpu.VMEM((half, head, 2 * head), BF16)],
            compiler_params=LIMIT,
            cost_estimate=cost(0.5, 2),
        )(staged, *(found[step] for step in range(1, half)))
        came = lax.ppermute(total, "ctx", [(c, (c + half) % ctx_count) for c in range(ctx_count)])
    w_late, w_near, w_mine = after((w_far, w_next, w_out), staged)
    with jax.named_scope("weights"):
        w_core, w_far_core, w_next_core = flip(w_mine, 1), flip(w_late, 1), flip(w_near, 1)
    with jax.named_scope("finish"):
        own, other = pl.pallas_call(
            finish,
            in_specs=[VMEM] * 3,
            out_specs=[VMEM] * 2,
            out_shape=[shape((SUBS // 2, zs, 16, head), BF16)] * 2,
            scratch_shapes=[pltpu.VMEM((zs, SUBS // 2, 2, 16, head), BF16)],
            compiler_params=LIMIT,
            cost_estimate=cost(2, 4),
        )(staged, before, came)
    with jax.named_scope("exchange"):
        sibling = flip(other, 1)
        kept, *sent = pl.pallas_call(
            regroup,
            in_specs=[VMEM] * 2,
            out_specs=[VMEM] * 4,
            out_shape=[shape((2, zs, 16, head), BF16)] * 4,
            compiler_params=LIMIT,
            cost_estimate=cost(0.5, 0.5),
        )(own, sibling)
        got = {f: flip(sent[f - 1], 2 * f) for f in (3, 1, 2)}
    with jax.named_scope("spread"):
        held, begun = pl.pallas_call(
            spread,
            in_specs=[VMEM] * 7,
            out_specs=[VMEM] * 2,
            out_shape=[shape((4 * head, model), BF16), shape((zs * 16, model), F32)],
            scratch_shapes=[pltpu.VMEM((zs * 16, 2 * head), BF16)],
            compiler_params=LIMIT,
            cost_estimate=cost(2, 2),
        )(kept, w_out, w_core, w_far, w_far_core, w_next, w_next_core)
        (w_late,) = after((w_both,), kept)
        w_both_core = flip(w_late, 1)
        parts = pl.pallas_call(
            combine,
            in_specs=[VMEM] * 7,
            out_specs=VMEM,
            out_shape=shape((zs, 16, model), BF16),
            scratch_shapes=[pltpu.VMEM((3, zs * 16, 2 * head), BF16)],
            compiler_params=LIMIT,
            cost_estimate=cost(1, 1),
        )(begun, got[3], got[1], got[2], held, w_both, w_both_core)
    with jax.named_scope("reduce"):
        total = parts[0].astype(F32)
        for part in [flip(parts[k], SUBS * k) for k in (2, 1, 3)]:
            total = total + part.astype(F32)
        return total.astype(BF16)


def after(values, token):
    return lax.optimization_barrier((*values, token))[: len(values)]


def solution(mesh):
    in_specs = (
        P("ctx", None),
        P(None, None, "head"),
        P(None, None, "head"),
        P(),
        P(None, "head"),
        P("head"),
        P("head"),
        P(None, "head"),
        P(),
        P(None, "head"),
        P(),
        P("head", None),
    )
    out_specs = P(("ctx", "head"), None)
    return jax.shard_map(
        on_device, mesh=mesh, in_specs=in_specs, out_specs=out_specs, check_vma=False
    )
```
